32 devices in a mesh: chan: 4 (over x, core), frames: 8 (over z, y).
Axes of the slice: x: 2, y: 2, z: 4, core: 2. Of those that a mesh axis runs over, the one named last changes fastest.
Arguments:
- signal: bfloat16 [2688, 8192], P('frames', 'chan'), may hold values from -7.2 to 7.2
- clip_ids: int32 [2688], P('frames'), may hold values from 0 to 4, never falling along the last dimension, each value on 1 to 1075 neighbouring positions
- output_grad: bfloat16 [2688, 8192], P('frames', 'chan'), may hold values from -8.4 to 8.4
- first_weight: float32 [1280, 256], P('frames', 'chan'), may hold values from -0.1875 to 0.1875
- first_mean: float32 [1280, 256], P('frames', 'chan'), may hold values from -0.046875 to 0.046875
- first_square: float32 [1280, 256], P('frames', 'chan'), may hold values from 4.7643007e-06 to 1.9057203e-05
- wide_weight: float32 [3, 2304, 256], P(None, 'frames', 'chan'), may hold values from -0.125 to 0.125
- wide_mean: float32 [3, 2304, 256], P(None, 'frames', 'chan'), may hold values from -0.046875 to 0.046875
- wide_square: float32 [3, 2304, 256], P(None, 'frames', 'chan'), may hold values from 4.7643007e-06 to 1.9057203e-05
- norm_params: float32 [2, 7, 128], P(None, None, 'chan'), may hold values from -1.2 to 2.6
- norm_mean: float32 [2, 7, 128], P(None, None, 'chan'), may hold values from -0.046875 to 0.046875
- norm_square: float32 [2, 7, 128], P(None, None, 'chan'), may hold values from 4.7643007e-06 to 1.9057203e-05
Outputs:
- block_out: float32 [2688, 8192], P('frames', 'chan')
- input_grad: float32 [2688, 8192], P('frames', 'chan')
- grad_norm: float32 [], replicated
- first_next: float32 [1280, 256], P('frames', 'chan')
- first_mean_next: float32 [1280, 256], P('frames', 'chan')
- first_square_next: float32 [1280, 256], P('frames', 'chan')
- first_rounded: bfloat16 [1280, 256], P('frames', 'chan')
- wide_next: float32 [3, 2304, 256], P(None, 'frames', 'chan')
- wide_mean_next: float32 [3, 2304, 256], P(None, 'frames', 'chan')
- wide_square_next: float32 [3, 2304, 256], P(None, 'frames', 'chan')
- wide_rounded: bfloat16 [3, 2304, 256], P(None, 'frames', 'chan')
- norm_next: float32 [2, 7, 128], P(None, None, 'chan')
- norm_mean_next: float32 [2, 7, 128], P(None, None, 'chan')
- norm_square_next: float32 [2, 7, 128], P(None, None, 'chan')
The draws below stay inside these ranges and needn't reach their ends.
Inputs may be any that keep to these rules, and one draw needn't show every extreme that they name: `clip_ids`: clip number of each frame: 0 at the first frame, never falling, rising by one where a clip begins; every clip has 1 to 1075 frames.
All inputs are finite; a program needn't handle non-finite values.
Results may differ from the reference program's by a relative error of at most 0.024.
Values may be sent and summed in bfloat16 or wider, within the bound.
No kernel may reach another device: no remote copies, remote signals or barrier semaphores. Data moves between devices by JAX's collectives and lax.ppermute only.
A program may use at most 384 MiB of HBM per device.

```python
import functools
import math
import jax
import jax.numpy as jnp
import numpy as np
from jax import lax

C0 = 128
C = 256
B0 = 64
STEP = 10
B1 = 32
FRAMES = 2688
CLIPS = 5
PARAMS = 2098944


def ramp_of(count, top):
    place = jnp.arange(count, dtype=jnp.float32) / (count - 1)
    return 1.0 + (top - 1.0) * place


def draw_signal(key, part):
    key = jax.random.fold_in(key, 11)
    noise = jax.random.truncated_normal(key, -4.0, 4.0, (FRAMES, C0 * B0), jnp.float32)
    values = 0.6 * noise * ramp_of(FRAMES, 3.0)[:, None]
    return values.astype(jnp.bfloat16)


def draw_output_grad(key, part):
    key = jax.random.fold_in(key, 12)
    noise = jax.random.truncated_normal(key, -4.0, 4.0, (FRAMES, C * B1), jnp.float32)
    values = 0.7 * noise * ramp_of(FRAMES, 3.0)[:, None]
    return values.astype(jnp.bfloat16)


def draw_norm_params(key, part):
    key = jax.random.fold_in(key, 13)
    key_gain, key_bias = jax.random.split(key)
    place = jnp.arange(C0, dtype=jnp.float32) / (C0 - 1)
    wobble = jnp.exp(jax.random.uniform(key_gain, (7, C0), jnp.float32, -0.25, 0.25))
    gains = 0.6 * (1.0 + 2.0 * place) * wobble
    biases = 0.3 * jax.random.truncated_normal(key_bias, -4.0, 4.0, (7, C0), jnp.float32)
    return jnp.stack([gains, biases])


def levels(own_key, dims, cuts, least, largest):
    factor_of, own = 1.0, jax.random.fold_in(own_key, 6)
    for axis_at, parts in cuts:
        heights = jnp.exp(jax.random.uniform(jax.random.fold_in(own, axis_at), (parts,), jnp.float32, least / len(cuts), largest / len(cuts)))
        factor_of = factor_of * jnp.repeat(heights, dims[axis_at] // parts).reshape([-1 if axis == axis_at else 1 for axis in range(len(dims))])
    return factor_of


def split_up(number_of, total, most, slope):
    weights = [(1 << 20) // math.isqrt(grade ** slope) + 1 for grade in range(2, number_of + 1)]
    spare, holding = total - most - (number_of - 1), [1] * (number_of - 1)
    while spare > 0:
        candidates = [i for i in range(number_of - 1) if holding[i] < most]
        whole, left = sum([weights[i] for i in candidates]), spare
        for i in candidates:
            more = min(most - holding[i], max(1, left * weights[i] // whole), spare)
            holding[i] = holding[i] + more
            spare = spare - more
    return np.array([most] + holding)


def uneven(rng, number_of, total, bound, lean):
    if number_of == 2:
        one = jax.random.randint(rng, (), max(1, total - bound), min(bound, total - 1) + 1)
        return jnp.stack([one, total - one])
    sizes = jnp.asarray(split_up(number_of, total, bound, lean), jnp.int32)
    couples = (number_of - 1) // 2
    donor, receiver = sizes[1:1 + 2 * couples:2], sizes[2:2 + 2 * couples:2]
    margin = jnp.minimum(donor - 1, bound - receiver)
    passed = jax.random.randint(jax.random.fold_in(rng, 1), (couples,), 0, 1 << 20) % (margin + 1)
    sizes = sizes.at[1:1 + 2 * couples:2].set(donor - passed).at[2:2 + 2 * couples:2].set(receiver + passed)
    return sizes[jax.random.permutation(jax.random.fold_in(rng, 2), number_of)]


def normal_values(own_key, extent, scale, bound, cuts=(), kind=jnp.bfloat16):
    factor_of = levels(own_key, extent, cuts, -0.22, 0.18) if cuts else 1.0
    entries = jax.random.normal(own_key, extent, jnp.float32) * scale * factor_of
    return jnp.minimum(jnp.maximum(entries, -bound), bound).astype(kind)


def setup_inputs(seed: int = 0) -> dict:
    keys = jax.random.split(jax.random.key(seed), 13)
    signal = draw_signal(jax.random.fold_in(keys[12], 71), 0)
    clip_ids = jnp.searchsorted(jnp.cumsum(uneven(keys[1], CLIPS, FRAMES, 2 * FRAMES // CLIPS, 0)), jnp.arange(FRAMES), side="right").astype(jnp.int32)
    output_grad = draw_output_grad(jax.random.fold_in(keys[12], 71), 0)
    first_weight = normal_values(keys[3], (10 * C0, C), (9 * C0) ** -0.5, 0.1875, ((0, 8), (1, 4)), jnp.float32)
    first_mean = normal_values(keys[4], (10 * C0, C), (11.0 * PARAMS ** -0.5), 0.046875, ((0, 8), (1, 4)), jnp.float32)
    first_square = jnp.clip(jnp.exp(math.log(1.9057202734984457e-05) - 1.3862944 * jax.random.uniform(keys[5], (10 * C0, C), jnp.float32) ** levels(keys[5], (10 * C0, C), ((0, 8), (1, 4)), -0.2, 0.2)), 4.764300683746114e-06, 1.9057202734984457e-05)
    wide_weight = normal_values(keys[6], (3, 9 * C, C), (9 * C) ** -0.5, 0.125, ((1, 8), (2, 4)), jnp.float32)
    wide_mean = normal_values(keys[7], (3, 9 * C, C), (11.0 * PARAMS ** -0.5), 0.046875, ((1, 8), (2, 4)), jnp.float32)
    wide_square = jnp.clip(jnp.exp(math.log(1.9057202734984457e-05) - 1.3862944 * jax.random.uniform(keys[8], (3, 9 * C, C), jnp.float32) ** levels(keys[8], (3, 9 * C, C), ((1, 8), (2, 4)), -0.2, 0.2)), 4.764300683746114e-06, 1.9057202734984457e-05)
    norm_params = draw_norm_params(jax.random.fold_in(keys[12], 71), 0)
    norm_mean = normal_values(keys[10], (2, 7, C0), (11.0 * PARAMS ** -0.5), 0.046875, ((2, 4),), jnp.float32)
    norm_square = jnp.clip(jnp.exp(math.log(1.9057202734984457e-05) - 1.3862944 * jax.random.uniform(keys[11], (2, 7, C0), jnp.float32) ** levels(keys[11], (2, 7, C0), ((2, 4),), -0.2, 0.2)), 4.764300683746114e-06, 1.9057202734984457e-05)
    return {"signal": signal, "clip_ids": clip_ids, "output_grad": output_grad, "first_weight": first_weight, "first_mean": first_mean, "first_square": first_square, "wide_weight": wide_weight, "wide_mean": wide_mean, "wide_square": wide_square, "norm_params": norm_params, "norm_mean": norm_mean, "norm_square": norm_square}


@jax.custom_vjp
def low(v):
    return lax.optimization_barrier(v.astype(jnp.bfloat16)).astype(jnp.float32)

@jax.custom_vjp
def low_back(v):
    return v

def low_keep(v):
    return (low(v), None)

def low_pass(kept, grad):
    return (grad,)

def back_keep(v):
    return (v, None)

def back_low(kept, grad):
    return (low(grad),)
low.defvjp(low_keep, low_pass)
low_back.defvjp(back_keep, back_low)
norm_epsilon = 1e-05
clip_limit = 100.0
beta_first = 0.9
beta_second = 0.999
adam_epsilon = 1e-08
conv_rate = 0.05
norm_rate = 0.5
weight_decay = 0.01
highest = lax.Precision.HIGHEST

def norm_pair(params, norm_index):
    if norm_index == 0:
        return (params[0, 0], params[1, 0])
    row_pair = params[:, 2 * norm_index - 1:2 * norm_index + 1]
    packed = jnp.transpose(row_pair, (0, 2, 1)).reshape(2, -1)
    return (packed[0], packed[1])

def activate(values, norm_gain, norm_bias):
    total_count = values.shape[0] * values.shape[1]
    average = lax.optimization_barrier(jnp.sum(values, axis=(0, 1))) / total_count
    square_mean = lax.optimization_barrier(jnp.sum(values * values, axis=(0, 1))) / total_count
    inverse_spread = lax.rsqrt(square_mean - average * average + norm_epsilon)
    scaled = (values - average) * inverse_spread
    return jax.nn.silu(scaled * norm_gain + norm_bias)

@functools.partial(jax.checkpoint, static_argnums=(4,))
def convolve(inputs, taps, mask_prev, mask_next, stride):
    frames = inputs.shape[0]
    out_bins = inputs.shape[1] // stride
    padded = jnp.pad(inputs, ((1, 1), (1, 1), (0, 0)))
    summed = jnp.zeros((frames, out_bins, taps.shape[2]), jnp.float32)
    for time_tap in range(3):
        partial_sum = jnp.zeros_like(summed)
        for freq_tap in range(3):
            window = padded[time_tap:time_tap + frames, freq_tap:freq_tap + stride * (out_bins - 1) + 1:stride]
            partial_sum = partial_sum + jnp.einsum('fbi,io->fbo', window, taps[:, 3 * time_tap + freq_tap], precision=highest)
        if time_tap == 0:
            partial_sum = partial_sum * mask_prev
        if time_tap == 2:
            partial_sum = partial_sum * mask_next
        summed = summed + partial_sum
    return summed

def forward(signal_values, first_values, wide_values, params, mask_prev, mask_next):
    first_low = low(first_values)
    wide_low = low(wide_values)
    taps_first = first_low[:9 * C0].reshape(C0, 9, C)
    short_taps = first_low[9 * C0:]
    act_one = low(activate(signal_values, *norm_pair(params, 0)))
    hidden_one = low_back(convolve(act_one, taps_first, mask_prev, mask_next, 2))
    shortcut = low_back(jnp.einsum('fbi,io->fbo', act_one[:, 0::2], short_taps, precision=highest))
    mid_one = low(activate(hidden_one, *norm_pair(params, 1)))
    residual = low_back(convolve(mid_one, wide_low[0].reshape(C, 9, C), mask_prev, mask_next, 1)) + shortcut
    act_two = low(activate(residual, *norm_pair(params, 2)))
    hidden_two = low_back(convolve(act_two, wide_low[1].reshape(C, 9, C), mask_prev, mask_next, 1))
    mid_two = low(activate(hidden_two, *norm_pair(params, 3)))
    return residual + low_back(convolve(mid_two, wide_low[2].reshape(C, 9, C), mask_prev, mask_next, 1))

def adam_step(weight, moment, square, gradient, step_rate, decay_rate):
    moment_next = beta_first * moment + (1.0 - beta_first) * gradient
    square_next = beta_second * square + (1.0 - beta_second) * gradient * gradient
    corrected = moment_next / (1.0 - beta_first ** STEP)
    divisor = jnp.sqrt(square_next / (1.0 - beta_second ** STEP)) + adam_epsilon
    weight_next = weight - step_rate * (corrected / divisor + decay_rate * weight)
    return (weight_next, moment_next, square_next)

def reference(signal, clip_ids, output_grad, first_weight, first_mean, first_square, wide_weight, wide_mean, wide_square, norm_params, norm_mean, norm_square):
    same_clip = (clip_ids[1:] == clip_ids[:-1]).astype(jnp.float32)
    edge_zero = jnp.zeros((1,), jnp.float32)
    mask_prev = jnp.concatenate([edge_zero, same_clip])[:, None, None]
    mask_next = jnp.concatenate([same_clip, edge_zero])[:, None, None]
    signal_cube = jnp.transpose(signal.astype(jnp.float32).reshape(FRAMES, C0, B0), (0, 2, 1))
    grad_cube = jnp.transpose(output_grad.astype(jnp.float32).reshape(FRAMES, C, B1), (0, 2, 1))
    bound_forward = functools.partial(forward, mask_prev=mask_prev, mask_next=mask_next)
    block_cube, pullback = jax.vjp(bound_forward, signal_cube, first_weight, wide_weight, norm_params)
    input_cube, first_grad, wide_grad, norm_grad = pullback(grad_cube)
    block_out = jnp.transpose(block_cube, (0, 2, 1)).reshape(FRAMES, C * B1)
    input_grad = jnp.transpose(input_cube, (0, 2, 1)).reshape(FRAMES, C0 * B0)
    squares = jnp.sum(first_grad * first_grad) + jnp.sum(wide_grad * wide_grad) + jnp.sum(norm_grad * norm_grad)
    grad_norm = jnp.sqrt(squares)
    factor = clip_limit / jnp.maximum(grad_norm, clip_limit)
    first_next, first_mean_next, first_square_next = adam_step(first_weight, first_mean, first_square, first_grad * factor, conv_rate, weight_decay)
    wide_next, wide_mean_next, wide_square_next = adam_step(wide_weight, wide_mean, wide_square, wide_grad * factor, conv_rate, weight_decay)
    norm_next, norm_mean_next, norm_square_next = adam_step(norm_params, norm_mean, norm_square, norm_grad * factor, norm_rate, 0.0)
    return (block_out, input_grad, grad_norm, first_next, first_mean_next, first_square_next, first_next.astype(jnp.bfloat16), wide_next, wide_mean_next, wide_square_next, wide_next.astype(jnp.bfloat16), norm_next, norm_mean_next, norm_square_next)
```

```python
import functools

import jax
import jax.numpy as jnp
import numpy as np
from jax import lax
from jax.experimental import pallas as pl
from jax.experimental.pallas import tpu as pltpu
from jax.sharding import PartitionSpec as P

B0 = 64
STEP = 10
B1 = 32
HALO = 6

norm_epsilon = 1e-05
clip_limit = 100.0
beta_first = 0.9
beta_second = 0.999
adam_epsilon = 1e-08
conv_rate = 0.05
norm_rate = 0.5
weight_decay = 0.01

BOTH = ("chan", "frames")
VMEM_BYTES = 56 * 1024 * 1024
F32 = jnp.float32
BF16 = jnp.bfloat16


def total_sum(vector):
    count = lax.axis_size("chan") * lax.axis_size("frames")
    copies = jnp.broadcast_to(vector[None], (count,) + vector.shape)
    return jnp.sum(lax.all_to_all(copies, BOTH, 0, 0, tiled=True), axis=0)


def frame_edges(block, width):
    count = lax.axis_size("frames")
    forward = [(i, i + 1) for i in range(count - 1)]
    backward = [(b, a) for a, b in forward]
    low = lax.ppermute(block[block.shape[0] - width :], "frames", forward)
    high = lax.ppermute(block[:width], "frames", backward)
    return jnp.concatenate([low, block, high], axis=0)


def to_frames(block):
    parts = lax.axis_size("chan")
    own = block.shape[0] // parts
    padded = frame_edges(block, HALO)
    windows = jnp.stack([padded[k * own : k * own + own + 2 * HALO] for k in range(parts)])
    return lax.all_to_all(windows, "chan", 0, 0, tiled=True)


def halves(axis):
    step = lax.axis_size(axis) // 2
    steps = []
    while step:
        steps.append(step)
        step //= 2
    return steps


def scatter_sum(block, axis):
    size = lax.axis_size(axis)
    for step in halves(axis):
        half = block.shape[0] // 2
        mine = (lax.axis_index(axis) // step) % 2
        send = lax.dynamic_slice_in_dim(block, (1 - mine) * half, half, 0)
        keep = lax.dynamic_slice_in_dim(block, mine * half, half, 0)
        came = lax.ppermute(send, axis, [(i, i ^ step) for i in range(size)])
        block = (keep.astype(F32) + came.astype(F32)).astype(BF16)
    return block


def sigmoid(z):
    return 1.0 / (1.0 + jnp.exp(-z))


def shifts(flat):
    rows = flat.shape[0]
    bins = lax.broadcasted_iota(jnp.int32, flat.shape, 0) % B1
    below = jnp.where(bins == 0, 0.0, pltpu.roll(flat, 1, 0))
    above = jnp.where(bins == B1 - 1, 0.0, pltpu.roll(flat, rows - 1, 0))
    return below, above


def fit(count, target, unit=1):
    return max([k for k in range(unit, target + 1, unit) if count % k == 0], default=count)


def loop(low, high, target, body, unit=1):
    chunk = fit(high - low, target, unit)

    def step(i, carry):
        body(low + i * chunk, chunk)
        return carry

    if chunk == high - low:
        body(low, chunk)
    else:
        lax.fori_loop(0, (high - low) // chunk, step, 0)


def mask_frames(partial, mask_ref, base, chunk):
    cube = partial.reshape(chunk, B1, partial.shape[-1])
    return jnp.concatenate([cube[k] * mask_ref[base + k] for k in range(chunk)], axis=0)


def taps_sum(cols_ref, taps_ref, masks, base, chunk):
    total = None
    for tap in (1, 0, 2):
        rows = cols_ref[pl.ds(base + tap - 1, chunk)].reshape(chunk * B1, cols_ref.shape[-1])
        partial = jnp.dot(rows, taps_ref[tap], preferred_element_type=F32)
        if tap == 0:
            partial = mask_frames(partial, masks[0], base, chunk)
        if tap == 2:
            partial = mask_frames(partial, masks[1], base, chunk)
        total = partial if total is None else total + partial
    return total


def own_rows(value, base, chunk, low, high):
    frame = base + lax.broadcasted_iota(jnp.int32, value.shape, 0) // B1
    return jnp.where((frame >= low) & (frame < high), value, 0.0)


def add_sums(sums_ref, first, second):
    rows, channels = first.shape
    sums_ref[0] += jnp.sum(first.reshape(rows // 8, 8, channels), axis=0)
    sums_ref[1] += jnp.sum(second.reshape(rows // 8, 8, channels), axis=0)


def rows_of(ref, base, chunk):
    return ref[pl.ds(base, chunk)].reshape(chunk * B1, ref.shape[-1])


def put(ref, base, chunk, value):
    ref[pl.ds(base, chunk)] = value.reshape(chunk, B1, value.shape[-1]).astype(ref.dtype)


def normal(values, vec_ref):
    return (values - vec_ref[0:1]) * vec_ref[1:2]


def transposed(rows):
    channels = rows.shape[1]
    eye = (
        lax.broadcasted_iota(jnp.int32, (channels, channels), 0)
        == lax.broadcasted_iota(jnp.int32, (channels, channels), 1)
    ).astype(BF16)
    return lax.dot_general(
        eye, rows, (((1,), (1,)), ((), ())), preferred_element_type=F32
    ).astype(BF16)


def first_kernel(own, prev_ref, next_ref, x_ref, vec_ref, taps_ref, short_ref, h_ref, s_ref, a_ref, sums_ref, cols_ref):
    total = x_ref.shape[1]

    def build(base, chunk):
        acts = []
        for parity in range(2):
            flat = rows_of(x_ref.at[parity], base, chunk).astype(F32)
            z = normal(flat, vec_ref) * vec_ref[2:3] + vec_ref[3:4]
            act = z * sigmoid(z)
            put(a_ref.at[parity], base, chunk, act)
            acts.append(act)
        below, _ = shifts(acts[1])
        put(cols_ref, base, chunk, jnp.concatenate([below, acts[0], acts[1]], axis=1))

    loop(0, total, 8, build)
    sums_ref[...] = jnp.zeros_like(sums_ref)

    def conv(base, chunk):
        result = taps_sum(cols_ref, taps_ref, (prev_ref, next_ref), base, chunk)
        put(h_ref, base, chunk, result)
        mine = own_rows(result, base, chunk, HALO, HALO + own)
        add_sums(sums_ref, mine, mine * mine)
        short = jnp.dot(rows_of(a_ref.at[0], base, chunk), short_ref[...], preferred_element_type=F32)
        put(s_ref, base, chunk, short)

    loop(1, total - 1, 47, conv)


def forward_kernel(own, lead, chunk, with_short, prev_ref, next_ref, h_ref, vec_ref, taps_ref, *rest):
    if with_short:
        s_ref, out_ref, a_ref, sums_ref, cols_ref = rest
    else:
        out_ref, a_ref, sums_ref, cols_ref = rest
    total = h_ref.shape[0]
    activate_into(h_ref, vec_ref, a_ref, cols_ref, lead - 1)
    sums_ref[...] = jnp.zeros_like(sums_ref)

    def conv(base, chunk):
        result = taps_sum(cols_ref, taps_ref, (prev_ref, next_ref), base, chunk)
        if with_short:
            result = result + rows_of(s_ref, base, chunk)
        put(out_ref, base, chunk, result)
        mine = own_rows(result, base, chunk, HALO, HALO + own)
        add_sums(sums_ref, mine, mine * mine)

    loop(lead, total - lead, chunk, conv)


def activate_into(h_ref, vec_ref, a_ref, cols_ref, lead):
    total = h_ref.shape[0]

    def build(base, chunk):
        flat = rows_of(h_ref, base, chunk)
        z = normal(flat, vec_ref) * vec_ref[2:3] + vec_ref[3:4]
        act = z * sigmoid(z)
        put(a_ref, base, chunk, act)
        below, above = shifts(act)
        put(cols_ref, base, chunk, jnp.concatenate([below, act, above], axis=1))

    loop(lead, total - lead, 2, build)


def back_through(q, values, vec_ref):
    xhat = normal(values, vec_ref)
    z = xhat * vec_ref[2:3] + vec_ref[3:4]
    gate = sigmoid(z)
    return q * gate * (1.0 + z * (1.0 - gate)), xhat


def weight_grad(own, u_ref, cols_ref, masks, out_ref, turned_ref):
    rows = own * B1
    for tap in range(3):
        def turn(base, chunk):
            u = u_ref[pl.ds(HALO + base, chunk)].reshape(chunk * B1, u_ref.shape[-1])
            if tap != 1:
                u = mask_frames(u.astype(F32), masks[0 if tap == 0 else 1], HALO + base, chunk).astype(BF16)
            turned_ref[:, pl.ds(pl.multiple_of(base * B1, chunk * B1), chunk * B1)] = transposed(u)

        loop(0, own, 12, turn, 4)
        other = cols_ref[pl.ds(HALO + 1 - tap, own)].reshape(rows, cols_ref.shape[-1])
        out_ref[tap] = jnp.dot(turned_ref[...], other, preferred_element_type=F32).astype(out_ref.dtype)


def shift_into(value, base, chunk, cols_ref):
    below, above = shifts(value)
    put(cols_ref, base, chunk, jnp.concatenate([above, value, below], axis=1))


def last_kernel(
    own, prev_ref, next_ref, h_ref, x_ref, e_ref, vec_ref, taps_ref, turned_taps_ref,
    y_ref, dz_ref, sums_ref, grad_ref, cols_ref, a_ref, turned_ref,
):
    total = h_ref.shape[0]
    activate_into(h_ref, vec_ref, a_ref, cols_ref, 3)

    def conv(base, chunk):
        result = taps_sum(cols_ref, taps_ref, (prev_ref, next_ref), base, chunk) + rows_of(x_ref, base, chunk)
        put(y_ref, base - HALO, chunk, result)

    loop(HALO, HALO + own, 12, conv)

    def build(base, chunk):
        shift_into(rows_of(e_ref, base, chunk).astype(F32), base, chunk, cols_ref)

    loop(2, total - 2, 2, build)
    sums_ref[...] = jnp.zeros_like(sums_ref)

    def back(base, chunk):
        q = taps_sum(cols_ref, turned_taps_ref, (prev_ref, next_ref), base, chunk)
        dz, xhat = back_through(q, rows_of(h_ref, base, chunk), vec_ref)
        put(dz_ref, base, chunk, dz)
        mine = own_rows(dz, base, chunk, HALO, HALO + own)
        add_sums(sums_ref, mine, mine * xhat)

    loop(3, total - 3, 15, back)
    weight_grad(own, a_ref, cols_ref, (next_ref, prev_ref), grad_ref, turned_ref)


def middle_kernel(
    own, lead, chunk, with_top, prev_ref, next_ref, dz_ref, h_ref, low_ref, u_ref, vec_ref, coef_ref, low_vec_ref, turned_taps_ref, *rest,
):
    if with_top:
        e_ref, even_ref, dz_out_ref, sums_ref, grad_ref, short_ref, e1_ref, cols_ref, turned_ref = rest
    else:
        dz_out_ref, sums_ref, grad_ref, cols_ref, turned_ref = rest
    total = h_ref.shape[0]

    def build(base, size):
        xhat = normal(rows_of(h_ref, base, size), vec_ref)
        d = vec_ref[2:3] * vec_ref[1:2] * (rows_of(dz_ref, base, size) - coef_ref[0:1] - xhat * coef_ref[1:2])
        if with_top:
            d = d + rows_of(e_ref, base, size).astype(F32)
            put(e1_ref, base, size, d)
        shift_into(d, base, size, cols_ref)

    loop(lead - 1, total - lead + 1, 2, build)
    sums_ref[...] = jnp.zeros_like(sums_ref)

    def back(base, chunk):
        q = taps_sum(cols_ref, turned_taps_ref, (prev_ref, next_ref), base, chunk)
        dz, xhat = back_through(q, rows_of(low_ref, base, chunk), low_vec_ref)
        put(dz_out_ref, base, chunk, dz)
        mine = own_rows(dz, base, chunk, HALO, HALO + own)
        add_sums(sums_ref, mine, mine * xhat)

    loop(lead, total - lead, chunk, back)
    weight_grad(own, u_ref, cols_ref, (next_ref, prev_ref), grad_ref, turned_ref)
    if with_top:
        rows = own * B1
        def turn(base, size):
            u = even_ref[pl.ds(HALO + base, size)].reshape(size * B1, even_ref.shape[-1])
            turned_ref[0 : even_ref.shape[-1], pl.ds(pl.multiple_of(base * B1, size * B1), size * B1)] = transposed(u)

        loop(0, own, 12, turn, 4)
        short_ref[...] = jnp.dot(
            turned_ref[0 : even_ref.shape[-1]],
            e1_ref[pl.ds(HALO, own)].reshape(rows, e1_ref.shape[-1]),
            preferred_element_type=F32,
        ).astype(BF16)


def bottom_kernel(
    own, prev_ref, next_ref, dz_ref, h_ref, x_ref, a_ref, e1_ref, vec_ref, coef_ref, low_vec_ref, turned_taps_ref, turned_short_ref,
    dz_out_ref, sums_ref, grad_ref, cols_ref, turned_ref,
):
    total = h_ref.shape[0]

    def build(base, size):
        xhat = normal(rows_of(h_ref, base, size), vec_ref)
        d = vec_ref[2:3] * vec_ref[1:2] * (rows_of(dz_ref, base, size) - coef_ref[0:1] - xhat * coef_ref[1:2])
        _, above = shifts(d)
        put(cols_ref, base, size, jnp.concatenate([d, above], axis=1))

    loop(HALO - 1, total - HALO + 1, 2, build)
    sums_ref[...] = jnp.zeros_like(sums_ref)
    half = x_ref.shape[-1]

    def back(base, chunk):
        q = taps_sum(cols_ref, turned_taps_ref, (prev_ref, next_ref), base, chunk)
        r = jnp.dot(rows_of(e1_ref, base, chunk), turned_short_ref[...], preferred_element_type=F32)
        parts = (q[:, :half] + r, q[:, half:])
        for parity in range(2):
            dz, xhat = back_through(parts[parity], rows_of(x_ref.at[parity], base, chunk).astype(F32), low_vec_ref)
            put(dz_out_ref.at[parity], base - HALO, chunk, dz)
            add_sums(sums_ref, dz, dz * xhat)

    loop(HALO, HALO + own, 12, back)
    rows = own * B1
    for tap in range(3):
        def turn(base, chunk):
            for parity in range(2):
                u = a_ref[parity, pl.ds(HALO + base, chunk)].reshape(chunk * B1, half)
                if tap != 1:
                    u = mask_frames(u.astype(F32), next_ref if tap == 0 else prev_ref, HALO + base, chunk).astype(BF16)
                turned_ref[parity * half : parity * half + half, pl.ds(pl.multiple_of(base * B1, chunk * B1), chunk * B1)] = transposed(u)

        loop(0, own, 12, turn, 4)
        other = cols_ref[pl.ds(HALO + 1 - tap, own)].reshape(rows, cols_ref.shape[-1])
        grad_ref[tap] = jnp.dot(turned_ref[...], other, preferred_element_type=F32).astype(grad_ref.dtype)


def input_kernel(own, dz_ref, x_ref, vec_ref, coef_ref, g_ref):
    def build(base, chunk):
        for parity in range(2):
            xhat = normal(rows_of(x_ref.at[parity], HALO + base, chunk).astype(F32), vec_ref)
            dz = rows_of(dz_ref.at[parity], base, chunk)
            g = vec_ref[2:3] * vec_ref[1:2] * (dz - coef_ref[0:1] - xhat * coef_ref[1:2])
            put(g_ref.at[parity], base, chunk, g)

    loop(0, own, 4, build)


SMEM = pl.BlockSpec(memory_space=pltpu.SMEM)
VMEM = pl.BlockSpec(memory_space=pltpu.VMEM)


def run(kernel, masks, operands, outs, scratch):
    return pl.pallas_call(
        kernel,
        in_specs=[SMEM] * len(masks) + [VMEM] * len(operands),
        out_specs=[VMEM] * len(outs),
        out_shape=[jax.ShapeDtypeStruct(shape, kind) for shape, kind in outs],
        scratch_shapes=[pltpu.VMEM(shape, kind) for shape, kind in scratch],
        compiler_params=pltpu.CompilerParams(vmem_limit_bytes=VMEM_BYTES),
    )(*masks, *operands)


def norm_pair(params, norm_index):
    if norm_index == 0:
        return (params[0, 0], params[1, 0])
    row_pair = params[:, 2 * norm_index - 1 : 2 * norm_index + 1]
    packed = jnp.transpose(row_pair, (0, 2, 1)).reshape(2, -1)
    return (packed[0], packed[1])


def pack_norms(vectors):
    blocks = [vectors[0][None]]
    for vector in vectors[1:]:
        blocks.append(vector.reshape(-1, 2).T)
    return jnp.concatenate(blocks, axis=0)


def adam_step(weight, moment, square, gradient, step_rate, decay_rate):
    moment_next = beta_first * moment + (1.0 - beta_first) * gradient
    square_next = beta_second * square + (1.0 - beta_second) * gradient * gradient
    corrected = moment_next / (1.0 - beta_first**STEP)
    divisor = jnp.sqrt(square_next / (1.0 - beta_second**STEP)) + adam_epsilon
    weight_next = weight - step_rate * (corrected / divisor + decay_rate * weight)
    return (weight_next, moment_next, square_next)


def vectors(sums, count, pair):
    average = sums[0] / count
    spread = lax.rsqrt(sums[1] / count - average * average + norm_epsilon)
    return jnp.stack([average, spread, pair[0], pair[1]])


def body(
    signal,
    clip_ids,
    output_grad,
    first_weight,
    first_mean,
    first_square,
    wide_weight,
    wide_mean,
    wide_square,
    norm_params,
    norm_mean,
    norm_square,
):
    chan_count = lax.axis_size("chan")
    frame_count = lax.axis_size("frames")
    chan = lax.axis_index("chan")
    group = signal.shape[0]
    own = group // chan_count
    total = own + 2 * HALO
    frames = group * frame_count
    in_local = signal.shape[1] // B0
    in_channels = in_local * chan_count
    wide_local = output_grad.shape[1] // B1
    wide = wide_local * chan_count

    ids = frame_edges(clip_ids + 1, HALO + 1)
    ids = lax.dynamic_slice_in_dim(ids, chan * own, total + 2, 0)
    prev_mask = (ids[:-2] == ids[1:-1]).astype(F32)
    next_mask = (ids[2:] == ids[1:-1]).astype(F32)
    masks = (prev_mask, next_mask)

    local = signal.astype(F32).reshape(group, in_local, B0)
    local_sums = jnp.stack([jnp.sum(local, axis=(0, 2)), jnp.sum(local * local, axis=(0, 2))])
    placed = lax.dynamic_update_slice(jnp.zeros((2, in_channels), F32), local_sums, (0, chan * in_local))
    sums_zero = total_sum(placed)

    came = to_frames(signal).reshape(chan_count, total, in_local, B1, 2)
    x_zero = jnp.transpose(came, (4, 1, 3, 0, 2)).reshape(2, total, B1, in_channels)
    came = to_frames(output_grad).reshape(chan_count, total, wide_local, B1)
    top = jnp.transpose(came, (1, 3, 0, 2)).reshape(total, B1, wide)

    columns = first_weight.shape[1]
    first_all = lax.all_gather(first_weight.astype(BF16), ("frames", "chan"), axis=0)
    first_all = first_all.reshape(frame_count, chan_count, -1, columns)
    first_all = jnp.transpose(first_all, (0, 2, 1, 3)).reshape(-1, chan_count * columns)
    wide_all = lax.all_gather(wide_weight.astype(BF16), ("frames", "chan"), axis=0)
    wide_all = wide_all.reshape(frame_count, chan_count, 3, -1, 9, columns)
    wide_all = jnp.transpose(wide_all, (2, 4, 0, 3, 1, 5)).reshape(3, 9, wide, wide)
    first_taps = jnp.transpose(first_all[: 9 * in_channels].reshape(in_channels, 9, wide), (1, 0, 2))
    short_taps = first_all[9 * in_channels :]
    taps_one = first_taps.reshape(3, 3 * in_channels, wide)
    taps = [wide_all[k].reshape(3, 3 * wide, wide) for k in range(3)]
    turned = jnp.transpose(wide_all, (0, 1, 3, 2)).reshape(3, 3, 3, wide, wide)
    turned = [turned[k][::-1].reshape(3, 3 * wide, wide) for k in range(3)]
    back_first = jnp.transpose(first_taps, (0, 2, 1)).reshape(3, 3, wide, in_channels)[::-1]
    turned_one = jnp.concatenate(
        [
            jnp.concatenate([back_first[:, 1], back_first[:, 2]], axis=2),
            jnp.concatenate([jnp.zeros_like(back_first[:, 0]), back_first[:, 0]], axis=2),
        ],
        axis=1,
    )
    turned_short = short_taps.T

    params = lax.all_gather(norm_params, "chan", axis=2, tiled=True)
    pairs = [norm_pair(params, k) for k in range(4)]

    count_zero = frames * B0
    count = frames * B1
    cube = (total, B1, wide)
    cols = (total, B1, 3 * wide)
    turned_shape = (wide, own * B1)

    def gathered(sums):
        return total_sum(jnp.sum(sums, axis=1))

    vec_zero = vectors(sums_zero, count_zero, pairs[0])
    hidden_one, shortcut, act_one, sums = run(
        functools.partial(first_kernel, own),
        masks,
        (x_zero, vec_zero, taps_one, short_taps),
        [(cube, F32), (cube, F32), ((2, total, B1, in_channels), BF16), ((2, 8, wide), F32)],
        [((total, B1, 3 * in_channels), BF16)],
    )
    vec_one = vectors(gathered(sums), count, pairs[1])
    residual, mid_one, sums = run(
        functools.partial(forward_kernel, own, 2, 23, True),
        masks,
        (hidden_one, vec_one, taps[0], shortcut),
        [(cube, F32), (cube, BF16), ((2, 8, wide), F32)],
        [(cols, BF16)],
    )
    vec_two = vectors(gathered(sums), count, pairs[2])
    hidden_two, act_two, sums = run(
        functools.partial(forward_kernel, own, 3, 15, False),
        masks,
        (residual, vec_two, taps[1]),
        [(cube, F32), (cube, BF16), ((2, 8, wide), F32)],
        [(cols, BF16)],
    )
    vec_three = vectors(gathered(sums), count, pairs[3])
    block_cube, dz_three, sums_three, grad_four = run(
        functools.partial(last_kernel, own),
        masks,
        (hidden_two, residual, top, vec_three, taps[2], turned[2]),
        [((own, B1, wide), BF16), (cube, F32), ((2, 8, wide), F32), ((3, wide, 3 * wide), BF16)],
        [(cols, BF16), (cube, BF16), (turned_shape, BF16)],
    )
    norm_three = gathered(sums_three)
    dz_two, sums_two, grad_three = run(
        functools.partial(middle_kernel, own, 4, 11, False),
        masks,
        (dz_three, hidden_two, residual, act_two, vec_three, norm_three / count, vec_two, turned[1]),
        [(cube, F32), ((2, 8, wide), F32), ((3, wide, 3 * wide), BF16)],
        [(cols, BF16), (turned_shape, BF16)],
    )
    norm_two = gathered(sums_two)
    dz_one, sums_one, grad_two, grad_short, low_top = run(
        functools.partial(middle_kernel, own, 5, 43, True),
        masks,
        (dz_two, residual, hidden_one, mid_one, vec_two, norm_two / count, vec_one, turned[0], top, act_one[0]),
        [(cube, F32), ((2, 8, wide), F32), ((3, wide, 3 * wide), BF16), ((in_channels, wide), BF16), (cube, BF16)],
        [(cols, BF16), (turned_shape, BF16)],
    )
    norm_one = gathered(sums_one)
    dz_zero, sums_last, grad_one = run(
        functools.partial(bottom_kernel, own),
        masks,
        (dz_one, hidden_one, x_zero, act_one, low_top, vec_one, norm_one / count, vec_zero, turned_one, turned_short),
        [((2, own, B1, in_channels), F32), ((2, 8, in_channels), F32), ((3, 2 * in_channels, 2 * wide), BF16)],
        [((total, B1, 2 * wide), BF16), ((2 * in_channels, own * B1), BF16)],
    )
    norm_zero = gathered(sums_last)
    (input_cube,) = run(
        functools.partial(input_kernel, own),
        (),
        (dz_zero, x_zero, vec_zero, norm_zero / count_zero),
        [((2, own, B1, in_channels), BF16)],
        [],
    )

    out = jnp.transpose(block_cube.reshape(own, B1, chan_count, wide_local), (2, 0, 3, 1))
    out = lax.all_to_all(out.reshape(chan_count, own, wide_local * B1), "chan", 0, 0, tiled=True)
    block_out = out.reshape(group, -1).astype(F32)
    out = jnp.transpose(input_cube.reshape(2, own, B1, chan_count, in_local), (3, 1, 4, 2, 0))
    out = lax.all_to_all(out.reshape(chan_count, own, in_local * B0), "chan", 0, 0, tiled=True)
    input_grad = out.reshape(group, -1).astype(F32)

    def split_columns(rows):
        return jnp.transpose(rows.reshape(rows.shape[0], chan_count, columns), (1, 0, 2))

    g = grad_one.reshape(3, 2, in_channels, 2, wide)
    g = jnp.stack([g[:, 1, :, 1], g[:, 0, :, 0], g[:, 1, :, 0]], axis=1).reshape(9, in_channels, wide)
    g = jnp.concatenate([jnp.transpose(g, (1, 0, 2)).reshape(-1, wide), grad_short], axis=0)
    parts = split_columns(g).reshape(chan_count, frame_count, -1, columns)
    layers = []
    for grad in (grad_two, grad_three, grad_four):
        rows = jnp.transpose(grad.reshape(3, wide, 3, wide), (1, 0, 2, 3)).reshape(-1, wide)
        layers.append(split_columns(rows).reshape(chan_count, frame_count, -1, columns))
    parts = jnp.concatenate([parts] + layers, axis=2)
    mine = scatter_sum(parts, "chan")[0]
    mine = scatter_sum(mine, "frames")[0].astype(F32)
    grad_first = mine[: first_weight.shape[0]]
    grad_wide = mine[first_weight.shape[0] :].reshape(wide_weight.shape)

    norm_sums = [norm_zero, norm_one, norm_two, norm_three]
    grad_norms = jnp.stack([pack_norms([s[1] for s in norm_sums]), pack_norms([s[0] for s in norm_sums])])
    grad_norms = lax.dynamic_slice_in_dim(grad_norms, chan * norm_params.shape[2], norm_params.shape[2], 2)
    own_squares = jnp.sum(grad_first * grad_first) + jnp.sum(grad_wide * grad_wide)
    own_squares = own_squares + jnp.where(lax.axis_index("frames") == 0, jnp.sum(grad_norms * grad_norms), 0.0)
    squares = total_sum(jnp.broadcast_to(own_squares, (1, 128)))[0, 0]
    grad_norm = jnp.sqrt(squares)
    factor = clip_limit / jnp.maximum(grad_norm, clip_limit)
    first_next, first_mean_next, first_square_next = adam_step(
        first_weight, first_mean, first_square, grad_first * factor, conv_rate, weight_decay
    )
    wide_next, wide_mean_next, wide_square_next = adam_step(
        wide_weight, wide_mean, wide_square, grad_wide * factor, conv_rate, weight_decay
    )
    norm_next, norm_mean_next, norm_square_next = adam_step(
        norm_params, norm_mean, norm_square, grad_norms * factor, norm_rate, 0.0
    )
    return (
        block_out,
        input_grad,
        grad_norm,
        first_next,
        first_mean_next,
        first_square_next,
        first_next.astype(BF16),
        wide_next,
        wide_mean_next,
        wide_square_next,
        wide_next.astype(BF16),
        norm_next,
        norm_mean_next,
        norm_square_next,
    )


def solution(mesh):
    rows = P("frames", "chan")
    deep = P(None, "frames", "chan")
    norms = P(None, None, "chan")
    in_specs = (rows, P("frames"), rows, rows, rows, rows, deep, deep, deep, norms, norms, norms)
    out_specs = (rows, rows, P(), rows, rows, rows, rows, deep, deep, deep, deep, norms, norms, norms)
    return jax.shard_map(body, mesh=mesh, in_specs=in_specs, out_specs=out_specs, check_vma=False)
```

```python
import functools
import math

import jax
import jax.numpy as jnp
from jax import lax
from jax.experimental import pallas as pl
from jax.experimental.pallas import tpu as pltpu
from jax.sharding import PartitionSpec as P

B0 = 64
STEP = 10
B1 = 32
HALO = 6
LANES = 128

norm_epsilon = 1e-05
clip_limit = 100.0
beta_first = 0.9
beta_second = 0.999
adam_epsilon = 1e-08
conv_rate = 0.05
norm_rate = 0.5
weight_decay = 0.01

BOTH = ("chan", "frames")
VMEM_BYTES = 58 * 1024 * 1024
F32 = jnp.float32
BF16 = jnp.bfloat16
NT = (((1,), (1,)), ((), ()))


def to_all(copies):
    return lax.all_to_all(copies, BOTH, 0, 0, tiled=True)


def to_frames(block):
    parts = lax.axis_size("chan")
    count = lax.axis_size("frames")
    chan = lax.axis_index("chan")
    own = block.shape[0] // parts
    forward = [(i, i + 1) for i in range(count - 1)]
    backward = [(b, a) for a, b in forward]
    padded = jnp.pad(block, ((HALO, HALO), (0, 0), (0, 0)))
    windows = [lax.dynamic_slice_in_dim(padded, (chan ^ d) * own, own + 2 * HALO, 0) for d in range(parts)]
    swaps = [[(i, i ^ d) for i in range(parts)] for d in range(parts)]
    came = list(windows)
    for d in range(parts - 1, 0, -1):
        came[d] = lax.ppermute(windows[d], "chan", swaps[d])
    low = lax.ppermute(block[block.shape[0] - HALO :], "frames", forward)
    high = lax.ppermute(block[:HALO], "frames", backward)
    edge = jnp.concatenate([low, high], axis=0)
    edges = [edge] + [lax.ppermute(edge, "chan", swaps[d]) for d in range(1, parts)]
    return came, edges, windows


def halves(axis, size):
    steps = []
    while size > 1:
        size //= 2
        steps.append((axis, size))
    return steps


def code_of(order, place):
    return sum(((place[axis] // step) % 2) << k for k, (axis, step) in enumerate(order))


def scatter_steps(keeps, sends, order):
    steps = order[::-1]
    for number, (axis, step) in enumerate(steps):
        size = lax.axis_size(axis)
        swap = [(i, i ^ step) for i in range(size)]
        came = [lax.ppermute(send, axis, swap) for send in sends]
        half = keeps[0].shape[0] // 2

        def added(part):
            return jnp.concatenate([(k[part].astype(F32) + c[part].astype(F32)).astype(BF16) for k, c in zip(keeps, came)], axis=1)

        if number + 1 == len(steps):
            return added(slice(None))[0]
        keeps, sends = [added(slice(0, half))], [added(slice(half, None))]


def after(value, *others):
    return lax.optimization_barrier((value, *others))[0]


def fit(count, target, unit=1):
    return max([k for k in range(unit, target + 1, unit) if count % k == 0], default=count)


def loop(low, high, target, body, unit=1):
    return spans(low, high - low, target, body, unit)


def spans(low, count, target, body, unit=1):
    chunk = fit(count, target, unit)

    def step(i, carry):
        body(low + i * chunk, chunk, i)
        return carry

    if chunk == count:
        body(low, chunk, 0)
    else:
        lax.fori_loop(0, count // chunk, step, 0)
    return chunk


class Fetched:
    def __init__(self, source, ref, sems):
        self.source, self.ref, self.sems = source, ref, sems
        self.pieces = sems.shape[0]
        self.size = ref.shape[0] // self.pieces

    def copy(self, number):
        rows = pl.ds(number * self.size, self.size)
        return pltpu.make_async_copy(self.source.at[rows], self.ref.at[rows], self.sems.at[number])

    def start(self):
        for number in range(self.pieces):
            self.copy(number).start()

    def need(self, number):
        self.copy(number).wait()

    def need_all(self):
        for number in range(self.pieces):
            self.need(number)


class Sent:
    def __init__(self, target, ref, sems):
        self.target, self.ref, self.sems = target, ref, sems
        self.shape, self.dtype = ref.shape, ref.dtype

    def copy(self, base, chunk, number):
        rows = pl.ds(base, chunk)
        return pltpu.make_async_copy(self.ref.at[rows], self.target.at[rows], self.sems.at[number])

    def send(self, base, chunk, number):
        self.copy(base, chunk, number).start()

    def finish(self, low, high, chunk):
        for number in range((high - low) // chunk):
            self.copy(low + number * chunk, chunk, number).wait()


def sigmoid(z):
    return 0.5 * jnp.tanh(0.5 * z) + 0.5


def dot(a, b):
    return jnp.dot(a, b, preferred_element_type=F32)


def dot_nt(a, b):
    return lax.dot_general(a, b, NT, preferred_element_type=F32)


def chosen(rows, columns, source):
    r = lax.broadcasted_iota(jnp.int32, (rows, columns), 0)
    c = lax.broadcasted_iota(jnp.int32, (rows, columns), 1)
    return (c == source(r)).astype(BF16)


def same(r):
    return r


def transposed(rows):
    return dot_nt(chosen(rows.shape[1], rows.shape[1], same), rows).astype(BF16)


def shifts(flat):
    rows = flat.shape[0]
    bins = lax.broadcasted_iota(jnp.int32, flat.shape, 0) % B1
    below = jnp.where(bins == 0, 0.0, pltpu.roll(flat, 1, 0))
    above = jnp.where(bins == B1 - 1, 0.0, pltpu.roll(flat, rows - 1, 0))
    return below, above


def mask_frames(partial, mask_ref, base, chunk):
    cube = partial.reshape(chunk, B1, partial.shape[-1])
    return jnp.concatenate([cube[k] * mask_ref[base + k] for k in range(chunk)], axis=0)


def rows_of(ref, base, chunk):
    return ref[pl.ds(base, chunk)].reshape(chunk * B1, ref.shape[-1])


def put(ref, base, chunk, value):
    ref[pl.ds(base, chunk)] = value.reshape(chunk, B1, value.shape[-1]).astype(ref.dtype)


def taps_sum(cols_ref, taps_ref, masks, base, chunk, product=dot):
    total = None
    for tap in (1, 0, 2):
        partial = product(rows_of(cols_ref, base + tap - 1, chunk), taps_ref[tap])
        if tap == 0:
            partial = mask_frames(partial, masks[0], base, chunk)
        if tap == 2:
            partial = mask_frames(partial, masks[1], base, chunk)
        total = partial if total is None else total + partial
    return total


def own_rows(value, base, chunk, low, high):
    frame = base + lax.broadcasted_iota(jnp.int32, value.shape, 0) // B1
    return jnp.where((frame >= low) & (frame < high), value, 0.0)


def add_sums(acc_ref, first, second):
    rows, channels = first.shape
    acc_ref[0] += jnp.sum(first.reshape(rows // 8, 8, channels), axis=0)
    acc_ref[1] += jnp.sum(second.reshape(rows // 8, 8, channels), axis=0)


def spread_sums(acc_ref, copies_ref):
    channels = acc_ref.shape[-1]
    for k in range(2):
        row = jnp.sum(acc_ref[k], axis=0, keepdims=True)
        copies_ref[:, :, k * channels : (k + 1) * channels] = jnp.broadcast_to(
            row[None], (copies_ref.shape[0], 1, channels)
        )


def came_sums(came_ref):
    total = jnp.sum(came_ref[...], axis=0)
    half = total.shape[-1] // 2
    return total[:, :half], total[:, half:]


def norm_of(came_ref, pair_ref, count):
    first, second = came_sums(came_ref)
    mean = first / count
    spread = lax.rsqrt(second / count - mean * mean + norm_epsilon)
    return mean, spread, pair_ref[0:1], pair_ref[1:2]


def norm_rows(vec_ref):
    return vec_ref[0:1], vec_ref[1:2], vec_ref[2:3], vec_ref[3:4]


def normal(values, norm):
    return (values.astype(F32) - norm[0]) * norm[1]


def activated(values, norm):
    z = normal(values, norm) * norm[2] + norm[3]
    return z * sigmoid(z)


def back_act(q, values, norm):
    xhat = normal(values, norm)
    z = xhat * norm[2] + norm[3]
    gate = sigmoid(z)
    return q * gate * (1.0 + z * (1.0 - gate)), xhat


def back_norm(dz, values, norm, sums, count):
    xhat = normal(values, norm)
    return norm[2] * norm[1] * (dz.astype(F32) - sums[0] / count - xhat * (sums[1] / count))


def swap_halves(value):
    return pltpu.roll(value, LANES // 2, 1)


def halves_of(first, second):
    low = lax.broadcasted_iota(jnp.int32, first.shape, 1) < LANES // 2
    return jnp.where(low, first, swap_halves(second)), jnp.where(low, swap_halves(first), second)


def unpack_wide(layer, chans, all_ref, taps_out, came_ref, sems):
    fetch = pltpu.make_async_copy(all_ref.at[:, layer], came_ref, sems.at[0])
    fetch.start()
    devices, groups, rows, _ = came_ref.shape
    taps_ref = taps_out.ref
    count = devices // chans
    per = LANES // (taps_ref.shape[2] // chans)
    wide = per * LANES
    piece = LANES // per
    spread = chosen(wide, wide, lambda r: (r % LANES) // piece * LANES + r // LANES * piece + r % piece)
    fetch.wait()
    for frame in range(count):
        for side in range(chans // per):
            parts = []
            for k in range(per):
                parts.append(came_ref[frame * chans + side * per + k].reshape(groups * rows, LANES))
            result = dot_nt(jnp.concatenate(parts, axis=1), spread).astype(BF16)
            for slab in range(per):
                for group in range(groups):
                    if slab * groups + group < 9:
                        taps_ref[slab * groups + group, frame * rows : (frame + 1) * rows, side * LANES : (side + 1) * LANES] = result[
                            group * rows : (group + 1) * rows, slab * LANES : (slab + 1) * LANES
                        ]
    taps_out.send(0, 9, 0)
    taps_out.finish(0, 9, 9)


def turn_taps(taps, turned_ref):
    wide = taps.ref.shape[-1]
    taps.need_all()
    for kt in range(3):
        for kf in range(3):
            turned_ref[2 - kt, :, kf * wide : (kf + 1) * wide] = taps.ref[kt, kf * wide : (kf + 1) * wide]


def pack_wide(order, chans, me_ref, slabs, out_ref):
    devices, groups, rows, _ = out_ref.shape
    count = devices // chans
    per = LANES // (slabs[0].shape[1] // chans)
    wide = per * LANES
    piece = LANES // per
    gather = chosen(wide, wide, lambda r: (r % LANES) // piece * LANES + r // LANES * piece + r % piece)
    for group in range(groups):
        for side in range(chans // per):
            parts = []
            for slab in range(per):
                tap = slab * groups + group
                tap = tap if tap < 9 else 8
                parts.append(slabs[tap][:, side * LANES : (side + 1) * LANES])
            result = dot_nt(jnp.concatenate(parts, axis=1), gather).astype(BF16)
            for k in range(per):
                for frame in range(count):
                    at = code_of(order, {"chan": side * per + k, "frames": frame}) ^ me_ref[0]
                    out_ref[at, group] = result[frame * rows : (frame + 1) * rows, k * LANES : (k + 1) * LANES]


def unpack_first(chans, shard, count_zero, came, taps_ref, short_ref, vec_ref, pairs_ref, raw_ref):
    came_ref = came.ref
    came.need_all()
    devices = came_ref.shape[0]
    count = devices // chans
    ins, outs = short_ref.shape
    per = LANES // (outs // chans)
    rows = packed_rows(shard, per)
    wide = per * LANES
    piece = LANES // per
    spread = chosen(wide, wide, lambda r: (r % LANES) // piece * LANES + r // LANES * piece + r % piece)
    for frame in range(count):
        for side in range(chans // per):
            parts = [came_ref[(side * per + k) * count + frame, 0:rows] for k in range(per)]
            result = dot_nt(jnp.concatenate(parts, axis=1), spread)
            for slab in range(per):
                start = slab * rows
                size = min(rows, shard - start)
                if size > 0:
                    raw_ref[side, frame * shard + start : frame * shard + start + size] = result[
                        :size, slab * LANES : (slab + 1) * LANES
                    ]
    for tap in range(9):
        kt, kf = tap // 3, tap % 3
        for side in range(outs // LANES):
            lanes = slice(side * LANES, (side + 1) * LANES)
            taps_ref[kt, kf * ins : (kf + 1) * ins, lanes] = raw_ref[side, pl.ds(tap, ins, stride=9)].astype(BF16)
    for side in range(outs // LANES):
        short_ref[:, side * LANES : (side + 1) * LANES] = raw_ref[side, 9 * ins : 10 * ins].astype(BF16)
    parts = [jnp.sum(came_ref[:, rows + 16 * k : rows + 16 * (k + 1)].astype(F32), axis=0) for k in range(2)]
    sums = parts[0] + parts[1]
    average = sums[0:1] / count_zero
    vec_ref[0:1] = average
    vec_ref[1:2] = lax.rsqrt(sums[1:2] / count_zero - average * average + norm_epsilon)
    vec_ref[2:3] = sums[2:3]
    vec_ref[3:4] = sums[9:10]
    c = lax.broadcasted_iota(jnp.int32, (LANES, 2 * LANES), 1)
    r = lax.broadcasted_iota(jnp.int32, (LANES, 2 * LANES), 0)
    for side in range(2):
        place = (c == 2 * r + side).astype(BF16)
        spread_rows = [dot(part.astype(BF16), place) for part in (parts[0], parts[1])]
        both = spread_rows[0] + spread_rows[1]
        for k in range(3):
            for kind in range(2):
                row = both[2 + 7 * kind + 1 + 2 * k + side : 2 + 7 * kind + 2 + 2 * k + side]
                pairs_ref[k, kind : kind + 1] = row if side == 0 else pairs_ref[k, kind : kind + 1] + row


def turn_first(taps, short, turned_ref):
    ins, outs = short.ref.shape
    taps.need_all()
    short.need_all()
    for kt in range(3):
        turned_ref[2 - kt, 0:ins, 0:outs] = taps.ref[kt, ins : 2 * ins]
        turned_ref[2 - kt, 0:ins, outs:] = jnp.zeros((ins, outs), BF16)
        turned_ref[2 - kt, ins:, 0:outs] = taps.ref[kt, 2 * ins :]
        turned_ref[2 - kt, ins:, outs:] = taps.ref[kt, 0:ins]


def pack_first(order, chans, shard, me_ref, raw_ref, out_ref):
    devices, rows, _ = out_ref.shape
    count = devices // chans
    outs = raw_ref.shape[0] * LANES
    per = LANES // (outs // chans)
    wide = per * LANES
    piece = LANES // per
    gather = chosen(wide, wide, lambda r: (r % LANES) // piece * LANES + r // LANES * piece + r % piece)
    for frame in range(count):
        for side in range(chans // per):
            parts = [raw_ref[side, frame * shard + slab * rows : frame * shard + (slab + 1) * rows] for slab in range(per)]
            result = dot_nt(jnp.concatenate(parts, axis=1).astype(BF16), gather).astype(BF16)
            for k in range(per):
                at = code_of(order, {"chan": side * per + k, "frames": frame}) ^ me_ref[0]
                out_ref[at] = result[:, k * LANES : (k + 1) * LANES]


def packed_rows(shard, per):
    return -(-shard // (per * 16)) * 16


def frames_in(chan_ref, mains, edge_refs, total, target, body):
    parts = len(mains)
    for main in mains:
        main.need_all()
    for low, at, part in ((0, 0, 0), (total - HALO, HALO, parts - 1)):

        @pl.when(chan_ref[0] == part)
        def _():
            for main, edge_ref in zip(mains, edge_refs):
                main.ref[low : low + HALO] = edge_ref[at : at + HALO]

    def piece(at, chunk, _):
        cubes = jnp.concatenate([main.ref[pl.ds(at, chunk)] for main in mains], axis=1)
        body(cubes.reshape(chunk * cubes.shape[1], LANES), at, chunk)

    loop(0, total, target, piece, 2)


def lane_row(chan_ref, q, size):
    return (q // size ^ chan_ref[0]) * size + q % size


def frames_out(rows, count, out_ref, at):
    parts, _, size, _ = out_ref.shape
    cube = rows.reshape(count, parts * size, LANES)
    for s in range(parts):
        out_ref[s, pl.ds(at, count)] = cube[:, s * size : (s + 1) * size].astype(out_ref.dtype)


def pieces_of(total):
    return fit(total, 4)


def channels_of(ref, base, chunk, parity):
    return ref[pl.ds(base, chunk), parity].reshape(chunk * B1, ref.shape[-1])


def signal_kernel(parts, chan_ref, *rest):
    mains, edge_refs, x_out = rest[:parts], rest[parts : 2 * parts], rest[2 * parts]
    x_ref = x_out.ref
    size = mains[0].ref.shape[1]
    total = x_ref.shape[0]
    channels = x_ref.shape[-1]
    half = LANES // 2
    split = chosen(LANES, LANES, lambda r: r // half * half + r % B1 * 2 + r % half // B1)
    order = chosen(channels, channels, lambda r: r // half + lane_row(chan_ref, r % half, size) * 2)

    def turn(values, base, chunk):
        turned = dot_nt(split, values)
        for parity in range(2):
            pairs = []
            for pair in range(chunk // 2):
                lanes = turned[:, pair * LANES : (pair + 1) * LANES]
                even = lanes[parity * B1 : (parity + 1) * B1]
                odd = lanes[half + parity * B1 : half + (parity + 1) * B1]
                pairs.extend(halves_of(even, odd))
            x = dot(jnp.concatenate(pairs, axis=0).astype(BF16), order)
            x_ref[pl.ds(base, chunk), parity] = x.reshape(chunk, B1, channels).astype(BF16)

    frames_in(chan_ref, mains, edge_refs, total, 48, turn)
    x_out.send(0, total, 0)
    x_out.finish(0, total, total)


def first_kernel(own, prev_ref, next_ref, x, taps, short, vec_ref, h_out, s_out, copies_ref, cols_ref, acc_ref):
    total = x.ref.shape[0]
    channels = x.ref.shape[-1]
    norm = norm_rows(vec_ref)

    def build(base, chunk):
        acts = [activated(channels_of(x.ref, base, chunk, parity), norm) for parity in range(2)]
        below, _ = shifts(acts[1])
        put(cols_ref, base, chunk, jnp.concatenate([below, acts[0], acts[1]], axis=1))

    by_pieces([x], total, 12, build)
    acc_ref[...] = jnp.zeros_like(acc_ref)
    taps.need_all()
    short.need_all()

    def conv(base, chunk, number):
        result = taps_sum(cols_ref, taps.ref, (prev_ref, next_ref), base, chunk)
        put(h_out.ref, base, chunk, result)
        h_out.send(base, chunk, number)
        mine = own_rows(result, base, chunk, HALO, HALO + own)
        add_sums(acc_ref, mine, mine * mine)
        even = rows_of(cols_ref, base, chunk)[:, channels : 2 * channels]
        put(s_out.ref, base, chunk, dot(even, short.ref[...]))
        s_out.send(base, chunk, number)

    chunk = loop(1, total - 1, 47, conv)
    spread_sums(acc_ref, copies_ref)
    h_out.finish(1, total - 1, chunk)
    s_out.finish(1, total - 1, chunk)


def by_pieces(fetched, total, target, body):
    pieces = fetched[0].pieces
    size = total // pieces

    def piece(number, carry):
        for operand in fetched:
            operand.need(number)
        spans(number * size, size, target, lambda base, chunk, _: body(base, chunk))
        return carry

    lax.fori_loop(0, pieces, piece, 0)


def activate_into(h, norm, cols_ref):
    def build(base, chunk):
        act = activated(rows_of(h.ref, base, chunk), norm)
        below, above = shifts(act)
        put(cols_ref, base, chunk, jnp.concatenate([below, act, above], axis=1))

    by_pieces([h], cols_ref.shape[0], 24, build)


def forward_kernel(own, count, lead, target, with_short, prev_ref, next_ref, h, taps, *rest):
    if with_short:
        s, came_ref, pair_ref, out, copies_ref, cols_ref, acc_ref = rest
    else:
        came_ref, pair_ref, out, copies_ref, cols_ref, acc_ref = rest
    total = cols_ref.shape[0]
    activate_into(h, norm_of(came_ref, pair_ref, count), cols_ref)
    acc_ref[...] = jnp.zeros_like(acc_ref)
    taps.need_all()

    def conv(base, chunk, number):
        result = taps_sum(cols_ref, taps.ref, (prev_ref, next_ref), base, chunk)
        if with_short:
            pl.when(number == 0)(s.need_all)
            result = result + rows_of(s.ref, base, chunk).astype(F32)
        put(out.ref, base, chunk, result)
        out.send(base, chunk, number)
        mine = own_rows(result, base, chunk, HALO, HALO + own)
        add_sums(acc_ref, mine, mine * mine)

    chunk = loop(lead, total - lead, target, conv)
    spread_sums(acc_ref, copies_ref)
    out.finish(lead, total - lead, chunk)


def shift_into(value, base, chunk, cols_ref):
    below, above = shifts(value)
    put(cols_ref, base, chunk, jnp.concatenate([above, value, below], axis=1))


def top_kernel(parts, chan_ref, *rest):
    mains, edge_refs, e_out = rest[:parts], rest[parts : 2 * parts], rest[2 * parts]
    size = mains[0].ref.shape[1]
    total, _, wide = e_out.shape
    quarter = LANES // 4
    half = LANES // 2
    order = chosen(wide, wide, lambda r: r // half + lane_row(chan_ref, r % half, size) * 4)
    eye = chosen(LANES, LANES, same)

    def turn(values, base, chunk):
        turned = dot_nt(eye, values)
        frames = []
        for pair in range(chunk // 2):
            lanes = turned[:, pair * LANES : (pair + 1) * LANES]
            sides = [
                halves_of(
                    lanes[2 * side * quarter : (2 * side + 1) * quarter],
                    lanes[(2 * side + 1) * quarter : (2 * side + 2) * quarter],
                )
                for side in range(2)
            ]
            frames.extend([jnp.concatenate([sides[0][k], sides[1][k]], axis=1) for k in range(2)])
        put(e_out.ref, base, chunk, dot(jnp.concatenate(frames, axis=0).astype(BF16), order))

    frames_in(chan_ref, mains, edge_refs, total, 48, turn)
    e_out.send(0, total, 0)
    e_out.finish(0, total, total)


def top_back_kernel(prev_ref, next_ref, e, taps, q_out, cols_ref, turned_ref):
    total = q_out.shape[0]

    def build(base, chunk):
        shift_into(rows_of(e.ref, base, chunk).astype(F32), base, chunk, cols_ref)

    by_pieces([e], total, 24, build)
    turn_taps(taps, turned_ref)

    def back(base, chunk, number):
        put(q_out.ref, base, chunk, taps_sum(cols_ref, turned_ref, (prev_ref, next_ref), base, chunk, dot_nt))
        q_out.send(base, chunk, number)

    chunk = loop(3, total - 3, 30, back)
    q_out.finish(3, total - 3, chunk)


def top_norm_kernel(own, count, q, h, came_ref, pair_ref, dz_out, copies_ref, acc_ref):
    total = dz_out.shape[0]
    norm = norm_of(came_ref, pair_ref, count)
    acc_ref[...] = jnp.zeros_like(acc_ref)

    def back(base, chunk):
        dz, xhat = back_act(rows_of(q.ref, base, chunk).astype(F32), rows_of(h.ref, base, chunk), norm)
        put(dz_out.ref, base, chunk, dz)
        mine = own_rows(dz, base, chunk, HALO, HALO + own)
        add_sums(acc_ref, mine, own_rows(dz * xhat, base, chunk, HALO, HALO + own))

    by_pieces([q, h], total, 24, back)
    dz_out.send(0, total, 0)
    spread_sums(acc_ref, copies_ref)
    dz_out.finish(0, total, total)


def last_kernel(own, count, prev_ref, next_ref, h, taps, x, came_ref, pair_ref, y_ref, cols_ref):
    wide = cols_ref.shape[-1] // 3
    half = LANES // 2
    order = chosen(wide, wide, lambda r: r // half + r % half * 4)
    eye = chosen(LANES, LANES, same)
    activate_into(h, norm_of(came_ref, pair_ref, count), cols_ref)
    taps.need_all()
    x.need_all()

    def conv(base, chunk, _):
        result = taps_sum(cols_ref, taps.ref, (prev_ref, next_ref), base, chunk) + rows_of(x.ref, base, chunk).astype(F32)
        mixed = dot_nt(result.astype(BF16), order)
        cube = mixed.reshape(chunk, B1, wide)
        for pair in range(chunk // 2):
            stack = []
            for side in range(wide // LANES):
                lanes = slice(side * LANES, (side + 1) * LANES)
                stack.extend(halves_of(cube[2 * pair][:, lanes], cube[2 * pair + 1][:, lanes]))
            turned = dot_nt(eye, jnp.concatenate(stack, axis=0).astype(BF16))
            frames_out(turned, 2, y_ref, base - HALO + 2 * pair)

    loop(HALO, HALO + own, 28, conv, 2)


def middle_kernel(own, count, lead, target, with_top, prev_ref, next_ref, dz, h, *rest):
    if with_top:
        e, *rest = rest
    taps, low, back_ref, came_ref, pair_ref, low_came_ref, low_pair_ref, d_out, dz_out, copies_ref, cols_ref, acc_ref, turned_ref = rest
    total = cols_ref.shape[0]
    norm = norm_of(came_ref, pair_ref, count)
    low_norm = norm_of(low_came_ref, low_pair_ref, count)
    sums = came_sums(back_ref)

    def build(base, size):
        d = back_norm(rows_of(dz.ref, base, size), rows_of(h.ref, base, size), norm, sums, count)
        if with_top:
            d = d + rows_of(e.ref, base, size).astype(F32)
        put(d_out.ref, base, size, d)
        shift_into(d, base, size, cols_ref)

    by_pieces([dz, h, e] if with_top else [dz, h], total, 24, build)
    d_out.send(0, total, 0)
    acc_ref[...] = jnp.zeros_like(acc_ref)
    turn_taps(taps, turned_ref)

    def back(base, chunk, number):
        q = taps_sum(cols_ref, turned_ref, (prev_ref, next_ref), base, chunk, dot_nt)
        pl.when(number == 0)(low.need_all)
        new, xhat = back_act(q, rows_of(low.ref, base, chunk), low_norm)
        put(dz_out.ref, base, chunk, new)
        dz_out.send(base, chunk, number)
        mine = own_rows(new, base, chunk, HALO, HALO + own)
        add_sums(acc_ref, mine, mine * xhat)

    chunk = loop(lead, total - lead, target, back)
    spread_sums(acc_ref, copies_ref)
    d_out.finish(0, total, total)
    dz_out.finish(lead, total - lead, chunk)


def give(buffer_ref, keep_ref, send_ref, sems):
    half = keep_ref.shape[0]
    keep = pltpu.make_async_copy(buffer_ref.at[pl.ds(0, half)], keep_ref, sems.at[0])
    send = pltpu.make_async_copy(buffer_ref.at[pl.ds(half, half)], send_ref, sems.at[1])
    keep.start()
    send.start()
    keep.wait()
    send.wait()


def weight_kernel(
    own, count, order, chans, me_ref, prev_ref, next_ref, d, h, came_ref, pair_ref, keep_ref, send_ref,
    cols_ref, turned_ref, buffer_ref, sems,
):
    norm = norm_of(came_ref, pair_ref, count)
    wide = h.ref.shape[-1]

    def build(base, chunk):
        shift_into(rows_of(d.ref, base, chunk).astype(F32), base, chunk, cols_ref)

    by_pieces([d], cols_ref.shape[0], 24, build)
    h.need_all()

    def turn(base, chunk, _):
        u = activated(rows_of(h.ref, HALO + base, chunk), norm)
        columns = pl.ds(pl.multiple_of(base * B1, chunk * B1), chunk * B1)
        masked = (mask_frames(u, next_ref, HALO + base, chunk), u, mask_frames(u, prev_ref, HALO + base, chunk))
        for tap in range(3):
            turned_ref[tap, :, columns] = transposed(masked[tap].astype(BF16))

    loop(0, own, 28, turn, 4)
    slabs = []
    for tap in range(3):
        other = cols_ref[pl.ds(HALO + 1 - tap, own)].reshape(own * B1, cols_ref.shape[-1])
        grad = dot(turned_ref[tap], other).astype(BF16)
        slabs.extend([grad[:, k * wide : (k + 1) * wide] for k in range(3)])
    pack_wide(order, chans, me_ref, slabs, buffer_ref)
    give(buffer_ref, keep_ref, send_ref, sems)


def bottom_kernel(
    own, count, prev_ref, next_ref, dz, h, taps, short, e1, x, back_ref, came_ref, pair_ref, vec_ref,
    d_out, dz_out, copies_ref, cols_ref, acc_ref, turned_ref,
):
    total = cols_ref.shape[0]
    norm = norm_of(came_ref, pair_ref, count)
    low_norm = norm_rows(vec_ref)
    sums = came_sums(back_ref)
    channels = x.ref.shape[-1]

    def build(base, size):
        d = back_norm(rows_of(dz.ref, base, size), rows_of(h.ref, base, size), norm, sums, count)
        put(d_out.ref, base, size, d)
        _, above = shifts(d)
        put(cols_ref, base, size, jnp.concatenate([d, above], axis=1))

    by_pieces([dz, h], total, 24, build)
    d_out.send(0, total, 0)
    acc_ref[...] = jnp.zeros_like(acc_ref)
    turn_first(taps, short, turned_ref)
    e1.need_all()
    x.need_all()

    def back(base, chunk, number):
        q = taps_sum(cols_ref, turned_ref, (prev_ref, next_ref), base, chunk, dot_nt)
        r = dot_nt(rows_of(e1.ref, base, chunk), short.ref[...])
        parts = (q[:, :channels] + r, q[:, channels:])
        for parity in range(2):
            new, xhat = back_act(parts[parity], channels_of(x.ref, base, chunk, parity), low_norm)
            dz_out.ref[pl.ds(base - HALO, chunk), parity] = new.reshape(chunk, B1, channels).astype(BF16)
            add_sums(acc_ref, new, new * xhat)
        dz_out.send(base - HALO, chunk, number)

    chunk = loop(HALO, HALO + own, 28, back)
    spread_sums(acc_ref, copies_ref)
    d_out.finish(0, total, total)
    dz_out.finish(0, own, chunk)


def first_weight_kernel(
    own, order, chans, shard, me_ref, prev_ref, next_ref, d, x, e1, vec_ref, keep_ref, send_ref,
    cols_ref, turned_ref, raw_ref, buffer_ref, sems,
):
    norm = norm_rows(vec_ref)
    channels = x.ref.shape[-1]
    wide = d.ref.shape[-1]

    def build(base, size):
        value = rows_of(d.ref, base, size)
        _, above = shifts(value.astype(F32))
        put(cols_ref, base, size, jnp.concatenate([value, above.astype(BF16)], axis=1))

    by_pieces([d], cols_ref.shape[0], 24, build)
    x.need_all()
    e1.need_all()

    def turn(base, chunk, _):
        columns = pl.ds(pl.multiple_of(base * B1, chunk * B1), chunk * B1)
        for parity in range(2):
            u = activated(channels_of(x.ref, HALO + base, chunk, parity), norm)
            masked = (mask_frames(u, next_ref, HALO + base, chunk), u, mask_frames(u, prev_ref, HALO + base, chunk))
            for tap in range(3):
                turned_ref[tap, parity * channels : (parity + 1) * channels, columns] = transposed(masked[tap].astype(BF16))

    loop(0, own, 28, turn, 4)
    for tap in range(3):
        other = cols_ref[pl.ds(HALO + 1 - tap, own)].reshape(own * B1, cols_ref.shape[-1])
        grad = dot(turned_ref[tap], other)
        slabs = (grad[channels:, wide:], grad[:channels, :wide], grad[channels:, :wide])
        for kf in range(3):
            for side in range(wide // LANES):
                raw_ref[side, pl.ds(3 * tap + kf, channels, stride=9)] = slabs[kf][:, side * LANES : (side + 1) * LANES]
    short = dot(turned_ref[1, 0:channels], e1.ref[pl.ds(HALO, own)].reshape(own * B1, wide))
    rest = raw_ref.shape[1] - 10 * channels
    for side in range(wide // LANES):
        raw_ref[side, 9 * channels : 10 * channels] = short[:, side * LANES : (side + 1) * LANES]
        raw_ref[side, 10 * channels :] = jnp.zeros((rest, LANES), F32)
    pack_first(order, chans, shard, me_ref, raw_ref, buffer_ref)
    give(buffer_ref, keep_ref, send_ref, sems)


def input_kernel(own, count, dz, x, back_ref, vec_ref, out_ref):
    norm = norm_rows(vec_ref)
    sums = came_sums(back_ref)
    channels = x.ref.shape[-1]
    half = LANES // 2
    order = chosen(channels, channels, lambda r: r // half + r % half * 2)
    eye = chosen(LANES, LANES, same)
    split = chosen(LANES, LANES, lambda r: r // half * half + r % 2 * B1 + r % half // 2)
    dz.need_all()
    x.need_all()

    def build(base, chunk, _):
        mixed = []
        for parity in range(2):
            g = back_norm(
                channels_of(dz.ref, base, chunk, parity), channels_of(x.ref, HALO + base, chunk, parity), norm, sums, count
            )
            mixed.append(dot_nt(g.astype(BF16), order).reshape(chunk, B1, channels))
        for pair in range(chunk // 2):
            even, odd = [], []
            for parity in range(2):
                first, second = halves_of(mixed[parity][2 * pair], mixed[parity][2 * pair + 1])
                even.append(first)
                odd.append(second)
            stack = jnp.concatenate(even + odd, axis=0).astype(BF16)
            turned = dot_nt(eye, dot(split, stack).astype(BF16))
            frames_out(turned, 2, out_ref, base + 2 * pair)

    loop(0, own, 28, build, 2)


SMEM = pl.BlockSpec(memory_space=pltpu.SMEM)
VMEM = pl.BlockSpec(memory_space=pltpu.VMEM)
HBM = pl.BlockSpec(memory_space=pl.ANY)
DMA = pltpu.SemaphoreType.DMA


def run(kernel, scalars, fetched, operands, sent, outs, scratch, micros, plain=(), loose=()):
    arrays = [array for array, _ in fetched]
    buffers = [pltpu.VMEM(array.shape, array.dtype) for array in arrays] + [pltpu.VMEM(shape, kind) for shape, kind, _ in sent]
    sems = [DMA((pieces,)) for _, pieces in fetched] + [DMA((pieces,)) for _, _, pieces in sent]
    counts = (len(scalars), len(fetched), len(loose), len(operands), len(sent), len(plain), len(outs), len(scratch), len(buffers), len(sems))

    def whole(*refs):
        groups, at = [], 0
        for count in counts:
            groups.append(refs[at : at + count])
            at += count
        small, sources, left, inputs, targets, copied, results, own, held, marks = groups
        incoming = [Fetched(*triple) for triple in zip(sources, held, marks)]
        leaving = [Sent(*triple) for triple in zip(targets, held[len(incoming) :], marks[len(incoming) :])]
        for operand in incoming:
            operand.start()
        kernel(*small, *incoming, *left, *inputs, *leaving, *copied, *results, *own)

    made = [(shape, kind) for shape, kind, _ in sent] + list(plain) + list(outs)
    moved = sum(x.size * x.dtype.itemsize for x in arrays + list(operands))
    return pl.pallas_call(
        whole,
        in_specs=[SMEM] * len(scalars) + [HBM] * (len(arrays) + len(loose)) + [VMEM] * len(operands),
        out_specs=[HBM] * (len(sent) + len(plain)) + [VMEM] * len(outs),
        out_shape=[jax.ShapeDtypeStruct(shape, kind) for shape, kind in made],
        scratch_shapes=[pltpu.VMEM(*one) if isinstance(one, tuple) else one for one in scratch] + buffers + sems,
        compiler_params=pltpu.CompilerParams(vmem_limit_bytes=VMEM_BYTES),
        cost_estimate=pl.CostEstimate(flops=int(micros * 1.15e9), bytes_accessed=moved, transcendentals=0),
    )(*scalars, *arrays, *loose, *operands)


def norm_pair(params, norm_index):
    if norm_index == 0:
        return jnp.stack([params[0, 0], params[1, 0]])
    row_pair = params[:, 2 * norm_index - 1 : 2 * norm_index + 1]
    return jnp.transpose(row_pair, (0, 2, 1)).reshape(2, -1)


def pack_norms(vectors):
    blocks = [vectors[0][None]]
    for vector in vectors[1:]:
        blocks.append(vector.reshape(-1, 2).T)
    return jnp.concatenate(blocks, axis=0)


def adam_step(weight, moment, square, gradient, step_rate, decay_rate):
    moment_next = beta_first * moment + (1.0 - beta_first) * gradient
    square_next = beta_second * square + (1.0 - beta_second) * gradient * gradient
    corrected = moment_next / (1.0 - beta_first**STEP)
    divisor = jnp.sqrt(square_next / (1.0 - beta_second**STEP)) + adam_epsilon
    weight_next = weight - step_rate * (corrected / divisor + decay_rate * weight)
    return (weight_next, moment_next, square_next)


def body(
    signal,
    clip_ids,
    output_grad,
    first_weight,
    first_mean,
    first_square,
    wide_weight,
    wide_mean,
    wide_square,
    norm_params,
    norm_mean,
    norm_square,
):
    chans = lax.axis_size("chan")
    groups_of_frames = lax.axis_size("frames")
    devices = chans * groups_of_frames
    chan = lax.axis_index("chan")
    me = {"chan": chan, "frames": lax.axis_index("frames")}
    group = signal.shape[0]
    own = group // chans
    total = own + 2 * HALO
    frames = group * groups_of_frames
    in_local = signal.shape[1] // B0
    ins = in_local * chans
    wide_local = output_grad.shape[1] // B1
    wide = wide_local * chans
    columns = first_weight.shape[1]
    per = LANES // columns
    count_zero = frames * B0
    count = frames * B1

    order_grads = halves("chan", chans)[:-1] + halves("frames", groups_of_frames) + [("chan", 1)]
    signal_rows = signal.reshape(group, -1, LANES)
    signal_main, signal_edges, windows = to_frames(signal_rows)

    count_of_groups = lax.axis_size("frames")
    forward = [(i, i + 1) for i in range(count_of_groups - 1)]
    low = lax.ppermute(clip_ids[group - HALO - 1 :] + 1, "frames", forward)
    high = lax.ppermute(clip_ids[: HALO + 1] + 1, "frames", [(b, a) for a, b in forward])
    ids = lax.dynamic_slice_in_dim(jnp.concatenate([low, clip_ids + 1, high]), chan * own, total + 2, 0)
    masks = ((ids[:-2] == ids[1:-1]).astype(F32), (ids[2:] == ids[1:-1]).astype(F32))

    shard = first_weight.shape[0]
    packed = packed_rows(shard, per)
    first_send = jnp.pad(after(first_weight, *windows).astype(BF16), ((0, per * packed - shard), (0, 0)))
    first_send = jnp.transpose(first_send.reshape(per, packed, columns), (1, 0, 2)).reshape(packed, LANES)
    local = signal.astype(F32)
    local_sums = jnp.stack([jnp.sum(local, axis=0), jnp.sum(local * local, axis=0)]).reshape(2, in_local, B0).sum(axis=2)
    shared = jnp.where(me["frames"] == 0, norm_params.reshape(-1, in_local), 0.0)
    small = jnp.concatenate([local_sums, shared], axis=0)
    places = jnp.arange(LANES) // in_local == chan
    small = jnp.where(places[None], jnp.tile(small, (1, LANES // in_local)), 0.0)
    big = lax.reduce_precision(small, 8, 7)
    send = jnp.concatenate([first_send, big.astype(BF16), (small - big).astype(BF16)], axis=0)
    first_all = to_all(jnp.broadcast_to(send[None], (devices,) + send.shape))

    layers = wide_weight.shape[0]
    rows = wide_weight.shape[1] // 9
    slab_groups = -(-9 // per)
    wide_send = jnp.transpose(after(wide_weight, first_send).astype(BF16).reshape(layers, rows, 9, columns), (0, 2, 1, 3))
    wide_send = jnp.pad(wide_send, ((0, 0), (0, per * slab_groups - 9), (0, 0), (0, 0)))
    wide_send = jnp.transpose(wide_send.reshape(layers, per, slab_groups, rows, columns), (0, 2, 3, 1, 4))
    wide_send = wide_send.reshape(layers, slab_groups, rows, LANES)
    wide_all = lax.all_gather(wide_send, ("frames", "chan"), axis=0)

    chan_scalar = jnp.reshape(chan, (1,)).astype(jnp.int32)
    code_grads = jnp.reshape(code_of(order_grads, me), (1,)).astype(jnp.int32)

    cube = (total, B1, wide)
    cols = (total, B1, 3 * wide)
    lane_rows = signal_rows.shape[1]
    copies = ((devices, 1, 2 * wide), F32)
    acc = ((2, 8, wide), F32)

    pieces = pieces_of(total)

    def steps(low, target):
        return (total - 2 * low) // fit(total - 2 * low, target)

    def wide_taps(layer):
        taps = run(
            functools.partial(unpack_wide, layer, chans),
            (),
            [],
            (),
            [((9, wide, wide), BF16, 1)],
            [],
            [((devices, slab_groups, rows, LANES), BF16), DMA((1,))],
            3,
            loose=(wide_all,),
        )[0]
        return taps.reshape(3, 3 * wide, wide)

    taps_one, short_taps, vec_zero, pairs = run(
        functools.partial(unpack_first, chans, shard, count_zero),
        (),
        [(first_all, 1)],
        (),
        [],
        [((3, 3 * ins, wide), BF16), ((ins, wide), BF16), ((4, ins), F32), ((3, 2, wide), F32)],
        [((wide // LANES, 10 * ins, LANES), F32)],
        4,
    )
    (x_zero,) = run(
        functools.partial(signal_kernel, chans),
        (chan_scalar,),
        [(main, 1) for main in signal_main],
        signal_edges,
        [((total, 2, B1, ins), BF16, 1)],
        [],
        [],
        6,
    )
    top_main, top_edges, _ = to_frames(after(output_grad, x_zero).reshape(group, -1, LANES))
    hidden_one, shortcut, sums = run(
        functools.partial(first_kernel, own),
        masks,
        [(x_zero, pieces), (taps_one, 1), (short_taps, 1)],
        (vec_zero,),
        [(cube, BF16, steps(1, 47)), (cube, BF16, steps(1, 47))],
        [copies],
        [((total, B1, 3 * ins), BF16), acc],
        8,
    )
    came_one = to_all(sums)
    taps_two = wide_taps(0)
    residual, sums = run(
        functools.partial(forward_kernel, own, count, 2, 46, True),
        masks,
        [(hidden_one, pieces), (taps_two, 1), (shortcut, 1)],
        (came_one, pairs[0]),
        [(cube, BF16, steps(2, 46))],
        [copies],
        [(cols, BF16), acc],
        9,
    )
    came_two = to_all(sums)
    taps_three = wide_taps(1)
    (top,) = run(
        functools.partial(top_kernel, chans),
        (chan_scalar,),
        [(main, 1) for main in top_main],
        after(top_edges, residual),
        [(cube, BF16, 1)],
        [],
        [],
        10,
    )
    hidden_two, sums = run(
        functools.partial(forward_kernel, own, count, 3, 30, False),
        masks,
        [(residual, pieces), (after(taps_three, top), 1)],
        (came_two, pairs[1]),
        [(cube, BF16, steps(3, 30))],
        [copies],
        [(cols, BF16), acc],
        9,
    )
    came_three = to_all(sums)
    taps_four = wide_taps(2)
    (top_back,) = run(
        top_back_kernel,
        masks,
        [(after(top, hidden_two), pieces), (taps_four, 1)],
        (),
        [(cube, BF16, steps(3, 30))],
        [],
        [(cols, BF16), ((3, wide, 3 * wide), BF16)],
        7,
    )
    dz_three, sums = run(
        functools.partial(top_norm_kernel, own, count),
        (),
        [(top_back, pieces), (hidden_two, pieces)],
        (came_three, pairs[2]),
        [(cube, BF16, 1)],
        [copies],
        [acc],
        4,
    )
    back_three = to_all(sums)

    def weight_grad(came, pair, values, d):
        blocks = (devices, slab_groups, rows, LANES)
        kept = ((devices // 2,) + blocks[1:], BF16)
        return run(
            functools.partial(weight_kernel, own, count, order_grads, chans),
            (code_grads,) + masks,
            [(d, pieces), (values, 1)],
            (came, pair),
            [],
            [],
            [(cols, BF16), ((3, wide, own * B1), BF16), (blocks, BF16), DMA((2,))],
            9,
            [kept, kept],
        )

    four = weight_grad(came_three, pairs[2], hidden_two, after(top, dz_three))
    d_three, dz_two, sums = run(
        functools.partial(middle_kernel, own, count, 4, 44, False),
        masks,
        [(dz_three, pieces), (hidden_two, pieces), (after(taps_three, *four), 1), (residual, 1)],
        (back_three, came_three, pairs[2], came_two, pairs[1]),
        [(cube, BF16, 1), (cube, BF16, steps(4, 44))],
        [copies],
        [(cols, BF16), acc, ((3, wide, 3 * wide), BF16)],
        9,
    )
    back_two = to_all(sums)
    three = weight_grad(came_two, pairs[1], residual, d_three)
    (block_rows,) = run(
        functools.partial(last_kernel, own, count),
        masks,
        [(after(hidden_two, dz_two), pieces), (taps_four, 1), (residual, 1)],
        (came_three, pairs[2]),
        [],
        [((chans, own, lane_rows, LANES), BF16)],
        [(cols, BF16)],
        12,
    )
    low_top, dz_one, sums = run(
        functools.partial(middle_kernel, own, count, 5, 43, True),
        masks,
        [(dz_two, pieces), (residual, pieces), (top, pieces), (after(taps_two, block_rows, *three), 1), (hidden_one, 1)],
        (back_two, came_two, pairs[1], came_one, pairs[0]),
        [(cube, BF16, 1), (cube, BF16, steps(5, 43))],
        [copies],
        [(cols, BF16), acc, ((3, wide, 3 * wide), BF16)],
        9,
    )
    back_one = to_all(sums)
    two = weight_grad(came_one, pairs[0], hidden_one, low_top)
    d_one, dz_zero, sums = run(
        functools.partial(bottom_kernel, own, count),
        masks,
        [(dz_one, pieces), (hidden_one, pieces), (after(taps_one, *two), 1), (short_taps, 1), (low_top, 1), (x_zero, 1)],
        (back_one, came_one, pairs[0], vec_zero),
        [(cube, BF16, 1), ((own, 2, B1, ins), BF16, own // fit(own, 28))],
        [((devices, 1, 2 * ins), F32)],
        [((total, B1, 2 * wide), BF16), ((2, 8, ins), F32), ((3, 2 * ins, 2 * wide), BF16)],
        8,
    )
    back_zero = to_all(sums)
    one_blocks = (devices, packed, LANES)
    one_kept = ((devices // 2,) + one_blocks[1:], BF16)
    one = run(
        functools.partial(first_weight_kernel, own, order_grads, chans, shard),
        (code_grads,) + masks,
        [(d_one, pieces), (x_zero, 1), (low_top, 1)],
        (vec_zero,),
        [],
        [],
        [
            ((total, B1, 2 * wide), BF16),
            ((3, 2 * ins, own * B1), BF16),
            ((wide // LANES, 10 * ins + per * packed, LANES), F32),
            (one_blocks, BF16),
            DMA((2,)),
        ],
        8,
        [one_kept, one_kept],
    )
    (input_rows,) = run(
        functools.partial(input_kernel, own, count_zero),
        (),
        [(after(dz_zero, *one), 1), (x_zero, 1)],
        (back_zero, vec_zero),
        [],
        [((chans, own, lane_rows, LANES), BF16)],
        [],
        8,
    )

    block_out = lax.all_to_all(block_rows, "chan", 0, 0, tiled=True).reshape(group, -1).astype(F32)
    input_grad = lax.all_to_all(input_rows, "chan", 0, 0, tiled=True).reshape(group, -1).astype(F32)

    wide_sum = scatter_steps([two[0], three[0], four[0]], [two[1], three[1], four[1]], order_grads).astype(F32)
    wide_sum = jnp.transpose(wide_sum.reshape(3, slab_groups, rows, per, columns), (0, 3, 1, 2, 4))
    wide_sum = wide_sum.reshape(3, per * slab_groups, rows, columns)[:, :9]
    grad_wide = jnp.transpose(wide_sum, (0, 2, 1, 3)).reshape(wide_weight.shape)
    first_sum = scatter_steps([one[0]], [one[1]], order_grads).astype(F32)
    grad_first = jnp.transpose(first_sum.reshape(packed, per, columns), (1, 0, 2)).reshape(-1, columns)[:shard]

    norm_sums = [jnp.sum(came, axis=(0, 1)).reshape(2, -1) for came in (back_zero, back_one, back_two, back_three)]
    grad_norms = jnp.stack([pack_norms([s[1] for s in norm_sums]), pack_norms([s[0] for s in norm_sums])])
    grad_norms = lax.dynamic_slice_in_dim(grad_norms, chan * norm_params.shape[2], norm_params.shape[2], 2)
    own_squares = jnp.sum(grad_first * grad_first) + jnp.sum(grad_wide * grad_wide)
    own_squares = own_squares + jnp.where(lax.axis_index("frames") == 0, jnp.sum(grad_norms * grad_norms), 0.0)
    squares = jnp.sum(to_all(jnp.broadcast_to(own_squares, (devices, 1, LANES)))[:, 0, 0])
    grad_norm = jnp.sqrt(squares)
    factor = clip_limit / jnp.maximum(grad_norm, clip_limit)
    first_next, first_mean_next, first_square_next = adam_step(
        first_weight, first_mean, first_square, grad_first * factor, conv_rate, weight_decay
    )
    wide_next, wide_mean_next, wide_square_next = adam_step(
        wide_weight, wide_mean, wide_square, grad_wide * factor, conv_rate, weight_decay
    )
    norm_next, norm_mean_next, norm_square_next = adam_step(
        norm_params, norm_mean, norm_square, grad_norms * factor, norm_rate, 0.0
    )
    return (
        block_out,
        input_grad,
        grad_norm,
        first_next,
        first_mean_next,
        first_square_next,
        first_next.astype(BF16),
        wide_next,
        wide_mean_next,
        wide_square_next,
        wide_next.astype(BF16),
        norm_next,
        norm_mean_next,
        norm_square_next,
    )


def solution(mesh):
    rows = P("frames", "chan")
    deep = P(None, "frames", "chan")
    norms = P(None, None, "chan")
    in_specs = (rows, P("frames"), rows, rows, rows, rows, deep, deep, deep, norms, norms, norms)
    out_specs = (rows, rows, P(), rows, rows, rows, rows, deep, deep, deep, deep, norms, norms, norms)
    return jax.shard_map(body, mesh=mesh, in_specs=in_specs, out_specs=out_specs, check_vma=False)
```

```python
import functools
import math

import jax
import jax.numpy as jnp
from jax import lax
from jax.experimental import pallas as pl
from jax.experimental.pallas import tpu as pltpu
from jax.sharding import PartitionSpec as P

B0 = 64
STEP = 10
B1 = 32
HALO = 6
LANES = 128

norm_epsilon = 1e-05
clip_limit = 100.0
beta_first = 0.9
beta_second = 0.999
adam_epsilon = 1e-08
conv_rate = 0.05
norm_rate = 0.5
weight_decay = 0.01

BOTH = ("chan", "frames")
VMEM_BYTES = 58 * 1024 * 1024
F32 = jnp.float32
BF16 = jnp.bfloat16
NT = (((1,), (1,)), ((), ()))


def to_all(copies):
    return lax.all_to_all(copies, BOTH, 0, 0, tiled=True)


def edges_of(block):
    count = lax.axis_size("frames")
    forward = [(i, i + 1) for i in range(count - 1)]
    low = lax.ppermute(block[block.shape[0] - HALO :].reshape(HALO, -1, LANES), "frames", forward)
    high = lax.ppermute(block[:HALO].reshape(HALO, -1, LANES), "frames", [(b, a) for a, b in forward])
    return jnp.concatenate([low, high], axis=0)


def by_distance(edge):
    parts = lax.axis_size("chan")
    return [edge] + [lax.ppermute(edge, "chan", [(i, i ^ d) for i in range(parts)]) for d in range(1, parts)]


def windows_of(block):
    parts = lax.axis_size("chan")
    own = block.shape[0] // parts
    padded = jnp.pad(block, ((HALO, HALO), (0, 0), (0, 0)))
    return jnp.stack([padded[k * own : k * own + own + 2 * HALO] for k in range(parts)])


def to_frames(block):
    parts = lax.axis_size("chan")
    chan = lax.axis_index("chan")
    own = block.shape[0] // parts
    padded = jnp.pad(block, ((HALO, HALO), (0, 0), (0, 0)))
    windows = [lax.dynamic_slice_in_dim(padded, (chan ^ d) * own, own + 2 * HALO, 0) for d in range(parts)]
    return [windows[0]] + [lax.ppermute(windows[d], "chan", [(i, i ^ d) for i in range(parts)]) for d in range(1, parts)]


def halves(axis, size):
    steps = []
    while size > 1:
        size //= 2
        steps.append((axis, size))
    return steps


def code_of(order, place):
    return sum(((place[axis] // step) % 2) << k for k, (axis, step) in enumerate(order))


def position(orders, me_ref, chan, frame):
    core = chan % 2
    return code_of(orders[core], {"chan": chan, "frames": frame}) ^ me_ref[core]


def exchange(value, orders, k):
    chans, count = lax.axis_size("chan"), lax.axis_size("frames")
    pairs = []
    for chan in range(chans):
        for frame in range(count):
            axis, step = orders[chan % 2][k]
            other = (chan ^ step, frame) if axis == "chan" else (chan, frame ^ step)
            pairs.append((chan * count + frame, other[0] * count + other[1]))
    return lax.ppermute(value, BOTH, pairs)


def gather_halves(block, orders, ties):
    blocks = []
    for k in range(len(orders[0]) - 1):
        block = jnp.concatenate([block, exchange(after(block, *ties[k]), orders, k)], axis=0)
        blocks.append(block)
    other = exchange(after(block, *ties[-1]), orders, len(orders[0]) - 1)
    return (block, other), blocks + [other]


def scatter_step(keeps, sends, orders, k):
    came = [exchange(send, orders, k) for send in sends]
    half = max(keeps[0].shape[0] // 2, 1)

    def added(part):
        return jnp.concatenate([(k[part].astype(F32) + c[part].astype(F32)).astype(BF16) for k, c in zip(keeps, came)], axis=1)

    return [added(slice(0, half))], [added(slice(half, None))]


def scatter_steps(keeps, sends, orders, count):
    for k in reversed(range(count)):
        keeps, sends = scatter_step(keeps, sends, orders, k)
    return keeps[0][0]


def after(value, *others):
    return lax.optimization_barrier((value, *others))[0]


def fit(count, target, unit=1):
    return max([k for k in range(unit, target + 1, unit) if count % k == 0], default=count)


def loop(low, high, target, body, unit=1):
    return spans(low, high - low, target, body, unit)


def spans(low, count, target, body, unit=1):
    chunk = fit(count, target, unit)

    def step(i, carry):
        body(low + i * chunk, chunk, i)
        return carry

    if chunk == count:
        body(low, chunk, 0)
    else:
        lax.fori_loop(0, count // chunk, step, 0)
    return chunk


class Fetched:
    def __init__(self, source, ref, sems):
        self.source, self.ref, self.sems = source, ref, sems
        self.pieces = sems.shape[0]
        self.size = ref.shape[0] // self.pieces

    def copy(self, number):
        rows = pl.ds(number * self.size, self.size)
        return pltpu.make_async_copy(self.source.at[rows], self.ref.at[rows], self.sems.at[number])

    def start(self):
        for number in range(self.pieces):
            self.copy(number).start()

    def need(self, number):
        self.copy(number).wait()

    def need_all(self):
        for number in range(self.pieces):
            self.need(number)


class Sent:
    def __init__(self, target, ref, sems):
        self.target, self.ref, self.sems = target, ref, sems
        self.shape, self.dtype = ref.shape, ref.dtype

    def copy(self, base, chunk, number):
        rows = pl.ds(base, chunk)
        return pltpu.make_async_copy(self.ref.at[rows], self.target.at[rows], self.sems.at[number])

    def send(self, base, chunk, number):
        self.copy(base, chunk, number).start()

    def finish(self, low, high, chunk):
        for number in range((high - low) // chunk):
            self.copy(low + number * chunk, chunk, number).wait()


def sigmoid(z):
    return 0.5 * jnp.tanh(0.5 * z) + 0.5


def dot(a, b):
    return jnp.dot(a, b, preferred_element_type=F32)


def dot_nt(a, b):
    return lax.dot_general(a, b, NT, preferred_element_type=F32)


def chosen(rows, columns, source):
    r = lax.broadcasted_iota(jnp.int32, (rows, columns), 0)
    c = lax.broadcasted_iota(jnp.int32, (rows, columns), 1)
    return (c == source(r)).astype(BF16)


def same(r):
    return r


def transposed(rows):
    return dot_nt(chosen(rows.shape[1], rows.shape[1], same), rows).astype(BF16)


def shifts(flat):
    rows = flat.shape[0]
    bins = lax.broadcasted_iota(jnp.int32, flat.shape, 0) % B1
    below = jnp.where(bins == 0, 0.0, pltpu.roll(flat, 1, 0))
    above = jnp.where(bins == B1 - 1, 0.0, pltpu.roll(flat, rows - 1, 0))
    return below, above


def mask_frames(partial, mask_ref, base, chunk):
    cube = partial.reshape(chunk, B1, partial.shape[-1])
    return jnp.concatenate([cube[k] * mask_ref[base + k] for k in range(chunk)], axis=0)


def rows_of(ref, base, chunk):
    return ref[pl.ds(base, chunk)].reshape(chunk * B1, ref.shape[-1])


def put(ref, base, chunk, value):
    ref[pl.ds(base, chunk)] = value.reshape(chunk, B1, value.shape[-1]).astype(ref.dtype)


def taps_sum(cols_ref, taps_ref, masks, base, chunk, product=dot):
    total = None
    for tap in (1, 0, 2):
        partial = product(rows_of(cols_ref, base + tap - 1, chunk), taps_ref[tap])
        if tap == 0:
            partial = mask_frames(partial, masks[0], base, chunk)
        if tap == 2:
            partial = mask_frames(partial, masks[1], base, chunk)
        total = partial if total is None else total + partial
    return total


def own_rows(value, base, chunk, low, high):
    frame = base + lax.broadcasted_iota(jnp.int32, value.shape, 0) // B1
    return jnp.where((frame >= low) & (frame < high), value, 0.0)


def add_sums(acc_ref, first, second):
    rows, channels = first.shape
    acc_ref[0] += jnp.sum(first.reshape(rows // 8, 8, channels), axis=0)
    acc_ref[1] += jnp.sum(second.reshape(rows // 8, 8, channels), axis=0)


def spread_sums(acc_ref, copies_ref):
    channels = acc_ref.shape[-1]
    for k in range(2):
        row = jnp.sum(acc_ref[k], axis=0, keepdims=True)
        copies_ref[:, :, k * channels : (k + 1) * channels] = jnp.broadcast_to(
            row[None], (copies_ref.shape[0], 1, channels)
        )


def came_sums(came_ref):
    total = jnp.sum(came_ref[...], axis=0)
    half = total.shape[-1] // 2
    return total[:, :half], total[:, half:]


def norm_of(came_ref, pair_ref, count):
    first, second = came_sums(came_ref)
    mean = first / count
    spread = lax.rsqrt(second / count - mean * mean + norm_epsilon)
    return mean, spread, pair_ref[0:1], pair_ref[1:2]


def norm_rows(vec_ref):
    return vec_ref[0:1], vec_ref[1:2], vec_ref[2:3], vec_ref[3:4]


def normal(values, norm):
    return (values.astype(F32) - norm[0]) * norm[1]


def activated(values, norm):
    z = normal(values, norm) * norm[2] + norm[3]
    return z * sigmoid(z)


def back_act(q, values, norm):
    xhat = normal(values, norm)
    z = xhat * norm[2] + norm[3]
    gate = sigmoid(z)
    return q * gate * (1.0 + z * (1.0 - gate)), xhat


def back_norm(dz, values, norm, sums, count):
    xhat = normal(values, norm)
    return norm[2] * norm[1] * (dz.astype(F32) - sums[0] / count - xhat * (sums[1] / count))


def swap_halves(value):
    return pltpu.roll(value, LANES // 2, 1)


def halves_of(first, second):
    low = lax.broadcasted_iota(jnp.int32, first.shape, 1) < LANES // 2
    return jnp.where(low, first, swap_halves(second)), jnp.where(low, swap_halves(first), second)


def fetch_wide(layer, own_ref, other_ref, came_ref, sems):
    half = own_ref.shape[0]
    fetches = [
        pltpu.make_async_copy(ref.at[:, layer], came_ref.at[pl.ds(k * half, half)], sems.at[k])
        for k, ref in enumerate((own_ref, other_ref))
    ]
    for fetch in fetches:
        fetch.start()
    return fetches


def unpack_wide(orders, chans, me_ref, came_ref, taps_ref):
    devices, groups, rows, _ = came_ref.shape
    count = devices // chans
    per = LANES // (taps_ref.shape[2] // chans)
    wide = per * LANES
    piece = LANES // per
    spread = chosen(wide, wide, lambda r: (r % LANES) // piece * LANES + r // LANES * piece + r % piece)
    for frame in range(count):
        for side in range(chans // per):
            parts = []
            for k in range(per):
                at = position(orders, me_ref, side * per + k, frame)
                parts.append(came_ref[at].reshape(groups * rows, LANES))
            result = dot_nt(jnp.concatenate(parts, axis=1), spread).astype(BF16)
            for slab in range(per):
                for group in range(groups):
                    if slab * groups + group < 9:
                        taps_ref[slab * groups + group, frame * rows : (frame + 1) * rows, side * LANES : (side + 1) * LANES] = result[
                            group * rows : (group + 1) * rows, slab * LANES : (slab + 1) * LANES
                        ]


def unpack_kernel(layers, orders, chans, me_ref, own_ref, other_ref, *rest):
    outs, came_refs, sems = rest[: len(layers)], rest[len(layers) : -1], rest[-1]
    fetches = [
        fetch_wide(layer, own_ref, other_ref, came_refs[n], sems.at[pl.ds(2 * n, 2)]) for n, layer in enumerate(layers)
    ]
    for n, out in enumerate(outs):
        for fetch in fetches[n]:
            fetch.wait()
        unpack_wide(orders, chans, me_ref, came_refs[n], out.ref)
        out.send(0, 9, 0)
    for out in outs:
        out.finish(0, 9, 9)


def turn_taps(taps_ref, turned_ref):
    wide = taps_ref.shape[-1]
    for kt in range(3):
        for kf in range(3):
            turned_ref[2 - kt, :, kf * wide : (kf + 1) * wide] = taps_ref[kt, kf * wide : (kf + 1) * wide]


def pack_wide(order, chans, me_ref, slabs, out_ref):
    devices, groups, rows, _ = out_ref.shape
    count = devices // chans
    per = LANES // (slabs[0].shape[1] // chans)
    wide = per * LANES
    piece = LANES // per
    gather = chosen(wide, wide, lambda r: (r % LANES) // piece * LANES + r // LANES * piece + r % piece)
    for group in range(groups):
        for side in range(chans // per):
            parts = []
            for slab in range(per):
                tap = slab * groups + group
                tap = tap if tap < 9 else 8
                parts.append(slabs[tap][:, side * LANES : (side + 1) * LANES])
            result = dot_nt(jnp.concatenate(parts, axis=1), gather).astype(BF16)
            for k in range(per):
                for frame in range(count):
                    at = position(order, me_ref, side * per + k, frame)
                    out_ref[at, group] = result[frame * rows : (frame + 1) * rows, k * LANES : (k + 1) * LANES]


def unpack_first(orders, chans, shard, me_ref, own_ref, other_ref, taps_ref, short_ref, raw_ref, came_ref, sems):
    half = own_ref.shape[0]
    fetches = [
        pltpu.make_async_copy(ref, came_ref.at[pl.ds(k * half, half)], sems.at[k]) for k, ref in enumerate((own_ref, other_ref))
    ]
    for fetch in fetches:
        fetch.start()
    for fetch in fetches:
        fetch.wait()
    devices = came_ref.shape[0]
    count = devices // chans
    ins, outs = short_ref.shape
    per = LANES // (outs // chans)
    rows = packed_rows(shard, per)
    wide = per * LANES
    piece = LANES // per
    spread = chosen(wide, wide, lambda r: (r % LANES) // piece * LANES + r // LANES * piece + r % piece)
    for frame in range(count):
        for side in range(chans // per):
            parts = [came_ref[position(orders, me_ref, side * per + k, frame)] for k in range(per)]
            result = dot_nt(jnp.concatenate(parts, axis=1), spread)
            for slab in range(per):
                start = slab * rows
                size = min(rows, shard - start)
                if size > 0:
                    raw_ref[side, frame * shard + start : frame * shard + start + size] = result[
                        :size, slab * LANES : (slab + 1) * LANES
                    ]
    for tap in range(9):
        kt, kf = tap // 3, tap % 3
        for side in range(outs // LANES):
            lanes = slice(side * LANES, (side + 1) * LANES)
            taps_ref[kt, kf * ins : (kf + 1) * ins, lanes] = raw_ref[side, pl.ds(tap, ins, stride=9)].astype(BF16)
    for side in range(outs // LANES):
        short_ref[:, side * LANES : (side + 1) * LANES] = raw_ref[side, 9 * ins : 10 * ins].astype(BF16)


def unpack_small(count_zero, came_ref, vec_ref, pairs_ref):
    parts = [jnp.sum(came_ref[:, 16 * k : 16 * (k + 1)].astype(F32), axis=0) for k in range(2)]
    sums = parts[0] + parts[1]
    average = sums[0:1] / count_zero
    vec_ref[0:1] = average
    vec_ref[1:2] = lax.rsqrt(sums[1:2] / count_zero - average * average + norm_epsilon)
    vec_ref[2:3] = sums[2:3]
    vec_ref[3:4] = sums[9:10]
    c = lax.broadcasted_iota(jnp.int32, (LANES, 2 * LANES), 1)
    r = lax.broadcasted_iota(jnp.int32, (LANES, 2 * LANES), 0)
    for side in range(2):
        place = (c == 2 * r + side).astype(BF16)
        spread_rows = [dot(part.astype(BF16), place) for part in (parts[0], parts[1])]
        both = spread_rows[0] + spread_rows[1]
        for k in range(3):
            for kind in range(2):
                row = both[2 + 7 * kind + 1 + 2 * k + side : 2 + 7 * kind + 2 + 2 * k + side]
                pairs_ref[k, kind : kind + 1] = row if side == 0 else pairs_ref[k, kind : kind + 1] + row


def turn_first(taps, short, turned_ref):
    ins, outs = short.ref.shape
    taps.need_all()
    short.need_all()
    for kt in range(3):
        turned_ref[2 - kt, 0:ins, 0:outs] = taps.ref[kt, ins : 2 * ins]
        turned_ref[2 - kt, 0:ins, outs:] = jnp.zeros((ins, outs), BF16)
        turned_ref[2 - kt, ins:, 0:outs] = taps.ref[kt, 2 * ins :]
        turned_ref[2 - kt, ins:, outs:] = taps.ref[kt, 0:ins]


def pack_first(order, chans, shard, me_ref, raw_ref, out_ref):
    devices, rows, _ = out_ref.shape
    count = devices // chans
    outs = raw_ref.shape[0] * LANES
    per = LANES // (outs // chans)
    wide = per * LANES
    piece = LANES // per
    gather = chosen(wide, wide, lambda r: (r % LANES) // piece * LANES + r // LANES * piece + r % piece)
    for frame in range(count):
        for side in range(chans // per):
            parts = [raw_ref[side, frame * shard + slab * rows : frame * shard + (slab + 1) * rows] for slab in range(per)]
            result = dot_nt(jnp.concatenate(parts, axis=1).astype(BF16), gather).astype(BF16)
            for k in range(per):
                at = position(order, me_ref, side * per + k, frame)
                out_ref[at] = result[:, k * LANES : (k + 1) * LANES]


def packed_rows(shard, per):
    return -(-shard // (per * 16)) * 16


def frames_in(chan_ref, mains, edges_ref, total, target, body):
    parts = len(mains)
    for main in mains:
        main.need_all()
    for low, at, part in ((0, 0, 0), (total - HALO, HALO, parts - 1)):

        @pl.when(chan_ref[0] == part)
        def _():
            for d, main in enumerate(mains):
                size = main.ref.shape[1]
                main.ref[low : low + HALO] = edges_ref[d, at : at + HALO, size : 2 * size]

    def piece(at, chunk, _):
        cubes = jnp.concatenate([main.ref[pl.ds(at, chunk)] for main in mains], axis=1)
        body(cubes.reshape(chunk * cubes.shape[1], LANES), at, chunk)

    loop(0, total, target, piece, 2)


def lane_row(chan_ref, q, size):
    return (q // size ^ chan_ref[0]) * size + q % size


def frames_out(rows, count, out_ref, at):
    parts, _, size, _ = out_ref.shape
    cube = rows.reshape(count, parts * size, LANES)
    for s in range(parts):
        out_ref[s, pl.ds(at, count)] = cube[:, s * size : (s + 1) * size].astype(out_ref.dtype)


def pieces_of(total):
    return fit(total, 4)


def channels_of(ref, base, chunk, parity):
    return ref[pl.ds(base, chunk), parity].reshape(chunk * B1, ref.shape[-1])


def signal_kernel(chan_ref, main, edges_ref, x_out):
    parts, _, size, _ = main.ref.shape
    x_ref = x_out.ref
    total = x_ref.shape[0]
    channels = x_ref.shape[-1]
    half = LANES // 2
    split = chosen(LANES, LANES, lambda r: r // half * half + r % B1 * 2 + r % half // B1)
    order = chosen(channels, channels, lambda r: r // half + r % half * 2)

    def turn(values, base, chunk):
        turned = dot_nt(split, values)
        for parity in range(2):
            pairs = []
            for pair in range(chunk // 2):
                lanes = turned[:, pair * LANES : (pair + 1) * LANES]
                even = lanes[parity * B1 : (parity + 1) * B1]
                odd = lanes[half + parity * B1 : half + (parity + 1) * B1]
                pairs.extend(halves_of(even, odd))
            x = dot(jnp.concatenate(pairs, axis=0).astype(BF16), order)
            x_ref[pl.ds(base, chunk), parity] = x.reshape(chunk, B1, channels).astype(BF16)

    main.need_all()
    for low, at, part in ((0, 0, 0), (total - HALO, HALO, parts - 1)):

        @pl.when(chan_ref[0] == part)
        def _():
            for s in range(parts):
                main.ref[s, low : low + HALO] = edges_ref[s ^ part, at : at + HALO, 0:size]

    def piece(at, chunk, _):
        cubes = jnp.concatenate([main.ref[s, pl.ds(at, chunk)] for s in range(parts)], axis=1)
        turn(cubes.reshape(chunk * parts * size, LANES), at, chunk)

    loop(0, total, 48, piece, 2)
    x_out.send(0, total, 0)
    x_out.finish(0, total, total)


def first_kernel(own, count_zero, prev_ref, next_ref, x, taps, short, small_ref, h_out, s_out, copies_ref, vec_ref, pairs_ref, cols_ref, acc_ref):
    unpack_small(count_zero, small_ref, vec_ref, pairs_ref)
    total = x.ref.shape[0]
    channels = x.ref.shape[-1]
    norm = norm_rows(vec_ref)

    def build(base, chunk):
        acts = [activated(channels_of(x.ref, base, chunk, parity), norm) for parity in range(2)]
        below, _ = shifts(acts[1])
        put(cols_ref, base, chunk, jnp.concatenate([below, acts[0], acts[1]], axis=1))

    by_pieces([x], total, 12, build)
    acc_ref[...] = jnp.zeros_like(acc_ref)
    taps.need_all()
    short.need_all()

    def conv(base, chunk, number):
        result = taps_sum(cols_ref, taps.ref, (prev_ref, next_ref), base, chunk)
        put(h_out.ref, base, chunk, result)
        h_out.send(base, chunk, number)
        mine = own_rows(result, base, chunk, HALO, HALO + own)
        add_sums(acc_ref, mine, mine * mine)
        even = rows_of(cols_ref, base, chunk)[:, channels : 2 * channels]
        put(s_out.ref, base, chunk, dot(even, short.ref[...]))
        s_out.send(base, chunk, number)

    chunk = loop(1, total - 1, 47, conv)
    spread_sums(acc_ref, copies_ref)
    h_out.finish(1, total - 1, chunk)
    s_out.finish(1, total - 1, chunk)


def by_pieces(fetched, total, target, body):
    pieces = fetched[0].pieces
    size = total // pieces

    def piece(number, carry):
        for operand in fetched:
            operand.need(number)
        spans(number * size, size, target, lambda base, chunk, _: body(base, chunk))
        return carry

    lax.fori_loop(0, pieces, piece, 0)


def activate_into(h, norm, cols_ref):
    def build(base, chunk):
        act = activated(rows_of(h.ref, base, chunk), norm)
        below, above = shifts(act)
        put(cols_ref, base, chunk, jnp.concatenate([below, act, above], axis=1))

    by_pieces([h], cols_ref.shape[0], 24, build)


def forward_kernel(own, count, lead, target, with_short, prev_ref, next_ref, h, taps, *rest):
    if with_short:
        s, came_ref, pair_ref, out, copies_ref, cols_ref, acc_ref = rest
    else:
        came_ref, pair_ref, out, copies_ref, cols_ref, acc_ref = rest
    total = cols_ref.shape[0]
    activate_into(h, norm_of(came_ref, pair_ref, count), cols_ref)
    acc_ref[...] = jnp.zeros_like(acc_ref)
    taps.need_all()

    def conv(base, chunk, number):
        result = taps_sum(cols_ref, taps.ref, (prev_ref, next_ref), base, chunk)
        if with_short:
            pl.when(number == 0)(s.need_all)
            result = result + rows_of(s.ref, base, chunk).astype(F32)
        put(out.ref, base, chunk, result)
        out.send(base, chunk, number)
        mine = own_rows(result, base, chunk, HALO, HALO + own)
        add_sums(acc_ref, mine, mine * mine)

    chunk = loop(lead, total - lead, target, conv)
    spread_sums(acc_ref, copies_ref)
    out.finish(lead, total - lead, chunk)


def shift_into(value, base, chunk, cols_ref):
    below, above = shifts(value)
    put(cols_ref, base, chunk, jnp.concatenate([above, value, below], axis=1))


def top_kernel(parts, chan_ref, *rest):
    mains, (edges_ref, e_out) = rest[:parts], rest[parts:]
    size = mains[0].ref.shape[1]
    total, _, wide = e_out.shape
    quarter = LANES // 4
    half = LANES // 2
    order = chosen(wide, wide, lambda r: r // half + lane_row(chan_ref, r % half, size) * 4)
    eye = chosen(LANES, LANES, same)

    def turn(values, base, chunk):
        turned = dot_nt(eye, values)
        frames = []
        for pair in range(chunk // 2):
            lanes = turned[:, pair * LANES : (pair + 1) * LANES]
            sides = [
                halves_of(
                    lanes[2 * side * quarter : (2 * side + 1) * quarter],
                    lanes[(2 * side + 1) * quarter : (2 * side + 2) * quarter],
                )
                for side in range(2)
            ]
            frames.extend([jnp.concatenate([sides[0][k], sides[1][k]], axis=1) for k in range(2)])
        put(e_out.ref, base, chunk, dot(jnp.concatenate(frames, axis=0).astype(BF16), order))

    frames_in(chan_ref, mains, edges_ref, total, 48, turn)
    e_out.send(0, total, 0)
    e_out.finish(0, total, total)


def top_back_kernel(layer, orders, chans, me_ref, prev_ref, next_ref, e, own_ref, other_ref, q_out, taps_out, cols_ref, turned_ref, came_ref, sems):
    total = q_out.shape[0]
    wide = e.ref.shape[-1]
    fetches = fetch_wide(layer, own_ref, other_ref, came_ref, sems)

    def build(base, chunk):
        shift_into(rows_of(e.ref, base, chunk).astype(F32), base, chunk, cols_ref)

    by_pieces([e], total, 24, build)
    for fetch in fetches:
        fetch.wait()
    unpack_wide(orders, chans, me_ref, came_ref, taps_out.ref)
    taps_out.send(0, 9, 0)
    for kt in range(3):
        for kf in range(3):
            turned_ref[2 - kt, :, kf * wide : (kf + 1) * wide] = taps_out.ref[3 * kt + kf]

    def back(base, chunk, number):
        put(q_out.ref, base, chunk, taps_sum(cols_ref, turned_ref, (prev_ref, next_ref), base, chunk, dot_nt))
        q_out.send(base, chunk, number)

    chunk = loop(3, total - 3, 30, back)
    taps_out.finish(0, 9, 9)
    q_out.finish(3, total - 3, chunk)


def top_norm_kernel(own, count, q, h, came_ref, pair_ref, dz_out, copies_ref, acc_ref):
    total = dz_out.shape[0]
    norm = norm_of(came_ref, pair_ref, count)
    acc_ref[...] = jnp.zeros_like(acc_ref)

    def back(base, chunk):
        dz, xhat = back_act(rows_of(q.ref, base, chunk).astype(F32), rows_of(h.ref, base, chunk), norm)
        put(dz_out.ref, base, chunk, dz)
        mine = own_rows(dz, base, chunk, HALO, HALO + own)
        add_sums(acc_ref, mine, own_rows(dz * xhat, base, chunk, HALO, HALO + own))

    by_pieces([q, h], total, 24, back)
    dz_out.send(0, total, 0)
    spread_sums(acc_ref, copies_ref)
    dz_out.finish(0, total, total)


def last_kernel(own, count, prev_ref, next_ref, h, taps, x, came_ref, pair_ref, y_ref, cols_ref):
    wide = cols_ref.shape[-1] // 3
    half = LANES // 2
    order = chosen(wide, wide, lambda r: r // half + r % half * 4)
    eye = chosen(LANES, LANES, same)
    activate_into(h, norm_of(came_ref, pair_ref, count), cols_ref)
    taps.need_all()
    x.need_all()

    def conv(base, chunk, _):
        result = taps_sum(cols_ref, taps.ref, (prev_ref, next_ref), base, chunk) + rows_of(x.ref, base, chunk).astype(F32)
        mixed = dot_nt(result.astype(BF16), order)
        cube = mixed.reshape(chunk, B1, wide)
        for pair in range(chunk // 2):
            stack = []
            for side in range(wide // LANES):
                lanes = slice(side * LANES, (side + 1) * LANES)
                stack.extend(halves_of(cube[2 * pair][:, lanes], cube[2 * pair + 1][:, lanes]))
            turned = dot_nt(eye, jnp.concatenate(stack, axis=0).astype(BF16))
            frames_out(turned, 2, y_ref, base - HALO + 2 * pair)

    loop(HALO, HALO + own, 28, conv, 2)


def middle_kernel(own, count, lead, target, with_top, prev_ref, next_ref, dz, h, *rest):
    if with_top:
        e, *rest = rest
    taps, low, back_ref, came_ref, pair_ref, low_came_ref, low_pair_ref, d_out, dz_out, copies_ref, cols_ref, acc_ref, turned_ref = rest
    total = cols_ref.shape[0]
    norm = norm_of(came_ref, pair_ref, count)
    low_norm = norm_of(low_came_ref, low_pair_ref, count)
    sums = came_sums(back_ref)

    def build(base, size):
        d = back_norm(rows_of(dz.ref, base, size), rows_of(h.ref, base, size), norm, sums, count)
        if with_top:
            d = d + rows_of(e.ref, base, size).astype(F32)
        put(d_out.ref, base, size, d)
        shift_into(d, base, size, cols_ref)

    by_pieces([dz, h, e] if with_top else [dz, h], total, 24, build)
    d_out.send(0, total, 0)
    acc_ref[...] = jnp.zeros_like(acc_ref)
    taps.need_all()
    turn_taps(taps.ref, turned_ref)

    def back(base, chunk, number):
        q = taps_sum(cols_ref, turned_ref, (prev_ref, next_ref), base, chunk, dot_nt)
        pl.when(number == 0)(low.need_all)
        new, xhat = back_act(q, rows_of(low.ref, base, chunk), low_norm)
        put(dz_out.ref, base, chunk, new)
        dz_out.send(base, chunk, number)
        mine = own_rows(new, base, chunk, HALO, HALO + own)
        add_sums(acc_ref, mine, mine * xhat)

    chunk = loop(lead, total - lead, target, back)
    spread_sums(acc_ref, copies_ref)
    d_out.finish(0, total, total)
    dz_out.finish(lead, total - lead, chunk)


def give(buffer_ref, keep_ref, send_ref, sems):
    half = keep_ref.shape[0]
    keep = pltpu.make_async_copy(buffer_ref.at[pl.ds(0, half)], keep_ref, sems.at[0])
    send = pltpu.make_async_copy(buffer_ref.at[pl.ds(half, half)], send_ref, sems.at[1])
    keep.start()
    send.start()
    keep.wait()
    send.wait()


def weight_kernel(
    own, count, order, chans, me_ref, prev_ref, next_ref, h, d, came_ref, pair_ref, keep_ref, send_ref,
    cols_ref, turned_ref, buffer_ref, sems,
):
    norm = norm_of(came_ref, pair_ref, count)
    wide = h.ref.shape[-1]

    def build(base, chunk):
        shift_into(rows_of(d.ref, base, chunk).astype(F32), base, chunk, cols_ref)

    chunk = fit(own, 28, 4)
    staged = all(HALO + chunk * (i + 1) <= h.size * (i + 2) for i in range(own // chunk)) and own // chunk + 1 == h.pieces
    if not staged:
        h.need_all()

    def turn(base, chunk, number):
        if staged:
            pl.when(number == 0)(lambda: h.need(0))
            h.need(number + 1)
        u = activated(rows_of(h.ref, HALO + base, chunk), norm)
        columns = pl.ds(pl.multiple_of(base * B1, chunk * B1), chunk * B1)
        masked = (mask_frames(u, next_ref, HALO + base, chunk), u, mask_frames(u, prev_ref, HALO + base, chunk))
        for tap in range(3):
            turned_ref[tap, :, columns] = transposed(masked[tap].astype(BF16))

    loop(0, own, 28, turn, 4)
    by_pieces([d], cols_ref.shape[0], 24, build)
    slabs = []
    for tap in range(3):
        other = cols_ref[pl.ds(HALO + 1 - tap, own)].reshape(own * B1, cols_ref.shape[-1])
        grad = dot(turned_ref[tap], other).astype(BF16)
        slabs.extend([grad[:, k * wide : (k + 1) * wide] for k in range(3)])
    pack_wide(order, chans, me_ref, slabs, buffer_ref)
    give(buffer_ref, keep_ref, send_ref, sems)


def bottom_kernel(
    own, count, prev_ref, next_ref, dz, h, taps, short, e1, x, back_ref, came_ref, pair_ref, vec_ref,
    d_out, dz_out, copies_ref, cols_ref, acc_ref, turned_ref,
):
    total = cols_ref.shape[0]
    norm = norm_of(came_ref, pair_ref, count)
    low_norm = norm_rows(vec_ref)
    sums = came_sums(back_ref)
    channels = x.ref.shape[-1]

    def build(base, size):
        d = back_norm(rows_of(dz.ref, base, size), rows_of(h.ref, base, size), norm, sums, count)
        put(d_out.ref, base, size, d)
        _, above = shifts(d)
        put(cols_ref, base, size, jnp.concatenate([d, above], axis=1))

    by_pieces([dz, h], total, 24, build)
    d_out.send(0, total, 0)
    acc_ref[...] = jnp.zeros_like(acc_ref)
    turn_first(taps, short, turned_ref)
    e1.need_all()
    x.need_all()

    def back(base, chunk, number):
        q = taps_sum(cols_ref, turned_ref, (prev_ref, next_ref), base, chunk, dot_nt)
        r = dot_nt(rows_of(e1.ref, base, chunk), short.ref[...])
        parts = (q[:, :channels] + r, q[:, channels:])
        for parity in range(2):
            new, xhat = back_act(parts[parity], channels_of(x.ref, base, chunk, parity), low_norm)
            dz_out.ref[pl.ds(base - HALO, chunk), parity] = new.reshape(chunk, B1, channels).astype(BF16)
            add_sums(acc_ref, new, new * xhat)
        dz_out.send(base - HALO, chunk, number)

    chunk = loop(HALO, HALO + own, 28, back)
    spread_sums(acc_ref, copies_ref)
    d_out.finish(0, total, total)
    dz_out.finish(0, own, chunk)


def first_weight_kernel(
    own, order, chans, shard, me_ref, prev_ref, next_ref, d, x, e1, vec_ref, keep_ref, send_ref,
    cols_ref, turned_ref, raw_ref, buffer_ref, sems,
):
    norm = norm_rows(vec_ref)
    channels = x.ref.shape[-1]
    wide = d.ref.shape[-1]

    def build(base, size):
        value = rows_of(d.ref, base, size)
        _, above = shifts(value.astype(F32))
        put(cols_ref, base, size, jnp.concatenate([value, above.astype(BF16)], axis=1))

    by_pieces([d], cols_ref.shape[0], 24, build)
    x.need_all()
    e1.need_all()

    def turn(base, chunk, _):
        columns = pl.ds(pl.multiple_of(base * B1, chunk * B1), chunk * B1)
        for parity in range(2):
            u = activated(channels_of(x.ref, HALO + base, chunk, parity), norm)
            masked = (mask_frames(u, next_ref, HALO + base, chunk), u, mask_frames(u, prev_ref, HALO + base, chunk))
            for tap in range(3):
                turned_ref[tap, parity * channels : (parity + 1) * channels, columns] = transposed(masked[tap].astype(BF16))

    loop(0, own, 28, turn, 4)
    for tap in range(3):
        other = cols_ref[pl.ds(HALO + 1 - tap, own)].reshape(own * B1, cols_ref.shape[-1])
        grad = dot(turned_ref[tap], other)
        slabs = (grad[channels:, wide:], grad[:channels, :wide], grad[channels:, :wide])
        for kf in range(3):
            for side in range(wide // LANES):
                raw_ref[side, pl.ds(3 * tap + kf, channels, stride=9)] = slabs[kf][:, side * LANES : (side + 1) * LANES]
    short = dot(turned_ref[1, 0:channels], e1.ref[pl.ds(HALO, own)].reshape(own * B1, wide))
    rest = raw_ref.shape[1] - 10 * channels
    for side in range(wide // LANES):
        raw_ref[side, 9 * channels : 10 * channels] = short[:, side * LANES : (side + 1) * LANES]
        raw_ref[side, 10 * channels :] = jnp.zeros((rest, LANES), F32)
    pack_first(order, chans, shard, me_ref, raw_ref, buffer_ref)
    give(buffer_ref, keep_ref, send_ref, sems)


def input_kernel(own, count, dz, x, back_ref, vec_ref, out_ref):
    norm = norm_rows(vec_ref)
    sums = came_sums(back_ref)
    channels = x.ref.shape[-1]
    half = LANES // 2
    order = chosen(channels, channels, lambda r: r // half + r % half * 2)
    eye = chosen(LANES, LANES, same)
    split = chosen(LANES, LANES, lambda r: r // half * half + r % 2 * B1 + r % half // 2)
    dz.need_all()
    x.need_all()

    def build(base, chunk, _):
        mixed = []
        for parity in range(2):
            g = back_norm(
                channels_of(dz.ref, base, chunk, parity), channels_of(x.ref, HALO + base, chunk, parity), norm, sums, count
            )
            mixed.append(dot_nt(g.astype(BF16), order).reshape(chunk, B1, channels))
        for pair in range(chunk // 2):
            even, odd = [], []
            for parity in range(2):
                first, second = halves_of(mixed[parity][2 * pair], mixed[parity][2 * pair + 1])
                even.append(first)
                odd.append(second)
            stack = jnp.concatenate(even + odd, axis=0).astype(BF16)
            turned = dot_nt(eye, dot(split, stack).astype(BF16))
            frames_out(turned, 2, out_ref, base + 2 * pair)

    loop(0, own, 28, build, 2)


SMEM = pl.BlockSpec(memory_space=pltpu.SMEM)
VMEM = pl.BlockSpec(memory_space=pltpu.VMEM)
HBM = pl.BlockSpec(memory_space=pl.ANY)
DMA = pltpu.SemaphoreType.DMA


def run(kernel, scalars, fetched, operands, sent, outs, scratch, micros, plain=(), loose=()):
    arrays = [array for array, _ in fetched]
    buffers = [pltpu.VMEM(array.shape, array.dtype) for array in arrays] + [pltpu.VMEM(shape, kind) for shape, kind, _ in sent]
    sems = [DMA((pieces,)) for _, pieces in fetched] + [DMA((pieces,)) for _, _, pieces in sent]
    counts = (len(scalars), len(fetched), len(loose), len(operands), len(sent), len(plain), len(outs), len(scratch), len(buffers), len(sems))

    def whole(*refs):
        groups, at = [], 0
        for count in counts:
            groups.append(refs[at : at + count])
            at += count
        small, sources, left, inputs, targets, copied, results, own, held, marks = groups
        incoming = [Fetched(*triple) for triple in zip(sources, held, marks)]
        leaving = [Sent(*triple) for triple in zip(targets, held[len(incoming) :], marks[len(incoming) :])]
        for operand in incoming:
            operand.start()
        kernel(*small, *incoming, *left, *inputs, *leaving, *copied, *results, *own)

    made = [(shape, kind) for shape, kind, _ in sent] + list(plain) + list(outs)
    moved = sum(x.size * x.dtype.itemsize for x in arrays + list(operands))
    return pl.pallas_call(
        whole,
        in_specs=[SMEM] * len(scalars) + [HBM] * (len(arrays) + len(loose)) + [VMEM] * len(operands),
        out_specs=[HBM] * (len(sent) + len(plain)) + [VMEM] * len(outs),
        out_shape=[jax.ShapeDtypeStruct(shape, kind) for shape, kind in made],
        scratch_shapes=[pltpu.VMEM(*one) if isinstance(one, tuple) else one for one in scratch] + buffers + sems,
        compiler_params=pltpu.CompilerParams(vmem_limit_bytes=VMEM_BYTES),
        cost_estimate=pl.CostEstimate(flops=int(micros * 1.15e9), bytes_accessed=moved // 10, transcendentals=0),
    )(*scalars, *arrays, *loose, *operands)


def norm_pair(params, norm_index):
    if norm_index == 0:
        return jnp.stack([params[0, 0], params[1, 0]])
    row_pair = params[:, 2 * norm_index - 1 : 2 * norm_index + 1]
    return jnp.transpose(row_pair, (0, 2, 1)).reshape(2, -1)


def pack_norms(vectors):
    blocks = [vectors[0][None]]
    for vector in vectors[1:]:
        blocks.append(vector.reshape(-1, 2).T)
    return jnp.concatenate(blocks, axis=0)


def adam_step(weight, moment, square, gradient, step_rate, decay_rate):
    moment_next = beta_first * moment + (1.0 - beta_first) * gradient
    square_next = beta_second * square + (1.0 - beta_second) * gradient * gradient
    corrected = moment_next / (1.0 - beta_first**STEP)
    divisor = jnp.sqrt(square_next / (1.0 - beta_second**STEP)) + adam_epsilon
    weight_next = weight - step_rate * (corrected / divisor + decay_rate * weight)
    return (weight_next, moment_next, square_next)


def body(
    signal,
    clip_ids,
    output_grad,
    first_weight,
    first_mean,
    first_square,
    wide_weight,
    wide_mean,
    wide_square,
    norm_params,
    norm_mean,
    norm_square,
):
    chans = lax.axis_size("chan")
    groups_of_frames = lax.axis_size("frames")
    devices = chans * groups_of_frames
    chan = lax.axis_index("chan")
    me = {"chan": chan, "frames": lax.axis_index("frames")}
    group = signal.shape[0]
    own = group // chans
    total = own + 2 * HALO
    frames = group * groups_of_frames
    in_local = signal.shape[1] // B0
    ins = in_local * chans
    wide_local = output_grad.shape[1] // B1
    wide = wide_local * chans
    columns = first_weight.shape[1]
    per = LANES // columns
    count_zero = frames * B0
    count = frames * B1

    core = [("chan", 1)]
    near, far = halves("chan", chans)[:-1], halves("frames", groups_of_frames)
    gather_orders = (far + near + core, far[:-2] + far[-1:] + near + far[-2:-1] + core)
    order_grads = (far[:-2] + near + far[-2:] + core, far[:-2] + near + far[-1:] + far[-2:-1] + core)
    first_order = (near + far + core,) * 2
    code_first = jnp.stack([code_of(order, me) for order in first_order]).astype(jnp.int32)
    code_gather = jnp.stack([code_of(order, me) for order in gather_orders]).astype(jnp.int32)
    code_grads = jnp.stack([code_of(order, me) for order in order_grads]).astype(jnp.int32)
    last_step = len(core + near + far) - 1
    signal_rows = signal.reshape(group, -1, LANES)
    shard = first_weight.shape[0]
    packed = packed_rows(shard, per)
    first_send = jnp.pad(first_weight.astype(BF16), ((0, per * packed - shard), (0, 0)))
    first_send = jnp.transpose(first_send.reshape(per, packed, columns), (1, 0, 2)).reshape(1, packed, LANES)
    windows = windows_of(signal_rows)
    signal_main = lax.all_to_all(windows, "chan", 0, 0, tiled=True)
    edge = edges_of(jnp.concatenate([signal, output_grad], axis=1))

    forward = [(i, i + 1) for i in range(groups_of_frames - 1)]
    low = lax.ppermute(clip_ids[group - HALO - 1 :] + 1, "frames", forward)
    high = lax.ppermute(clip_ids[: HALO + 1] + 1, "frames", [(b, a) for a, b in forward])
    ids = lax.dynamic_slice_in_dim(jnp.concatenate([low, clip_ids + 1, high]), chan * own, total + 2, 0)
    masks = ((ids[:-2] == ids[1:-1]).astype(F32), (ids[2:] == ids[1:-1]).astype(F32))

    local = signal.astype(F32)
    local_sums = jnp.stack([jnp.sum(local, axis=0), jnp.sum(local * local, axis=0)]).reshape(2, in_local, B0).sum(axis=2)
    shared = jnp.where(me["frames"] == 0, norm_params.reshape(-1, in_local), 0.0)
    small = jnp.concatenate([local_sums, shared], axis=0)
    places = jnp.arange(LANES) // in_local == chan
    small = jnp.where(places[None], jnp.tile(small, (1, LANES // in_local)), 0.0)
    big = lax.reduce_precision(small, 8, 7)
    send = jnp.concatenate([big.astype(BF16), (small - big).astype(BF16)], axis=0)
    send = jnp.broadcast_to(send[None], (devices,) + send.shape)

    first_steps, block = [], first_send
    for k in range(last_step):
        if k == 1:
            block = after(block, windows)
        block = jnp.concatenate([block, exchange(block, first_order, k)], axis=0)
        first_steps.append(block)
        if k == 1:
            edges = by_distance(after(edge, block))
        if k == 2:
            small_all = to_all(after(send, signal_main, block, *edges, *masks))
    edges = jnp.stack(edges)
    chan_scalar = jnp.reshape(chan, (1,)).astype(jnp.int32)
    (x_zero,) = run(
        signal_kernel,
        (chan_scalar,),
        [(signal_main, chans)],
        (edges,),
        [((total, 2, B1, ins), BF16, 1)],
        [],
        [],
        6,
    )
    first_halves = (block, exchange(after(block, x_zero, small_all), first_order, last_step))
    first_steps.append(first_halves[1])

    layers = wide_weight.shape[0]
    rows = wide_weight.shape[1] // 9
    slab_groups = -(-9 // per)
    wide_send = jnp.transpose(wide_weight.astype(BF16).reshape(layers, rows, 9, columns), (0, 2, 1, 3))
    wide_send = jnp.pad(wide_send, ((0, 0), (0, per * slab_groups - 9), (0, 0), (0, 0)))
    wide_send = jnp.transpose(wide_send.reshape(layers, per, slab_groups, rows, columns), (0, 2, 3, 1, 4))
    wide_send = wide_send.reshape(layers, slab_groups, rows, LANES)


    cube = (total, B1, wide)
    cols = (total, B1, 3 * wide)
    lane_rows = signal_rows.shape[1]
    copies = ((devices, 1, 2 * wide), F32)
    acc = ((2, 8, wide), F32)

    pieces = pieces_of(total)

    def steps(low, target):
        return (total - 2 * low) // fit(total - 2 * low, target)

    slab_blocks = ((devices, slab_groups, rows, LANES), BF16)
    slabs = ((9, wide, wide), BF16, 1)

    def conv_taps(taps):
        return taps.reshape(3, 3 * wide, wide)

    taps_one, short_taps = run(
        functools.partial(unpack_first, first_order, chans, shard),
        (code_first,),
        [],
        (),
        [],
        [((3, 3 * ins, wide), BF16), ((ins, wide), BF16)],
        [((wide // LANES, 10 * ins, LANES), F32), ((devices, packed, LANES), BF16), DMA((2,))],
        4,
        loose=first_halves,
    )
    hidden_one, shortcut, sums, vec_zero, pairs = run(
        functools.partial(first_kernel, own, count_zero),
        masks,
        [(x_zero, pieces), (taps_one, 1), (short_taps, 1)],
        (small_all,),
        [(cube, BF16, steps(1, 47)), (cube, BF16, steps(1, 47))],
        [copies, ((4, ins), F32), ((3, 2, wide), F32)],
        [((total, B1, 3 * ins), BF16), acc],
        8,
    )
    ties = [[first_steps[1]], [first_steps[2], edges], [x_zero, small_all]] + [[first_halves[1]]] * last_step
    ties[last_step] = [hidden_one]
    wide_halves, _ = gather_halves(wide_send[None], gather_orders, ties[: last_step + 1])
    top_main = to_frames(after(output_grad, hidden_one).reshape(group, -1, LANES))
    came_one = to_all(sums)
    taps_two, taps_three = run(
        functools.partial(unpack_kernel, (0, 1), gather_orders, chans),
        (code_gather,),
        [],
        (),
        [slabs, slabs],
        [],
        [slab_blocks, slab_blocks, DMA((4,))],
        5,
        loose=wide_halves,
    )
    taps_two, taps_three = conv_taps(taps_two), conv_taps(taps_three)
    residual, sums = run(
        functools.partial(forward_kernel, own, count, 2, 46, True),
        masks,
        [(hidden_one, pieces), (taps_two, 1), (shortcut, 1)],
        (came_one, pairs[0]),
        [(cube, BF16, steps(2, 46))],
        [copies],
        [(cols, BF16), acc],
        9,
    )
    came_two = to_all(sums)
    (top,) = run(
        functools.partial(top_kernel, chans),
        (chan_scalar,),
        [(main, 1) for main in top_main],
        (after(edges, residual),),
        [(cube, BF16, 1)],
        [],
        [],
        10,
    )
    hidden_two, sums = run(
        functools.partial(forward_kernel, own, count, 3, 30, False),
        masks,
        [(residual, pieces), (after(taps_three, top), 1)],
        (came_two, pairs[1]),
        [(cube, BF16, steps(3, 30))],
        [copies],
        [(cols, BF16), acc],
        9,
    )
    came_three = to_all(sums)
    top_back, taps_four = run(
        functools.partial(top_back_kernel, 2, gather_orders, chans),
        (code_gather,) + masks,
        [(after(top, hidden_two), pieces)],
        (),
        [(cube, BF16, steps(3, 30)), slabs],
        [],
        [(cols, BF16), ((3, wide, 3 * wide), BF16), slab_blocks, DMA((2,))],
        8,
        loose=wide_halves,
    )
    taps_four = conv_taps(taps_four)
    dz_three, sums = run(
        functools.partial(top_norm_kernel, own, count),
        (),
        [(top_back, pieces), (hidden_two, pieces)],
        (came_three, pairs[2]),
        [(cube, BF16, 1)],
        [copies],
        [acc],
        4,
    )
    back_three = to_all(sums)

    def weight_grad(came, pair, values, d):
        blocks = (devices, slab_groups, rows, LANES)
        kept = ((devices // 2,) + blocks[1:], BF16)
        return run(
            functools.partial(weight_kernel, own, count, order_grads, chans),
            (code_grads,) + masks,
            [(values, pieces), (d, pieces)],
            (came, pair),
            [],
            [],
            [(cols, BF16), ((3, wide, own * B1), BF16), (blocks, BF16), DMA((2,))],
            9,
            [kept, kept],
        )

    four = weight_grad(came_three, pairs[2], hidden_two, after(top, dz_three))
    d_three, dz_two, sums = run(
        functools.partial(middle_kernel, own, count, 4, 44, False),
        masks,
        [(dz_three, pieces), (hidden_two, pieces), (after(taps_three, *four), 1), (residual, 1)],
        (back_three, came_three, pairs[2], came_two, pairs[1]),
        [(cube, BF16, 1), (cube, BF16, steps(4, 44))],
        [copies],
        [(cols, BF16), acc, ((3, wide, 3 * wide), BF16)],
        9,
    )
    back_two = to_all(sums)
    three = weight_grad(came_two, pairs[1], residual, d_three)
    low_top, dz_one, sums = run(
        functools.partial(middle_kernel, own, count, 5, 43, True),
        masks,
        [(dz_two, pieces), (residual, pieces), (top, pieces), (after(taps_two, *three), 1), (hidden_one, 1)],
        (back_two, came_two, pairs[1], came_one, pairs[0]),
        [(cube, BF16, 1), (cube, BF16, steps(5, 43))],
        [copies],
        [(cols, BF16), acc, ((3, wide, 3 * wide), BF16)],
        9,
    )
    back_one = to_all(sums)
    two = weight_grad(came_one, pairs[0], hidden_one, low_top)
    d_one, dz_zero, sums = run(
        functools.partial(bottom_kernel, own, count),
        masks,
        [(dz_one, pieces), (hidden_one, pieces), (after(taps_one, *two), 1), (short_taps, 1), (low_top, 1), (x_zero, 1)],
        (back_one, came_one, pairs[0], vec_zero),
        [(cube, BF16, 1), ((own, 2, B1, ins), BF16, own // fit(own, 28))],
        [((devices, 1, 2 * ins), F32)],
        [((total, B1, 2 * wide), BF16), ((2, 8, ins), F32), ((3, 2 * ins, 2 * wide), BF16)],
        8,
    )
    back_zero = to_all(sums)
    gave = lax.optimization_barrier((*two, *three, *four, dz_zero))
    wide_keep, wide_send = scatter_step(gave[:6:2], gave[1:6:2], order_grads, last_step)
    one_blocks = (devices, packed, LANES)
    one_kept = ((devices // 2,) + one_blocks[1:], BF16)
    one = run(
        functools.partial(first_weight_kernel, own, order_grads, chans, shard),
        (code_grads,) + masks,
        [(after(d_one, *wide_keep, *wide_send), pieces), (x_zero, 1), (low_top, 1)],
        (vec_zero,),
        [],
        [],
        [
            ((total, B1, 2 * wide), BF16),
            ((3, 2 * ins, own * B1), BF16),
            ((wide // LANES, 10 * ins + per * packed, LANES), F32),
            (one_blocks, BF16),
            DMA((2,)),
        ],
        8,
        [one_kept, one_kept],
    )
    wide_keep, wide_send = scatter_step(wide_keep, wide_send, order_grads, last_step - 1)
    (block_rows,) = run(
        functools.partial(last_kernel, own, count),
        masks,
        [(after(hidden_two, *one, *wide_keep, *wide_send), pieces), (taps_four, 1), (residual, 1)],
        (came_three, pairs[2]),
        [],
        [((chans, own, lane_rows, LANES), BF16)],
        [(cols, BF16)],
        12,
    )

    first_keep, first_send_half = scatter_step([one[0]], [one[1]], order_grads, last_step)
    (input_rows,) = run(
        functools.partial(input_kernel, own, count_zero),
        (),
        [(after(dz_zero, block_rows), 1), (x_zero, 1)],
        (back_zero, vec_zero),
        [],
        [((chans, own, lane_rows, LANES), BF16)],
        [],
        8,
    )

    input_came = lax.all_to_all(input_rows, "chan", 0, 0, tiled=True)
    block_came = lax.all_to_all(block_rows, "chan", 0, 0, tiled=True)
    block_out = block_came.reshape(group, -1).astype(F32)
    input_grad = input_came.reshape(group, -1).astype(F32)

    first_keep, first_send_half, wide_keep, wide_send = (
        [after(x[0], input_rows)] for x in (first_keep, first_send_half, wide_keep, wide_send)
    )
    wide_keep, wide_send = scatter_step(wide_keep, wide_send, order_grads, last_step - 2)
    wide_keep, wide_send = ([after(x[0], block_came)] for x in (wide_keep, wide_send))
    wide_sum = scatter_steps(wide_keep, wide_send, order_grads, last_step - 2).astype(F32)
    wide_sum = jnp.transpose(wide_sum.reshape(3, slab_groups, rows, per, columns), (0, 3, 1, 2, 4))
    wide_sum = wide_sum.reshape(3, per * slab_groups, rows, columns)[:, :9]
    grad_wide = jnp.transpose(wide_sum, (0, 2, 1, 3)).reshape(wide_weight.shape)
    first_sum = scatter_steps(first_keep, first_send_half, order_grads, last_step).astype(F32)
    grad_first = jnp.transpose(first_sum.reshape(packed, per, columns), (1, 0, 2)).reshape(-1, columns)[:shard]

    norm_sums = [jnp.sum(came, axis=(0, 1)).reshape(2, -1) for came in (back_zero, back_one, back_two, back_three)]
    grad_norms = jnp.stack([pack_norms([s[1] for s in norm_sums]), pack_norms([s[0] for s in norm_sums])])
    grad_norms = lax.dynamic_slice_in_dim(grad_norms, chan * norm_params.shape[2], norm_params.shape[2], 2)
    own_squares = jnp.sum(grad_first * grad_first) + jnp.sum(grad_wide * grad_wide)
    own_squares = own_squares + jnp.where(lax.axis_index("frames") == 0, jnp.sum(grad_norms * grad_norms), 0.0)
    squares = jnp.sum(to_all(after(jnp.broadcast_to(own_squares, (devices, 1, LANES)), input_came))[:, 0, 0])
    grad_norm = jnp.sqrt(squares)
    factor = clip_limit / jnp.maximum(grad_norm, clip_limit)
    first_next, first_mean_next, first_square_next = adam_step(
        first_weight, first_mean, first_square, grad_first * factor, conv_rate, weight_decay
    )
    wide_next, wide_mean_next, wide_square_next = adam_step(
        wide_weight, wide_mean, wide_square, grad_wide * factor, conv_rate, weight_decay
    )
    norm_next, norm_mean_next, norm_square_next = adam_step(
        norm_params, norm_mean, norm_square, grad_norms * factor, norm_rate, 0.0
    )
    return (
        block_out,
        input_grad,
        grad_norm,
        first_next,
        first_mean_next,
        first_square_next,
        first_next.astype(BF16),
        wide_next,
        wide_mean_next,
        wide_square_next,
        wide_next.astype(BF16),
        norm_next,
        norm_mean_next,
        norm_square_next,
    )


def solution(mesh):
    rows = P("frames", "chan")
    deep = P(None, "frames", "chan")
    norms = P(None, None, "chan")
    in_specs = (rows, P("frames"), rows, rows, rows, rows, deep, deep, deep, norms, norms, norms)
    out_specs = (rows, rows, P(), rows, rows, rows, rows, deep, deep, deep, deep, norms, norms, norms)
    return jax.shard_map(body, mesh=mesh, in_specs=in_specs, out_specs=out_specs, check_vma=False)
```

```python
import functools
import math

import jax
import jax.numpy as jnp
from jax import lax
from jax.experimental import pallas as pl
from jax.experimental.pallas import tpu as pltpu
from jax.sharding import PartitionSpec as P

B0 = 64
STEP = 10
B1 = 32
HALO = 6
LANES = 128

norm_epsilon = 1e-05
clip_limit = 100.0
beta_first = 0.9
beta_second = 0.999
adam_epsilon = 1e-08
conv_rate = 0.05
norm_rate = 0.5
weight_decay = 0.01

BOTH = ("chan", "frames")
VMEM_BYTES = 58 * 1024 * 1024
F32 = jnp.float32
BF16 = jnp.bfloat16
NT = (((1,), (1,)), ((), ()))


def to_all(copies):
    return lax.all_to_all(copies, BOTH, 0, 0, tiled=True)


def edges_of(block):
    count = lax.axis_size("frames")
    forward = [(i, i + 1) for i in range(count - 1)]
    low = lax.ppermute(block[block.shape[0] - HALO :].reshape(HALO, -1, LANES), "frames", forward)
    high = lax.ppermute(block[:HALO].reshape(HALO, -1, LANES), "frames", [(b, a) for a, b in forward])
    return jnp.concatenate([low, high], axis=0)


def by_distance(edge):
    parts = lax.axis_size("chan")
    return [edge] + [lax.ppermute(edge, "chan", [(i, i ^ d) for i in range(parts)]) for d in range(1, parts)]


def windows_of(block):
    parts = lax.axis_size("chan")
    own = block.shape[0] // parts
    padded = jnp.pad(block, ((HALO, HALO), (0, 0), (0, 0)))
    return jnp.stack([padded[k * own : k * own + own + 2 * HALO] for k in range(parts)])


def to_frames(block):
    parts = lax.axis_size("chan")
    chan = lax.axis_index("chan")
    own = block.shape[0] // parts
    padded = jnp.pad(block, ((HALO, HALO), (0, 0), (0, 0)))
    windows = [lax.dynamic_slice_in_dim(padded, (chan ^ d) * own, own + 2 * HALO, 0) for d in range(parts)]
    return [windows[0]] + [lax.ppermute(windows[d], "chan", [(i, i ^ d) for i in range(parts)]) for d in range(1, parts)]


def halves(axis, size):
    steps = []
    while size > 1:
        size //= 2
        steps.append((axis, size))
    return steps


def code_of(order, place):
    return sum(((place[axis] // step) % 2) << k for k, (axis, step) in enumerate(order))


def position(orders, me_ref, chan, frame):
    core = chan % 2
    return code_of(orders[core], {"chan": chan, "frames": frame}) ^ me_ref[core]


def exchange(value, orders, k):
    chans, count = lax.axis_size("chan"), lax.axis_size("frames")
    pairs = []
    for chan in range(chans):
        for frame in range(count):
            axis, step = orders[chan % 2][k]
            other = (chan ^ step, frame) if axis == "chan" else (chan, frame ^ step)
            pairs.append((chan * count + frame, other[0] * count + other[1]))
    return lax.ppermute(value, BOTH, pairs)


def gather_halves(block, orders, ties):
    blocks = []
    for k in range(len(orders[0]) - 1):
        block = jnp.concatenate([block, exchange(after(block, *ties[k]), orders, k)], axis=0)
        blocks.append(block)
    other = exchange(after(block, *ties[-1]), orders, len(orders[0]) - 1)
    return (block, other), blocks + [other]


def scatter_step(keeps, sends, orders, k):
    came = [exchange(send, orders, k) for send in sends]
    half = max(keeps[0].shape[0] // 2, 1)

    def added(part):
        return jnp.concatenate([(k[part].astype(F32) + c[part].astype(F32)).astype(BF16) for k, c in zip(keeps, came)], axis=1)

    return [added(slice(0, half))], [added(slice(half, None))]


def scatter_steps(keeps, sends, orders, count):
    for k in reversed(range(count)):
        keeps, sends = scatter_step(keeps, sends, orders, k)
    return keeps[0][0]


def after(value, *others):
    return lax.optimization_barrier((value, *others))[0]


def fit(count, target, unit=1):
    return max([k for k in range(unit, target + 1, unit) if count % k == 0], default=count)


def loop(low, high, target, body, unit=1):
    return spans(low, high - low, target, body, unit)


def spans(low, count, target, body, unit=1):
    chunk = fit(count, target, unit)

    def step(i, carry):
        body(low + i * chunk, chunk, i)
        return carry

    if chunk == count:
        body(low, chunk, 0)
    else:
        lax.fori_loop(0, count // chunk, step, 0)
    return chunk


def unrolled(low, high, target, body):
    count = -(-(high - low) // target)
    ends = [low + (high - low) * k // count for k in range(count + 1)]
    for number in range(count):
        body(ends[number], ends[number + 1] - ends[number], number)


def steps_of(low, high, target):
    return -(-(high - low) // target)


class Fetched:
    def __init__(self, source, ref, sems):
        self.source, self.ref, self.sems = source, ref, sems
        self.pieces = sems.shape[0]
        self.size = ref.shape[0] // self.pieces

    def copy(self, number):
        rows = pl.ds(number * self.size, self.size)
        return pltpu.make_async_copy(self.source.at[rows], self.ref.at[rows], self.sems.at[number])

    def start(self):
        for number in range(self.pieces):
            self.copy(number).start()

    def need(self, number):
        self.copy(number).wait()

    def need_all(self):
        for number in range(self.pieces):
            self.need(number)


class Sent:
    def __init__(self, target, ref, sems):
        self.target, self.ref, self.sems = target, ref, sems
        self.shape, self.dtype = ref.shape, ref.dtype
        self.sent = []

    def copy(self, base, chunk, number):
        rows = pl.ds(base, chunk)
        return pltpu.make_async_copy(self.ref.at[rows], self.target.at[rows], self.sems.at[number])

    def send(self, base, chunk, number):
        self.sent.append((base, chunk, number))
        self.copy(base, chunk, number).start()

    def finish(self):
        for one in self.sent:
            self.copy(*one).wait()


def sigmoid(z):
    return 0.5 * jnp.tanh(0.5 * z) + 0.5


def dot(a, b):
    return jnp.dot(a, b, preferred_element_type=F32)


def dot_nt(a, b):
    return lax.dot_general(a, b, NT, preferred_element_type=F32)


def chosen(rows, columns, source):
    r = lax.broadcasted_iota(jnp.int32, (rows, columns), 0)
    c = lax.broadcasted_iota(jnp.int32, (rows, columns), 1)
    return (c == source(r)).astype(BF16)


def same(r):
    return r


def transposed(rows):
    return dot_nt(chosen(rows.shape[1], rows.shape[1], same), rows).astype(BF16)


def shifts(flat):
    rows = flat.shape[0]
    bins = lax.broadcasted_iota(jnp.int32, flat.shape, 0) % B1
    below = jnp.where(bins == 0, 0.0, pltpu.roll(flat, 1, 0))
    above = jnp.where(bins == B1 - 1, 0.0, pltpu.roll(flat, rows - 1, 0))
    return below, above


def mask_frames(partial, mask_ref, base, chunk):
    cube = partial.reshape(chunk, B1, partial.shape[-1])
    return jnp.concatenate([cube[k] * mask_ref[base + k] for k in range(chunk)], axis=0)


def rows_of(ref, base, chunk):
    return ref[pl.ds(base, chunk)].reshape(chunk * B1, ref.shape[-1])


def put(ref, base, chunk, value):
    ref[pl.ds(base, chunk)] = value.reshape(chunk, B1, value.shape[-1]).astype(ref.dtype)


def taps_sum(cols_ref, taps_ref, masks, base, chunk, product=dot):
    total = None
    for tap in (1, 0, 2):
        partial = product(rows_of(cols_ref, base + tap - 1, chunk), taps_ref[tap])
        if tap == 0:
            partial = mask_frames(partial, masks[0], base, chunk)
        if tap == 2:
            partial = mask_frames(partial, masks[1], base, chunk)
        total = partial if total is None else total + partial
    return total


def own_rows(value, base, chunk, low, high):
    if isinstance(base, int) and low <= base and base + chunk <= high:
        return value
    frame = base + lax.broadcasted_iota(jnp.int32, value.shape, 0) // B1
    return jnp.where((frame >= low) & (frame < high), value, 0.0)


def add_sums(acc_ref, first, second):
    rows, channels = first.shape
    acc_ref[0] += jnp.sum(first.reshape(rows // 8, 8, channels), axis=0)
    acc_ref[1] += jnp.sum(second.reshape(rows // 8, 8, channels), axis=0)


def spread_sums(acc_ref, copies_ref):
    channels = acc_ref.shape[-1]
    for k in range(2):
        row = jnp.sum(acc_ref[k], axis=0, keepdims=True)
        copies_ref[:, :, k * channels : (k + 1) * channels] = jnp.broadcast_to(
            row[None], (copies_ref.shape[0], 1, channels)
        )


def came_sums(came_ref):
    total = jnp.sum(came_ref[...], axis=0)
    half = total.shape[-1] // 2
    return total[:, :half], total[:, half:]


def norm_of(came_ref, pair_ref, count):
    first, second = came_sums(came_ref)
    mean = first / count
    spread = lax.rsqrt(second / count - mean * mean + norm_epsilon)
    return mean, spread, pair_ref[0:1], pair_ref[1:2]


def norm_rows(vec_ref):
    return vec_ref[0:1], vec_ref[1:2], vec_ref[2:3], vec_ref[3:4]


def normal(values, norm):
    return (values.astype(F32) - norm[0]) * norm[1]


def activated(values, norm):
    z = normal(values, norm) * norm[2] + norm[3]
    return z * sigmoid(z)


def back_act(q, values, norm):
    xhat = normal(values, norm)
    z = xhat * norm[2] + norm[3]
    gate = sigmoid(z)
    return q * gate * (1.0 + z * (1.0 - gate)), xhat


def back_norm(dz, values, norm, sums, count):
    xhat = normal(values, norm)
    return norm[2] * norm[1] * (dz.astype(F32) - sums[0] / count - xhat * (sums[1] / count))


def swap_halves(value):
    return pltpu.roll(value, LANES // 2, 1)


def halves_of(first, second):
    low = lax.broadcasted_iota(jnp.int32, first.shape, 1) < LANES // 2
    return jnp.where(low, first, swap_halves(second)), jnp.where(low, swap_halves(first), second)


def fetch_wide(layer, own_ref, other_ref, came_ref, sems):
    half = own_ref.shape[0]
    fetches = [
        pltpu.make_async_copy(ref.at[:, layer], came_ref.at[pl.ds(k * half, half)], sems.at[k])
        for k, ref in enumerate((own_ref, other_ref))
    ]
    for fetch in fetches:
        fetch.start()
    return fetches


def unpack_wide(orders, chans, me_ref, came_ref, taps_ref):
    devices, groups, rows, _ = came_ref.shape
    count = devices // chans
    per = LANES // (taps_ref.shape[2] // chans)
    wide = per * LANES
    piece = LANES // per
    spread = chosen(wide, wide, lambda r: (r % LANES) // piece * LANES + r // LANES * piece + r % piece)
    for frame in range(count):
        for side in range(chans // per):
            parts = []
            for k in range(per):
                at = position(orders, me_ref, side * per + k, frame)
                parts.append(came_ref[at].reshape(groups * rows, LANES))
            result = dot_nt(jnp.concatenate(parts, axis=1), spread).astype(BF16)
            for slab in range(per):
                for group in range(groups):
                    if slab * groups + group < 9:
                        taps_ref[slab * groups + group, frame * rows : (frame + 1) * rows, side * LANES : (side + 1) * LANES] = result[
                            group * rows : (group + 1) * rows, slab * LANES : (slab + 1) * LANES
                        ]


def unpack_kernel(layers, orders, chans, me_ref, own_ref, other_ref, *rest):
    outs, came_refs, sems = rest[: len(layers)], rest[len(layers) : -1], rest[-1]
    fetches = [
        fetch_wide(layer, own_ref, other_ref, came_refs[n], sems.at[pl.ds(2 * n, 2)]) for n, layer in enumerate(layers)
    ]
    for n, out in enumerate(outs):
        for fetch in fetches[n]:
            fetch.wait()
        unpack_wide(orders, chans, me_ref, came_refs[n], out.ref)
        out.send(0, 9, 0)
    for out in outs:
        out.finish()


def turn_taps(taps_ref, turned_ref):
    wide = taps_ref.shape[-1]
    for kt in range(3):
        for kf in range(3):
            turned_ref[2 - kt, :, kf * wide : (kf + 1) * wide] = taps_ref[kt, kf * wide : (kf + 1) * wide]


def pack_wide(order, chans, me_ref, slabs, out_ref):
    devices, groups, rows, _ = out_ref.shape
    count = devices // chans
    per = LANES // (slabs[0].shape[1] // chans)
    wide = per * LANES
    piece = LANES // per
    gather = chosen(wide, wide, lambda r: (r % LANES) // piece * LANES + r // LANES * piece + r % piece)
    for group in range(groups):
        for side in range(chans // per):
            parts = []
            for slab in range(per):
                tap = slab * groups + group
                tap = tap if tap < 9 else 8
                parts.append(slabs[tap][:, side * LANES : (side + 1) * LANES])
            result = dot_nt(jnp.concatenate(parts, axis=1), gather).astype(BF16)
            for k in range(per):
                for frame in range(count):
                    at = position(order, me_ref, side * per + k, frame)
                    out_ref[at, group] = result[frame * rows : (frame + 1) * rows, k * LANES : (k + 1) * LANES]


def unpack_first(orders, chans, shard, count_zero, me_ref, own_ref, other_ref, taps_ref, short_ref, vec_ref, pairs_ref, raw_ref, came_ref, sems):
    half = own_ref.shape[0]
    fetches = [
        pltpu.make_async_copy(ref, came_ref.at[pl.ds(k * half, half)], sems.at[k]) for k, ref in enumerate((own_ref, other_ref))
    ]
    for fetch in fetches:
        fetch.start()
    for fetch in fetches:
        fetch.wait()
    devices = came_ref.shape[0]
    count = devices // chans
    ins, outs = short_ref.shape
    per = LANES // (outs // chans)
    rows = packed_rows(shard, per)
    wide = per * LANES
    piece = LANES // per
    spread = chosen(wide, wide, lambda r: (r % LANES) // piece * LANES + r // LANES * piece + r % piece)
    for frame in range(count):
        for side in range(chans // per):
            parts = [came_ref[position(orders, me_ref, side * per + k, frame), 0:rows] for k in range(per)]
            result = dot_nt(jnp.concatenate(parts, axis=1), spread)
            for slab in range(per):
                start = slab * rows
                size = min(rows, shard - start)
                if size > 0:
                    raw_ref[side, frame * shard + start : frame * shard + start + size] = result[
                        :size, slab * LANES : (slab + 1) * LANES
                    ]
    for tap in range(9):
        kt, kf = tap // 3, tap % 3
        for side in range(outs // LANES):
            lanes = slice(side * LANES, (side + 1) * LANES)
            taps_ref[kt, kf * ins : (kf + 1) * ins, lanes] = raw_ref[side, pl.ds(tap, ins, stride=9)].astype(BF16)
    for side in range(outs // LANES):
        short_ref[:, side * LANES : (side + 1) * LANES] = raw_ref[side, 9 * ins : 10 * ins].astype(BF16)
    unpack_small(count_zero, came_ref, rows, vec_ref, pairs_ref)


def unpack_small(count_zero, came_ref, at, vec_ref, pairs_ref):
    parts = [jnp.sum(came_ref[:, at + 16 * k : at + 16 * (k + 1)].astype(F32), axis=0) for k in range(2)]
    sums = parts[0] + parts[1]
    average = sums[0:1] / count_zero
    vec_ref[0:1] = average
    vec_ref[1:2] = lax.rsqrt(sums[1:2] / count_zero - average * average + norm_epsilon)
    vec_ref[2:3] = sums[2:3]
    vec_ref[3:4] = sums[9:10]
    c = lax.broadcasted_iota(jnp.int32, (LANES, 2 * LANES), 1)
    r = lax.broadcasted_iota(jnp.int32, (LANES, 2 * LANES), 0)
    for side in range(2):
        place = (c == 2 * r + side).astype(BF16)
        spread_rows = [dot(part.astype(BF16), place) for part in (parts[0], parts[1])]
        both = spread_rows[0] + spread_rows[1]
        for k in range(3):
            for kind in range(2):
                row = both[2 + 7 * kind + 1 + 2 * k + side : 2 + 7 * kind + 2 + 2 * k + side]
                pairs_ref[k, kind : kind + 1] = row if side == 0 else pairs_ref[k, kind : kind + 1] + row


def turn_first(taps, short, turned_ref):
    ins, outs = short.ref.shape
    taps.need_all()
    short.need_all()
    for kt in range(3):
        turned_ref[2 - kt, 0:ins, 0:outs] = taps.ref[kt, ins : 2 * ins]
        turned_ref[2 - kt, 0:ins, outs:] = jnp.zeros((ins, outs), BF16)
        turned_ref[2 - kt, ins:, 0:outs] = taps.ref[kt, 2 * ins :]
        turned_ref[2 - kt, ins:, outs:] = taps.ref[kt, 0:ins]


def pack_first(order, chans, shard, me_ref, raw_ref, out_ref):
    devices, rows, _ = out_ref.shape
    count = devices // chans
    outs = raw_ref.shape[0] * LANES
    per = LANES // (outs // chans)
    wide = per * LANES
    piece = LANES // per
    gather = chosen(wide, wide, lambda r: (r % LANES) // piece * LANES + r // LANES * piece + r % piece)
    for frame in range(count):
        for side in range(chans // per):
            parts = [raw_ref[side, frame * shard + slab * rows : frame * shard + (slab + 1) * rows] for slab in range(per)]
            result = dot_nt(jnp.concatenate(parts, axis=1).astype(BF16), gather).astype(BF16)
            for k in range(per):
                at = position(order, me_ref, side * per + k, frame)
                out_ref[at] = result[:, k * LANES : (k + 1) * LANES]


def packed_rows(shard, per):
    return -(-shard // (per * 16)) * 16


def frames_in(chan_ref, mains, edges_ref, total, target, body):
    parts = len(mains)
    for main in mains:
        main.need_all()
    for low, at, part in ((0, 0, 0), (total - HALO, HALO, parts - 1)):

        @pl.when(chan_ref[0] == part)
        def _():
            for d, main in enumerate(mains):
                size = main.ref.shape[1]
                main.ref[low : low + HALO] = edges_ref[d, at : at + HALO, size : 2 * size]

    def piece(at, chunk, _):
        cubes = jnp.concatenate([main.ref[pl.ds(at, chunk)] for main in mains], axis=1)
        body(cubes.reshape(chunk * cubes.shape[1], LANES), at, chunk)

    loop(0, total, target, piece, 2)


def lane_row(chan_ref, q, size):
    return (q // size ^ chan_ref[0]) * size + q % size


def frames_out(rows, count, out_ref, at):
    parts, _, size, _ = out_ref.shape
    cube = rows.reshape(count, parts * size, LANES)
    for s in range(parts):
        out_ref[s, pl.ds(at, count)] = cube[:, s * size : (s + 1) * size].astype(out_ref.dtype)


def pieces_of(total):
    return fit(total, 4)


def channels_of(ref, base, chunk, parity):
    return ref[pl.ds(base, chunk), parity].reshape(chunk * B1, ref.shape[-1])


def signal_kernel(chan_ref, main, edges_ref, x_out):
    parts, _, size, _ = main.ref.shape
    x_ref = x_out.ref
    total = x_ref.shape[0]
    channels = x_ref.shape[-1]
    half = LANES // 2
    split = chosen(LANES, LANES, lambda r: r // half * half + r % B1 * 2 + r % half // B1)
    order = chosen(channels, channels, lambda r: r // half + r % half * 2)

    def turn(values, base, chunk):
        turned = dot_nt(split, values)
        for parity in range(2):
            pairs = []
            for pair in range(chunk // 2):
                lanes = turned[:, pair * LANES : (pair + 1) * LANES]
                even = lanes[parity * B1 : (parity + 1) * B1]
                odd = lanes[half + parity * B1 : half + (parity + 1) * B1]
                pairs.extend(halves_of(even, odd))
            x = dot(jnp.concatenate(pairs, axis=0).astype(BF16), order)
            x_ref[pl.ds(base, chunk), parity] = x.reshape(chunk, B1, channels).astype(BF16)

    main.need_all()
    for low, at, part in ((0, 0, 0), (total - HALO, HALO, parts - 1)):

        @pl.when(chan_ref[0] == part)
        def _():
            for s in range(parts):
                main.ref[s, low : low + HALO] = edges_ref[s ^ part, at : at + HALO, 0:size]

    def piece(at, chunk, _):
        cubes = jnp.concatenate([main.ref[s, pl.ds(at, chunk)] for s in range(parts)], axis=1)
        turn(cubes.reshape(chunk * parts * size, LANES), at, chunk)

    loop(0, total, 48, piece, 2)
    x_out.send(0, total, 0)
    x_out.finish()


def first_kernel(own, prev_ref, next_ref, x, taps, short, vec_ref, h_out, s_out, copies_ref, cols_ref, acc_ref):
    total = x.ref.shape[0]
    channels = x.ref.shape[-1]
    norm = norm_rows(vec_ref)

    def build(base, chunk):
        acts = [activated(channels_of(x.ref, base, chunk, parity), norm) for parity in range(2)]
        below, _ = shifts(acts[1])
        put(cols_ref, base, chunk, jnp.concatenate([below, acts[0], acts[1]], axis=1))

    by_pieces([x], total, 12, build)
    acc_ref[...] = jnp.zeros_like(acc_ref)
    taps.need_all()
    short.need_all()

    def conv(base, chunk, number):
        result = taps_sum(cols_ref, taps.ref, (prev_ref, next_ref), base, chunk)
        put(h_out.ref, base, chunk, result)
        h_out.send(base, chunk, number)
        mine = own_rows(result, base, chunk, HALO, HALO + own)
        add_sums(acc_ref, mine, mine * mine)
        even = rows_of(cols_ref, base, chunk)[:, channels : 2 * channels]
        put(s_out.ref, base, chunk, dot(even, short.ref[...]))
        s_out.send(base, chunk, number)

    unrolled(1, total - 1, 12, conv)
    spread_sums(acc_ref, copies_ref)
    h_out.finish()
    s_out.finish()


def by_pieces(fetched, total, target, body):
    pieces = fetched[0].pieces
    size = total // pieces

    def piece(number, carry):
        for operand in fetched:
            operand.need(number)
        spans(number * size, size, target, lambda base, chunk, _: body(base, chunk))
        return carry

    lax.fori_loop(0, pieces, piece, 0)


def activate_into(h, norm, cols_ref):
    def build(base, chunk):
        act = activated(rows_of(h.ref, base, chunk), norm)
        below, above = shifts(act)
        put(cols_ref, base, chunk, jnp.concatenate([below, act, above], axis=1))

    by_pieces([h], cols_ref.shape[0], 24, build)


def forward_kernel(own, count, lead, target, with_short, prev_ref, next_ref, h, taps, *rest):
    if with_short:
        s, came_ref, pair_ref, out, copies_ref, vec_ref, cols_ref, acc_ref = rest
    else:
        came_ref, pair_ref, out, copies_ref, vec_ref, cols_ref, acc_ref = rest
    total = cols_ref.shape[0]
    norm = norm_of(came_ref, pair_ref, count)
    for k in range(4):
        vec_ref[k : k + 1] = norm[k]
    activate_into(h, norm, cols_ref)
    acc_ref[...] = jnp.zeros_like(acc_ref)
    taps.need_all()

    def conv(base, chunk, number):
        result = taps_sum(cols_ref, taps.ref, (prev_ref, next_ref), base, chunk)
        if with_short:
            if number == 0:
                s.need_all()
            result = result + rows_of(s.ref, base, chunk).astype(F32)
        put(out.ref, base, chunk, result)
        out.send(base, chunk, number)
        mine = own_rows(result, base, chunk, HALO, HALO + own)
        add_sums(acc_ref, mine, mine * mine)

    unrolled(lead, total - lead, target, conv)
    spread_sums(acc_ref, copies_ref)
    out.finish()


def shift_into(value, base, chunk, cols_ref):
    below, above = shifts(value)
    put(cols_ref, base, chunk, jnp.concatenate([above, value, below], axis=1))


def top_kernel(parts, chan_ref, *rest):
    mains, (edges_ref, e_out) = rest[:parts], rest[parts:]
    size = mains[0].ref.shape[1]
    total, _, wide = e_out.shape
    quarter = LANES // 4
    half = LANES // 2
    order = chosen(wide, wide, lambda r: r // half + lane_row(chan_ref, r % half, size) * 4)
    eye = chosen(LANES, LANES, same)

    def turn(values, base, chunk):
        turned = dot_nt(eye, values)
        frames = []
        for pair in range(chunk // 2):
            lanes = turned[:, pair * LANES : (pair + 1) * LANES]
            sides = [
                halves_of(
                    lanes[2 * side * quarter : (2 * side + 1) * quarter],
                    lanes[(2 * side + 1) * quarter : (2 * side + 2) * quarter],
                )
                for side in range(2)
            ]
            frames.extend([jnp.concatenate([sides[0][k], sides[1][k]], axis=1) for k in range(2)])
        put(e_out.ref, base, chunk, dot(jnp.concatenate(frames, axis=0).astype(BF16), order))

    frames_in(chan_ref, mains, edges_ref, total, 48, turn)
    e_out.send(0, total, 0)
    e_out.finish()


def top_back_kernel(layer, orders, chans, me_ref, prev_ref, next_ref, e, own_ref, other_ref, q_out, taps_out, cols_ref, turned_ref, came_ref, sems):
    total = q_out.shape[0]
    wide = e.ref.shape[-1]
    fetches = fetch_wide(layer, own_ref, other_ref, came_ref, sems)

    def build(base, chunk):
        shift_into(rows_of(e.ref, base, chunk).astype(F32), base, chunk, cols_ref)

    by_pieces([e], total, 24, build)
    for fetch in fetches:
        fetch.wait()
    unpack_wide(orders, chans, me_ref, came_ref, taps_out.ref)
    taps_out.send(0, 9, 0)
    for kt in range(3):
        for kf in range(3):
            turned_ref[2 - kt, :, kf * wide : (kf + 1) * wide] = taps_out.ref[3 * kt + kf]

    def back(base, chunk, number):
        put(q_out.ref, base, chunk, taps_sum(cols_ref, turned_ref, (prev_ref, next_ref), base, chunk, dot_nt))
        q_out.send(base, chunk, number)

    unrolled(3, total - 3, 12, back)
    taps_out.finish()
    q_out.finish()


def top_norm_kernel(own, count, q, h, came_ref, pair_ref, dz_out, copies_ref, vec_ref, acc_ref):
    total = dz_out.shape[0]
    norm = norm_of(came_ref, pair_ref, count)
    for k in range(4):
        vec_ref[k : k + 1] = norm[k]
    acc_ref[...] = jnp.zeros_like(acc_ref)

    def back(base, chunk):
        dz, xhat = back_act(rows_of(q.ref, base, chunk).astype(F32), rows_of(h.ref, base, chunk), norm)
        put(dz_out.ref, base, chunk, dz)
        mine = own_rows(dz, base, chunk, HALO, HALO + own)
        add_sums(acc_ref, mine, own_rows(dz * xhat, base, chunk, HALO, HALO + own))

    by_pieces([q, h], total, 24, back)
    dz_out.send(0, total, 0)
    spread_sums(acc_ref, copies_ref)
    dz_out.finish()


def last_kernel(own, prev_ref, next_ref, h, taps, x, vec_ref, y_ref, cols_ref):
    wide = cols_ref.shape[-1] // 3
    half = LANES // 2
    order = chosen(wide, wide, lambda r: r // half + r % half * 4)
    eye = chosen(LANES, LANES, same)
    activate_into(h, norm_rows(vec_ref), cols_ref)
    taps.need_all()
    x.need_all()

    def conv(base, chunk, _):
        result = taps_sum(cols_ref, taps.ref, (prev_ref, next_ref), base, chunk) + rows_of(x.ref, base, chunk).astype(F32)
        mixed = dot_nt(result.astype(BF16), order)
        cube = mixed.reshape(chunk, B1, wide)
        for pair in range(chunk // 2):
            stack = []
            for side in range(wide // LANES):
                lanes = slice(side * LANES, (side + 1) * LANES)
                stack.extend(halves_of(cube[2 * pair][:, lanes], cube[2 * pair + 1][:, lanes]))
            turned = dot_nt(eye, jnp.concatenate(stack, axis=0).astype(BF16))
            frames_out(turned, 2, y_ref, base - HALO + 2 * pair)

    unrolled(HALO, HALO + own, 12, conv)


def middle_kernel(own, count, lead, target, with_top, prev_ref, next_ref, dz, h, *rest):
    if with_top:
        e, *rest = rest
    taps, low, back_ref, vec_ref, low_vec_ref, d_out, dz_out, copies_ref, sums_ref, cols_ref, acc_ref, turned_ref = rest
    total = cols_ref.shape[0]
    norm, low_norm = norm_rows(vec_ref), norm_rows(low_vec_ref)
    sums = came_sums(back_ref)
    sums_ref[0:1], sums_ref[1:2] = sums

    def build(base, size):
        d = back_norm(rows_of(dz.ref, base, size), rows_of(h.ref, base, size), norm, sums, count)
        if with_top:
            d = d + rows_of(e.ref, base, size).astype(F32)
        put(d_out.ref, base, size, d)
        shift_into(d, base, size, cols_ref)

    by_pieces([dz, h, e] if with_top else [dz, h], total, 24, build)
    d_out.send(0, total, 0)
    acc_ref[...] = jnp.zeros_like(acc_ref)
    taps.need_all()
    turn_taps(taps.ref, turned_ref)

    def back(base, chunk, number):
        q = taps_sum(cols_ref, turned_ref, (prev_ref, next_ref), base, chunk, dot_nt)
        if number == 0:
            low.need_all()
        new, xhat = back_act(q, rows_of(low.ref, base, chunk), low_norm)
        put(dz_out.ref, base, chunk, new)
        dz_out.send(base, chunk, number)
        mine = own_rows(new, base, chunk, HALO, HALO + own)
        add_sums(acc_ref, mine, mine * xhat)

    unrolled(lead, total - lead, target, back)
    spread_sums(acc_ref, copies_ref)
    d_out.finish()
    dz_out.finish()


def give(buffer_ref, keep_ref, send_ref, sems):
    half = keep_ref.shape[0]
    keep = pltpu.make_async_copy(buffer_ref.at[pl.ds(0, half)], keep_ref, sems.at[0])
    send = pltpu.make_async_copy(buffer_ref.at[pl.ds(half, half)], send_ref, sems.at[1])
    keep.start()
    send.start()
    keep.wait()
    send.wait()


def weight_kernel(
    own, order, chans, me_ref, h, d, vec_ref, lanes_ref, keep_ref, send_ref,
    cols_ref, turned_ref, buffer_ref, sems,
):
    norm = norm_rows(vec_ref)
    wide = h.ref.shape[-1]

    def build(base, chunk):
        shift_into(rows_of(d.ref, base, chunk).astype(F32), base, chunk, cols_ref)

    chunk = fit(own, 28, 4)
    staged = all(HALO + chunk * (i + 1) <= h.size * (i + 2) for i in range(own // chunk)) and own // chunk + 1 == h.pieces
    if not staged:
        h.need_all()

    def turn(base, chunk, number):
        if staged:
            if number == 0:
                h.need(0)
            h.need(number + 1)
        u = activated(rows_of(h.ref, HALO + base, chunk), norm)
        columns = pl.ds(base * B1, chunk * B1)
        turned = transposed(u.astype(BF16))
        turned_ref[0, :, columns] = turned * lanes_ref[1:2, columns]
        turned_ref[1, :, columns] = turned
        turned_ref[2, :, columns] = turned * lanes_ref[0:1, columns]

    for number in range(own // chunk):
        turn(number * chunk, chunk, number)
    by_pieces([d], cols_ref.shape[0], 24, build)
    slabs = []
    for tap in range(3):
        other = cols_ref[pl.ds(HALO + 1 - tap, own)].reshape(own * B1, cols_ref.shape[-1])
        grad = dot(turned_ref[tap], other).astype(BF16)
        slabs.extend([grad[:, k * wide : (k + 1) * wide] for k in range(3)])
    pack_wide(order, chans, me_ref, slabs, buffer_ref)
    give(buffer_ref, keep_ref, send_ref, sems)


def bottom_kernel(
    own, count, prev_ref, next_ref, dz, h, taps, short, e1, x, back_ref, high_vec_ref, vec_ref,
    d_out, dz_out, copies_ref, sums_ref, cols_ref, acc_ref, turned_ref,
):
    total = cols_ref.shape[0]
    norm, low_norm = norm_rows(high_vec_ref), norm_rows(vec_ref)
    sums = came_sums(back_ref)
    sums_ref[0:1], sums_ref[1:2] = sums
    channels = x.ref.shape[-1]

    def build(base, size):
        d = back_norm(rows_of(dz.ref, base, size), rows_of(h.ref, base, size), norm, sums, count)
        put(d_out.ref, base, size, d)
        _, above = shifts(d)
        put(cols_ref, base, size, jnp.concatenate([d, above], axis=1))

    by_pieces([dz, h], total, 24, build)
    d_out.send(0, total, 0)
    acc_ref[...] = jnp.zeros_like(acc_ref)
    turn_first(taps, short, turned_ref)
    e1.need_all()
    x.need_all()

    def back(base, chunk, number):
        q = taps_sum(cols_ref, turned_ref, (prev_ref, next_ref), base, chunk, dot_nt)
        r = dot_nt(rows_of(e1.ref, base, chunk), short.ref[...])
        parts = (q[:, :channels] + r, q[:, channels:])
        for parity in range(2):
            new, xhat = back_act(parts[parity], channels_of(x.ref, base, chunk, parity), low_norm)
            dz_out.ref[pl.ds(base - HALO, chunk), parity] = new.reshape(chunk, B1, channels).astype(BF16)
            add_sums(acc_ref, new, new * xhat)
        dz_out.send(base - HALO, chunk, number)

    unrolled(HALO, HALO + own, 12, back)
    spread_sums(acc_ref, copies_ref)
    d_out.finish()
    dz_out.finish()


def first_weight_kernel(
    own, order, chans, shard, me_ref, d, x, e1, vec_ref, lanes_ref, keep_ref, send_ref,
    cols_ref, turned_ref, raw_ref, buffer_ref, sems,
):
    norm = norm_rows(vec_ref)
    channels = x.ref.shape[-1]
    wide = d.ref.shape[-1]

    def build(base, size):
        value = rows_of(d.ref, base, size)
        _, above = shifts(value.astype(F32))
        put(cols_ref, base, size, jnp.concatenate([value, above.astype(BF16)], axis=1))

    by_pieces([d], cols_ref.shape[0], 24, build)
    x.need_all()
    e1.need_all()

    def turn(base, chunk):
        columns = pl.ds(base * B1, chunk * B1)
        for parity in range(2):
            place = slice(parity * channels, (parity + 1) * channels)
            turned = transposed(activated(channels_of(x.ref, HALO + base, chunk, parity), norm).astype(BF16))
            turned_ref[0, place, columns] = turned * lanes_ref[1:2, columns]
            turned_ref[1, place, columns] = turned
            turned_ref[2, place, columns] = turned * lanes_ref[0:1, columns]

    chunk = fit(own, 28, 4)
    for number in range(own // chunk):
        turn(number * chunk, chunk)
    for tap in range(3):
        other = cols_ref[pl.ds(HALO + 1 - tap, own)].reshape(own * B1, cols_ref.shape[-1])
        grad = dot(turned_ref[tap], other)
        slabs = (grad[channels:, wide:], grad[:channels, :wide], grad[channels:, :wide])
        for kf in range(3):
            for side in range(wide // LANES):
                raw_ref[side, pl.ds(3 * tap + kf, channels, stride=9)] = slabs[kf][:, side * LANES : (side + 1) * LANES]
    short = dot(turned_ref[1, 0:channels], e1.ref[pl.ds(HALO, own)].reshape(own * B1, wide))
    rest = raw_ref.shape[1] - 10 * channels
    for side in range(wide // LANES):
        raw_ref[side, 9 * channels : 10 * channels] = short[:, side * LANES : (side + 1) * LANES]
        raw_ref[side, 10 * channels :] = jnp.zeros((rest, LANES), F32)
    pack_first(order, chans, shard, me_ref, raw_ref, buffer_ref)
    give(buffer_ref, keep_ref, send_ref, sems)


def input_kernel(own, count, dz, x, back_ref, vec_ref, out_ref, sums_ref):
    norm = norm_rows(vec_ref)
    sums = came_sums(back_ref)
    sums_ref[0:1], sums_ref[1:2] = sums
    channels = x.ref.shape[-1]
    half = LANES // 2
    order = chosen(channels, channels, lambda r: r // half + r % half * 2)
    eye = chosen(LANES, LANES, same)
    split = chosen(LANES, LANES, lambda r: r // half * half + r % 2 * B1 + r % half // 2)
    dz.need_all()
    x.need_all()

    def build(base, chunk, _):
        mixed = []
        for parity in range(2):
            g = back_norm(
                channels_of(dz.ref, base, chunk, parity), channels_of(x.ref, HALO + base, chunk, parity), norm, sums, count
            )
            mixed.append(dot_nt(g.astype(BF16), order).reshape(chunk, B1, channels))
        for pair in range(chunk // 2):
            even, odd = [], []
            for parity in range(2):
                first, second = halves_of(mixed[parity][2 * pair], mixed[parity][2 * pair + 1])
                even.append(first)
                odd.append(second)
            stack = jnp.concatenate(even + odd, axis=0).astype(BF16)
            turned = dot_nt(eye, dot(split, stack).astype(BF16))
            frames_out(turned, 2, out_ref, base + 2 * pair)

    loop(0, own, 28, build, 2)


SMEM = pl.BlockSpec(memory_space=pltpu.SMEM)
VMEM = pl.BlockSpec(memory_space=pltpu.VMEM)
HBM = pl.BlockSpec(memory_space=pl.ANY)
DMA = pltpu.SemaphoreType.DMA


def run(kernel, scalars, fetched, operands, sent, outs, scratch, micros, plain=(), loose=()):
    arrays = [array for array, _ in fetched]
    buffers = [pltpu.VMEM(array.shape, array.dtype) for array in arrays] + [pltpu.VMEM(shape, kind) for shape, kind, _ in sent]
    sems = [DMA((pieces,)) for _, pieces in fetched] + [DMA((pieces,)) for _, _, pieces in sent]
    counts = (len(scalars), len(fetched), len(loose), len(operands), len(sent), len(plain), len(outs), len(scratch), len(buffers), len(sems))

    def whole(*refs):
        groups, at = [], 0
        for count in counts:
            groups.append(refs[at : at + count])
            at += count
        small, sources, left, inputs, targets, copied, results, own, held, marks = groups
        incoming = [Fetched(*triple) for triple in zip(sources, held, marks)]
        leaving = [Sent(*triple) for triple in zip(targets, held[len(incoming) :], marks[len(incoming) :])]
        for operand in incoming:
            operand.start()
        kernel(*small, *incoming, *left, *inputs, *leaving, *copied, *results, *own)

    made = [(shape, kind) for shape, kind, _ in sent] + list(plain) + list(outs)
    moved = sum(x.size * x.dtype.itemsize for x in arrays + list(operands))
    return pl.pallas_call(
        whole,
        in_specs=[SMEM] * len(scalars) + [HBM] * (len(arrays) + len(loose)) + [VMEM] * len(operands),
        out_specs=[HBM] * (len(sent) + len(plain)) + [VMEM] * len(outs),
        out_shape=[jax.ShapeDtypeStruct(shape, kind) for shape, kind in made],
        scratch_shapes=[pltpu.VMEM(*one) if isinstance(one, tuple) else one for one in scratch] + buffers + sems,
        compiler_params=pltpu.CompilerParams(vmem_limit_bytes=VMEM_BYTES),
        cost_estimate=pl.CostEstimate(flops=int(micros * 1.15e9), bytes_accessed=moved // 10, transcendentals=0),
    )(*scalars, *arrays, *loose, *operands)


def norm_pair(params, norm_index):
    if norm_index == 0:
        return jnp.stack([params[0, 0], params[1, 0]])
    row_pair = params[:, 2 * norm_index - 1 : 2 * norm_index + 1]
    return jnp.transpose(row_pair, (0, 2, 1)).reshape(2, -1)


def pack_norms(vectors):
    blocks = [vectors[0][None]]
    for vector in vectors[1:]:
        blocks.append(vector.reshape(-1, 2).T)
    return jnp.concatenate(blocks, axis=0)


def adam_step(weight, moment, square, gradient, step_rate, decay_rate):
    moment_next = beta_first * moment + (1.0 - beta_first) * gradient
    square_next = beta_second * square + (1.0 - beta_second) * gradient * gradient
    corrected = moment_next / (1.0 - beta_first**STEP)
    divisor = jnp.sqrt(square_next / (1.0 - beta_second**STEP)) + adam_epsilon
    weight_next = weight - step_rate * (corrected / divisor + decay_rate * weight)
    return (weight_next, moment_next, square_next)


def body(
    signal,
    clip_ids,
    output_grad,
    first_weight,
    first_mean,
    first_square,
    wide_weight,
    wide_mean,
    wide_square,
    norm_params,
    norm_mean,
    norm_square,
):
    chans = lax.axis_size("chan")
    groups_of_frames = lax.axis_size("frames")
    devices = chans * groups_of_frames
    chan = lax.axis_index("chan")
    me = {"chan": chan, "frames": lax.axis_index("frames")}
    group = signal.shape[0]
    own = group // chans
    total = own + 2 * HALO
    frames = group * groups_of_frames
    in_local = signal.shape[1] // B0
    ins = in_local * chans
    wide_local = output_grad.shape[1] // B1
    wide = wide_local * chans
    columns = first_weight.shape[1]
    per = LANES // columns
    count_zero = frames * B0
    count = frames * B1

    core = [("chan", 1)]
    near, far = halves("chan", chans)[:-1], halves("frames", groups_of_frames)
    gather_orders = (far + near + core, far[:-2] + far[-1:] + near + far[-2:-1] + core)
    order_grads = (far + near + core, far[:-2] + near + far[-2:] + core)
    first_order = (near + far[:-2] + far[-1:] + far[-2:-1] + core, near + far + core)
    code_first = jnp.stack([code_of(order, me) for order in first_order]).astype(jnp.int32)
    code_gather = jnp.stack([code_of(order, me) for order in gather_orders]).astype(jnp.int32)
    code_grads = jnp.stack([code_of(order, me) for order in order_grads]).astype(jnp.int32)
    last_step = len(core + near + far) - 1
    signal_rows = signal.reshape(group, -1, LANES)
    shard = first_weight.shape[0]
    packed = packed_rows(shard, per)
    first_send = jnp.pad(first_weight.astype(BF16), ((0, per * packed - shard), (0, 0)))
    first_send = jnp.transpose(first_send.reshape(per, packed, columns), (1, 0, 2)).reshape(packed, LANES)
    windows = windows_of(signal_rows)
    signal_main = lax.all_to_all(windows, "chan", 0, 0, tiled=True)
    edge = edges_of(jnp.concatenate([signal, output_grad], axis=1))

    local = signal.astype(F32)
    local_sums = jnp.stack([jnp.sum(local, axis=0), jnp.sum(local * local, axis=0)]).reshape(2, in_local, B0).sum(axis=2)
    shared = jnp.where(me["frames"] == 0, norm_params.reshape(-1, in_local), 0.0)
    small = jnp.concatenate([local_sums, shared], axis=0)
    places = jnp.arange(LANES) // in_local == chan
    small = jnp.where(places[None], jnp.tile(small, (1, LANES // in_local)), 0.0)
    big = lax.reduce_precision(small, 8, 7)
    first_send = jnp.concatenate([first_send, big.astype(BF16), (small - big).astype(BF16)], axis=0)[None]

    first_steps, block = [], first_send
    for k in range(last_step):
        if k == 1:
            block = after(block, windows)
        block = jnp.concatenate([block, exchange(block, first_order, k)], axis=0)
        first_steps.append(block)
        if k == 1:
            edges = by_distance(after(edge, block))
    forward = [(i, i + 1) for i in range(groups_of_frames - 1)]
    numbers = after(clip_ids, first_steps[0]) + 1
    low = lax.ppermute(numbers[group - HALO - 1 :], "frames", forward)
    high = lax.ppermute(numbers[: HALO + 1], "frames", [(b, a) for a, b in forward])
    ids = lax.dynamic_slice_in_dim(jnp.concatenate([low, numbers, high]), chan * own, total + 2, 0)
    masks = ((ids[:-2] == ids[1:-1]).astype(F32), (ids[2:] == ids[1:-1]).astype(F32))
    edges = jnp.stack(edges)
    chan_scalar = jnp.reshape(chan, (1,)).astype(jnp.int32)
    (x_zero,) = run(
        signal_kernel,
        (chan_scalar,),
        [(signal_main, chans)],
        (edges,),
        [((total, 2, B1, ins), BF16, 1)],
        [],
        [],
        6,
    )
    first_halves = (block, exchange(after(block, signal_main, edges, *masks), first_order, last_step))
    first_steps.append(first_halves[1])

    layers = wide_weight.shape[0]
    rows = wide_weight.shape[1] // 9
    slab_groups = -(-9 // per)
    wide_send = jnp.transpose(wide_weight.astype(BF16).reshape(layers, rows, 9, columns), (0, 2, 1, 3))
    wide_send = jnp.pad(wide_send, ((0, 0), (0, per * slab_groups - 9), (0, 0), (0, 0)))
    wide_send = jnp.transpose(wide_send.reshape(layers, per, slab_groups, rows, columns), (0, 2, 3, 1, 4))
    wide_send = wide_send.reshape(layers, slab_groups, rows, LANES)


    cube = (total, B1, wide)
    cols = (total, B1, 3 * wide)
    lane_rows = signal_rows.shape[1]
    copies = ((devices, 1, 2 * wide), F32)
    acc = ((2, 8, wide), F32)

    pieces = pieces_of(total)

    def steps(low, target):
        return steps_of(low, total - low, target)

    vec = ((4, wide), F32)
    both = ((2, wide), F32)
    lanes = jnp.stack([jnp.repeat(mask[HALO : HALO + own], B1) for mask in masks]).astype(BF16)

    slab_blocks = ((devices, slab_groups, rows, LANES), BF16)
    slabs = ((9, wide, wide), BF16, 1)

    def conv_taps(taps):
        return taps.reshape(3, 3 * wide, wide)

    taps_one, short_taps, vec_zero, pairs = run(
        functools.partial(unpack_first, first_order, chans, shard, count_zero),
        (code_first,),
        [],
        (),
        [],
        [((3, 3 * ins, wide), BF16), ((ins, wide), BF16), ((4, ins), F32), ((3, 2, wide), F32)],
        [((wide // LANES, 10 * ins, LANES), F32), ((devices,) + first_send.shape[1:], BF16), DMA((2,))],
        4,
        loose=first_halves,
    )
    hidden_one, shortcut, sums = run(
        functools.partial(first_kernel, own),
        masks,
        [(x_zero, pieces), (taps_one, 1), (short_taps, 1)],
        (vec_zero,),
        [(cube, BF16, steps(1, 12)), (cube, BF16, steps(1, 12))],
        [copies],
        [((total, B1, 3 * ins), BF16), acc],
        8,
    )
    ties = [[first_steps[0]], [first_steps[2]], [first_steps[3], edges]] + [[first_halves[1]]] * last_step
    ties[last_step] = [hidden_one]
    wide_halves, _ = gather_halves(wide_send[None], gather_orders, ties[: last_step + 1])
    top_main = to_frames(after(output_grad, hidden_one).reshape(group, -1, LANES))
    came_one = to_all(sums)
    taps_two, taps_three = run(
        functools.partial(unpack_kernel, (0, 1), gather_orders, chans),
        (code_gather,),
        [],
        (),
        [slabs, slabs],
        [],
        [slab_blocks, slab_blocks, DMA((4,))],
        5,
        loose=wide_halves,
    )
    taps_two, taps_three = conv_taps(taps_two), conv_taps(taps_three)
    residual, sums, vec_one = run(
        functools.partial(forward_kernel, own, count, 2, 12, True),
        masks,
        [(hidden_one, pieces), (taps_two, 1), (shortcut, 1)],
        (came_one, pairs[0]),
        [(cube, BF16, steps(2, 12))],
        [copies, vec],
        [(cols, BF16), acc],
        9,
    )
    came_two = to_all(sums)
    (top,) = run(
        functools.partial(top_kernel, chans),
        (chan_scalar,),
        [(main, 1) for main in top_main],
        (after(edges, residual),),
        [(cube, BF16, 1)],
        [],
        [],
        10,
    )
    hidden_two, sums, vec_two = run(
        functools.partial(forward_kernel, own, count, 3, 12, False),
        masks,
        [(residual, pieces), (after(taps_three, top), 1)],
        (came_two, pairs[1]),
        [(cube, BF16, steps(3, 12))],
        [copies, vec],
        [(cols, BF16), acc],
        9,
    )
    came_three = to_all(sums)
    top_back, taps_four = run(
        functools.partial(top_back_kernel, 2, gather_orders, chans),
        (code_gather,) + masks,
        [(after(top, hidden_two), pieces)],
        (),
        [(cube, BF16, steps(3, 12)), slabs],
        [],
        [(cols, BF16), ((3, wide, 3 * wide), BF16), slab_blocks, DMA((2,))],
        8,
        loose=wide_halves,
    )
    taps_four = conv_taps(taps_four)
    dz_three, sums, vec_three = run(
        functools.partial(top_norm_kernel, own, count),
        (),
        [(top_back, pieces), (hidden_two, pieces)],
        (came_three, pairs[2]),
        [(cube, BF16, 1)],
        [copies, vec],
        [acc],
        4,
    )
    back_three = to_all(sums)

    def weight_grad(vector, values, d):
        blocks = (devices, slab_groups, rows, LANES)
        kept = ((devices // 2,) + blocks[1:], BF16)
        return run(
            functools.partial(weight_kernel, own, order_grads, chans),
            (code_grads,),
            [(values, pieces), (d, pieces)],
            (vector, lanes),
            [],
            [],
            [(cols, BF16), ((3, wide, own * B1), BF16), (blocks, BF16), DMA((2,))],
            9,
            [kept, kept],
        )

    four = weight_grad(vec_three, hidden_two, after(top, dz_three))
    (block_rows,) = run(
        functools.partial(last_kernel, own),
        masks,
        [(after(hidden_two, dz_three), pieces), (taps_four, 1), (residual, 1)],
        (vec_three,),
        [],
        [((chans, own, lane_rows, LANES), BF16)],
        [(cols, BF16)],
        12,
    )

    block_came = lax.all_to_all(block_rows, "chan", 0, 0, tiled=True)
    d_three, dz_two, sums, norm_three = run(
        functools.partial(middle_kernel, own, count, 4, 12, False),
        masks,
        [(dz_three, pieces), (hidden_two, pieces), (after(taps_three, block_rows, *four), 1), (residual, 1)],
        (back_three, vec_three, vec_two),
        [(cube, BF16, 1), (cube, BF16, steps(4, 12))],
        [copies, both],
        [(cols, BF16), acc, ((3, wide, 3 * wide), BF16)],
        9,
    )
    back_two = to_all(sums)
    three = weight_grad(vec_two, residual, d_three)
    low_top, dz_one, sums, norm_two = run(
        functools.partial(middle_kernel, own, count, 5, 12, True),
        masks,
        [(dz_two, pieces), (residual, pieces), (top, pieces), (after(taps_two, block_came, *three), 1), (hidden_one, 1)],
        (back_two, vec_two, vec_one),
        [(cube, BF16, 1), (cube, BF16, steps(5, 12))],
        [copies, both],
        [(cols, BF16), acc, ((3, wide, 3 * wide), BF16)],
        9,
    )
    back_one = to_all(sums)
    two = weight_grad(vec_one, hidden_one, low_top)
    d_one, dz_zero, sums, norm_one = run(
        functools.partial(bottom_kernel, own, count),
        masks,
        [(dz_one, pieces), (hidden_one, pieces), (after(taps_one, *two), 1), (short_taps, 1), (low_top, 1), (x_zero, 1)],
        (back_one, vec_one, vec_zero),
        [(cube, BF16, 1), ((own, 2, B1, ins), BF16, steps_of(0, own, 12))],
        [((devices, 1, 2 * ins), F32), both],
        [((total, B1, 2 * wide), BF16), ((2, 8, ins), F32), ((3, 2 * ins, 2 * wide), BF16)],
        8,
    )
    back_zero = to_all(sums)
    gave = lax.optimization_barrier((*two, *three, *four, dz_zero))
    wide_keep, wide_send = scatter_step(gave[:6:2], gave[1:6:2], order_grads, last_step)
    one_blocks = (devices, packed, LANES)
    one_kept = ((devices // 2,) + one_blocks[1:], BF16)
    one = run(
        functools.partial(first_weight_kernel, own, first_order, chans, shard),
        (code_first,),
        [(after(d_one, *wide_keep, *wide_send), pieces), (x_zero, 1), (low_top, 1)],
        (vec_zero, lanes),
        [],
        [],
        [
            ((total, B1, 2 * wide), BF16),
            ((3, 2 * ins, own * B1), BF16),
            ((wide // LANES, 10 * ins + per * packed, LANES), F32),
            (one_blocks, BF16),
            DMA((2,)),
        ],
        8,
        [one_kept, one_kept],
    )
    wide_keep, wide_send = scatter_step(wide_keep, wide_send, order_grads, last_step - 1)
    input_rows, norm_zero = run(
        functools.partial(input_kernel, own, count_zero),
        (),
        [(after(dz_zero, *one), 1), (x_zero, 1)],
        (back_zero, vec_zero),
        [],
        [((chans, own, lane_rows, LANES), BF16), ((2, ins), F32)],
        [],
        8,
    )

    input_came = lax.all_to_all(input_rows, "chan", 0, 0, tiled=True)
    block_out = block_came.reshape(group, -1).astype(F32)
    input_grad = input_came.reshape(group, -1).astype(F32)

    wide_keep, wide_send = scatter_step(wide_keep, wide_send, order_grads, last_step - 2)
    wide_keep, wide_send = ([after(x[0], input_rows)] for x in (wide_keep, wide_send))
    first_keep, first_send_half = ([after(x, input_rows)] for x in one)
    wide_sum = scatter_steps(wide_keep, wide_send, order_grads, last_step - 2).astype(F32)
    wide_sum = jnp.transpose(wide_sum.reshape(3, slab_groups, rows, per, columns), (0, 3, 1, 2, 4))
    wide_sum = wide_sum.reshape(3, per * slab_groups, rows, columns)[:, :9]
    grad_wide = lax.optimization_barrier(jnp.transpose(wide_sum, (0, 2, 1, 3)).reshape(wide_weight.shape))
    first_sum = scatter_steps(first_keep, first_send_half, first_order, last_step + 1).astype(F32)
    grad_first = jnp.transpose(first_sum.reshape(packed, per, columns), (1, 0, 2)).reshape(-1, columns)[:shard]
    grad_first = lax.optimization_barrier(grad_first)

    norm_sums = [norm_zero, norm_one, norm_two, norm_three]
    grad_norms = jnp.stack([pack_norms([s[1] for s in norm_sums]), pack_norms([s[0] for s in norm_sums])])
    grad_norms = lax.dynamic_slice_in_dim(grad_norms, chan * norm_params.shape[2], norm_params.shape[2], 2)
    own_squares = jnp.sum(grad_first * grad_first) + jnp.sum(grad_wide * grad_wide)
    own_squares = own_squares + jnp.where(lax.axis_index("frames") == 0, jnp.sum(grad_norms * grad_norms), 0.0)
    squares = jnp.sum(to_all(after(jnp.broadcast_to(own_squares, (devices, 1, LANES)), input_came))[:, 0, 0])
    grad_norm = jnp.sqrt(squares)
    factor = clip_limit / jnp.maximum(grad_norm, clip_limit)
    first_next, first_mean_next, first_square_next = adam_step(
        first_weight, first_mean, first_square, grad_first * factor, conv_rate, weight_decay
    )
    wide_next, wide_mean_next, wide_square_next = adam_step(
        wide_weight, wide_mean, wide_square, grad_wide * factor, conv_rate, weight_decay
    )
    norm_next, norm_mean_next, norm_square_next = adam_step(
        norm_params, norm_mean, norm_square, grad_norms * factor, norm_rate, 0.0
    )
    return (
        block_out,
        input_grad,
        grad_norm,
        first_next,
        first_mean_next,
        first_square_next,
        first_next.astype(BF16),
        wide_next,
        wide_mean_next,
        wide_square_next,
        wide_next.astype(BF16),
        norm_next,
        norm_mean_next,
        norm_square_next,
    )


def solution(mesh):
    rows = P("frames", "chan")
    deep = P(None, "frames", "chan")
    norms = P(None, None, "chan")
    in_specs = (rows, P("frames"), rows, rows, rows, rows, deep, deep, deep, norms, norms, norms)
    out_specs = (rows, rows, P(), rows, rows, rows, rows, deep, deep, deep, deep, norms, norms, norms)
    return jax.shard_map(body, mesh=mesh, in_specs=in_specs, out_specs=out_specs, check_vma=False)
```

```python
import functools
import math

import jax
import jax.numpy as jnp
from jax import lax
from jax.experimental import pallas as pl
from jax.experimental.pallas import tpu as pltpu
from jax.sharding import PartitionSpec as P

B0 = 64
STEP = 10
B1 = 32
HALO = 6
LANES = 128

norm_epsilon = 1e-05
clip_limit = 100.0
beta_first = 0.9
beta_second = 0.999
adam_epsilon = 1e-08
conv_rate = 0.05
norm_rate = 0.5
weight_decay = 0.01

BOTH = ("chan", "frames")
VMEM_BYTES = 58 * 1024 * 1024
F32 = jnp.float32
BF16 = jnp.bfloat16
NT = (((1,), (1,)), ((), ()))


def to_all(copies):
    return lax.all_to_all(copies, BOTH, 0, 0, tiled=True)


def edges_of(block):
    count = lax.axis_size("frames")
    forward = [(i, i + 1) for i in range(count - 1)]
    low = lax.ppermute(block[block.shape[0] - HALO :].reshape(HALO, -1, LANES), "frames", forward)
    high = lax.ppermute(block[:HALO].reshape(HALO, -1, LANES), "frames", [(b, a) for a, b in forward])
    return jnp.concatenate([low, high], axis=0)


def by_distance(edge):
    parts = lax.axis_size("chan")
    return [edge] + [lax.ppermute(edge, "chan", [(i, i ^ d) for i in range(parts)]) for d in range(1, parts)]


def windows_of(block):
    parts = lax.axis_size("chan")
    own = block.shape[0] // parts
    padded = jnp.pad(block, ((HALO, HALO), (0, 0), (0, 0)))
    return jnp.stack([padded[k * own : k * own + own + 2 * HALO] for k in range(parts)])


def to_frames(block):
    parts = lax.axis_size("chan")
    chan = lax.axis_index("chan")
    own = block.shape[0] // parts
    padded = jnp.pad(block, ((HALO, HALO), (0, 0), (0, 0)))
    windows = [lax.dynamic_slice_in_dim(padded, (chan ^ d) * own, own + 2 * HALO, 0) for d in range(parts)]
    return [windows[0]] + [lax.ppermute(windows[d], "chan", [(i, i ^ d) for i in range(parts)]) for d in range(1, parts)]


def halves(axis, size):
    steps = []
    while size > 1:
        size //= 2
        steps.append((axis, size))
    return steps


def code_of(order, place):
    return sum(((place[axis] // step) % 2) << k for k, (axis, step) in enumerate(order))


def position(orders, me_ref, chan, frame):
    core = chan % 2
    return code_of(orders[core], {"chan": chan, "frames": frame}) ^ me_ref[core]


def code_gap(orders, me_ref, frame):
    code = 0
    for k, (axis, step) in enumerate(orders[0]):
        if axis == "frames":
            code = code + ((frame // step) % 2) * (1 << k)
    return code ^ me_ref[0]


def exchange(value, orders, k):
    chans, count = lax.axis_size("chan"), lax.axis_size("frames")
    pairs = []
    for chan in range(chans):
        for frame in range(count):
            axis, step = orders[chan % 2][k]
            other = (chan ^ step, frame) if axis == "chan" else (chan, frame ^ step)
            pairs.append((chan * count + frame, other[0] * count + other[1]))
    return lax.ppermute(value, BOTH, pairs)


def gather_halves(block, orders, ties):
    blocks = []
    for k in range(len(orders[0]) - 1):
        block = jnp.concatenate([block, exchange(after(block, *ties[k]), orders, k)], axis=0)
        blocks.append(block)
    other = exchange(after(block, *ties[-1]), orders, len(orders[0]) - 1)
    return (block, other), blocks + [other]


def scatter_step(keeps, sends, orders, k):
    came = [exchange(send, orders, k) for send in sends]
    half = max(keeps[0].shape[0] // 2, 1)

    def added(part):
        return jnp.concatenate([(k[part].astype(F32) + c[part].astype(F32)).astype(BF16) for k, c in zip(keeps, came)], axis=1)

    return [added(slice(0, half))], [added(slice(half, None))]


def scatter_steps(keeps, sends, orders, count):
    for k in reversed(range(count)):
        keeps, sends = scatter_step(keeps, sends, orders, k)
    return keeps[0][0]


def after(value, *others):
    return lax.optimization_barrier((value, *others))[0]


def fit(count, target, unit=1):
    return max([k for k in range(unit, target + 1, unit) if count % k == 0], default=count)


def loop(low, high, target, body, unit=1):
    return spans(low, high - low, target, body, unit)


def spans(low, count, target, body, unit=1):
    chunk = fit(count, target, unit)

    def step(i, carry):
        body(low + i * chunk, chunk, i)
        return carry

    if chunk == count:
        body(low, chunk, 0)
    else:
        lax.fori_loop(0, count // chunk, step, 0)
    return chunk


def unrolled(low, high, target, body):
    count = -(-(high - low) // target)
    ends = [low + (high - low) * k // count for k in range(count + 1)]
    for number in range(count):
        body(ends[number], ends[number + 1] - ends[number], number)


def steps_of(low, high, target):
    return -(-(high - low) // target)


class Fetched:
    def __init__(self, source, ref, sems):
        self.source, self.ref, self.sems = source, ref, sems
        self.pieces = sems.shape[0]
        self.size = ref.shape[0] // self.pieces

    def copy(self, number):
        rows = pl.ds(number * self.size, self.size)
        return pltpu.make_async_copy(self.source.at[rows], self.ref.at[rows], self.sems.at[number])

    def start(self):
        for number in range(self.pieces):
            self.copy(number).start()

    def need(self, number):
        self.copy(number).wait()

    def need_all(self):
        for number in range(self.pieces):
            self.need(number)


class Sent:
    def __init__(self, target, ref, sems):
        self.target, self.ref, self.sems = target, ref, sems
        self.shape, self.dtype = ref.shape, ref.dtype
        self.sent = []

    def copy(self, base, chunk, number):
        rows = pl.ds(base, chunk)
        return pltpu.make_async_copy(self.ref.at[rows], self.target.at[rows], self.sems.at[number])

    def send(self, base, chunk, number):
        self.sent.append((base, chunk, number))
        self.copy(base, chunk, number).start()

    def finish(self):
        for one in self.sent:
            self.copy(*one).wait()


def sigmoid(z):
    return 0.5 * jnp.tanh(0.5 * z) + 0.5


def dot(a, b):
    return jnp.dot(a, b, preferred_element_type=F32)


def dot_nt(a, b):
    return lax.dot_general(a, b, NT, preferred_element_type=F32)


def chosen(rows, columns, source):
    r = lax.broadcasted_iota(jnp.int32, (rows, columns), 0)
    c = lax.broadcasted_iota(jnp.int32, (rows, columns), 1)
    return (c == source(r)).astype(BF16)


def same(r):
    return r


def transposed(rows):
    return dot_nt(chosen(rows.shape[1], rows.shape[1], same), rows).astype(BF16)


def shifts(flat):
    rows = flat.shape[0]
    bins = lax.broadcasted_iota(jnp.int32, flat.shape, 0) % B1
    below = jnp.where(bins == 0, 0.0, pltpu.roll(flat, 1, 0))
    above = jnp.where(bins == B1 - 1, 0.0, pltpu.roll(flat, rows - 1, 0))
    return below, above


def mask_frames(partial, mask_ref, base, chunk):
    cube = partial.reshape(chunk, B1, partial.shape[-1])
    return jnp.concatenate([cube[k] * mask_ref[base + k] for k in range(chunk)], axis=0)


def rows_of(ref, base, chunk):
    return ref[pl.ds(base, chunk)].reshape(chunk * B1, ref.shape[-1])


def put(ref, base, chunk, value):
    ref[pl.ds(base, chunk)] = value.reshape(chunk, B1, value.shape[-1]).astype(ref.dtype)


def taps_sum(cols_ref, taps_ref, masks, base, chunk, product=dot):
    total = None
    for tap in (1, 0, 2):
        partial = product(rows_of(cols_ref, base + tap - 1, chunk), taps_ref[tap])
        if tap == 0:
            partial = mask_frames(partial, masks[0], base, chunk)
        if tap == 2:
            partial = mask_frames(partial, masks[1], base, chunk)
        total = partial if total is None else total + partial
    return total


def own_rows(value, base, chunk, low, high):
    if isinstance(base, int) and low <= base and base + chunk <= high:
        return value
    frame = base + lax.broadcasted_iota(jnp.int32, value.shape, 0) // B1
    return jnp.where((frame >= low) & (frame < high), value, 0.0)


def add_sums(acc_ref, first, second):
    rows, channels = first.shape
    acc_ref[0] += jnp.sum(first.reshape(rows // 8, 8, channels), axis=0)
    acc_ref[1] += jnp.sum(second.reshape(rows // 8, 8, channels), axis=0)


def spread_sums(acc_ref, copies_ref):
    channels = acc_ref.shape[-1]
    for k in range(2):
        row = jnp.sum(acc_ref[k], axis=0, keepdims=True)
        copies_ref[:, :, k * channels : (k + 1) * channels] = jnp.broadcast_to(
            row[None], (copies_ref.shape[0], 1, channels)
        )


def came_sums(came_ref):
    total = jnp.sum(came_ref[...], axis=0)
    half = total.shape[-1] // 2
    return total[:, :half], total[:, half:]


def norm_of(came_ref, pairs_ref, number, count):
    first, second = came_sums(came_ref)
    mean = first / count
    spread = lax.rsqrt(second / count - mean * mean + norm_epsilon)
    return mean, spread, pairs_ref[number, 0:1], pairs_ref[number, 1:2]


def norm_rows(vec_ref):
    return vec_ref[0:1], vec_ref[1:2], vec_ref[2:3], vec_ref[3:4]


def normal(values, norm):
    return (values.astype(F32) - norm[0]) * norm[1]


def activated(values, norm):
    z = normal(values, norm) * norm[2] + norm[3]
    return z * sigmoid(z)


def back_act(q, values, norm):
    xhat = normal(values, norm)
    z = xhat * norm[2] + norm[3]
    gate = sigmoid(z)
    return q * gate * (1.0 + z * (1.0 - gate)), xhat


def back_norm(dz, values, norm, sums, count):
    xhat = normal(values, norm)
    return norm[2] * norm[1] * (dz.astype(F32) - sums[0] / count - xhat * (sums[1] / count))


def swap_halves(value):
    return pltpu.roll(value, LANES // 2, 1)


def halves_of(first, second):
    low = lax.broadcasted_iota(jnp.int32, first.shape, 1) < LANES // 2
    return jnp.where(low, first, swap_halves(second)), jnp.where(low, swap_halves(first), second)


def fetch_wide(layer, own_ref, other_ref, came_ref, sems):
    half = own_ref.shape[0]
    fetches = [
        pltpu.make_async_copy(ref.at[:, layer], came_ref.at[pl.ds(k * half, half)], sems.at[k])
        for k, ref in enumerate((own_ref, other_ref))
    ]
    for fetch in fetches:
        fetch.start()
    return fetches


def unpack_wide(orders, chans, me_ref, came_ref, taps_ref):
    devices, groups, rows, _ = came_ref.shape
    count = devices // chans
    per = LANES // (taps_ref.shape[2] // chans)
    wide = per * LANES
    piece = LANES // per
    spread = chosen(wide, wide, lambda r: (r % LANES) // piece * LANES + r // LANES * piece + r % piece)
    for frame in range(count):
        for side in range(chans // per):
            parts = []
            for k in range(per):
                at = position(orders, me_ref, side * per + k, frame)
                parts.append(came_ref[at].reshape(groups * rows, LANES))
            result = dot_nt(jnp.concatenate(parts, axis=1), spread).astype(BF16)
            for slab in range(per):
                for group in range(groups):
                    if slab * groups + group < 9:
                        taps_ref[slab * groups + group, frame * rows : (frame + 1) * rows, side * LANES : (side + 1) * LANES] = result[
                            group * rows : (group + 1) * rows, slab * LANES : (slab + 1) * LANES
                        ]


def unpack_kernel(layers, orders, chans, me_ref, own_ref, other_ref, *rest):
    outs, came_refs, sems = rest[: len(layers)], rest[len(layers) : -1], rest[-1]
    fetches = [
        fetch_wide(layer, own_ref, other_ref, came_refs[n], sems.at[pl.ds(2 * n, 2)]) for n, layer in enumerate(layers)
    ]
    for n, out in enumerate(outs):
        for fetch in fetches[n]:
            fetch.wait()
        unpack_wide(orders, chans, me_ref, came_refs[n], out.ref)
        out.send(0, 9, 0)
    for out in outs:
        out.finish()


def turn_taps(taps_ref, turned_ref):
    wide = taps_ref.shape[-1]
    for kt in range(3):
        for kf in range(3):
            turned_ref[2 - kt, :, kf * wide : (kf + 1) * wide] = taps_ref[kt, kf * wide : (kf + 1) * wide]


def pack_wide(order, chans, me_ref, slabs, out_ref):
    devices, groups, rows, _ = out_ref.shape
    count = devices // chans
    per = LANES // (slabs[0].shape[1] // chans)
    wide = per * LANES
    piece = LANES // per
    gather = chosen(wide, wide, lambda r: (r % LANES) // piece * LANES + r // LANES * piece + r % piece)
    for group in range(groups):
        for side in range(chans // per):
            parts = []
            for slab in range(per):
                tap = slab * groups + group
                tap = tap if tap < 9 else 8
                parts.append(slabs[tap][:, side * LANES : (side + 1) * LANES])
            result = dot_nt(jnp.concatenate(parts, axis=1), gather).astype(BF16)
            for k in range(per):
                for frame in range(count):
                    at = position(order, me_ref, side * per + k, frame)
                    out_ref[at, group] = result[frame * rows : (frame + 1) * rows, k * LANES : (k + 1) * LANES]


def unpack_first(
    orders, chans, shard, count_zero, window, me_ref, place_ref, own_ref, other_ref, numbers_ref,
    taps_ref, short_ref, vec_ref, pairs_ref, masks_ref, raw_ref, came_ref, sems,
):
    half = own_ref.shape[0]
    fetches = [
        pltpu.make_async_copy(ref, came_ref.at[pl.ds(k * half, half)], sems.at[k]) for k, ref in enumerate((own_ref, other_ref))
    ]
    for fetch in fetches:
        fetch.start()
    for fetch in fetches:
        fetch.wait()
    devices = came_ref.shape[0]
    count = devices // chans
    ins, outs = short_ref.shape
    per = LANES // (outs // chans)
    rows = packed_rows(shard, per)
    wide = per * LANES
    piece = LANES // per
    spread = chosen(wide, wide, lambda r: (r % LANES) // piece * LANES + r // LANES * piece + r % piece)
    for frame in range(count):
        for side in range(chans // per):
            parts = [came_ref[position(orders, me_ref, side * per + k, frame), 0:rows] for k in range(per)]
            result = dot_nt(jnp.concatenate(parts, axis=1), spread)
            for slab in range(per):
                start = slab * rows
                size = min(rows, shard - start)
                if size > 0:
                    raw_ref[side, frame * shard + start : frame * shard + start + size] = result[
                        :size, slab * LANES : (slab + 1) * LANES
                    ]
    for tap in range(9):
        kt, kf = tap // 3, tap % 3
        for side in range(outs // LANES):
            lanes = slice(side * LANES, (side + 1) * LANES)
            taps_ref[kt, kf * ins : (kf + 1) * ins, lanes] = raw_ref[side, pl.ds(tap, ins, stride=9)].astype(BF16)
    for side in range(outs // LANES):
        short_ref[:, side * LANES : (side + 1) * LANES] = raw_ref[side, 9 * ins : 10 * ins].astype(BF16)
    unpack_small(count_zero, came_ref, rows, vec_ref, pairs_ref)
    chan, frame = place_ref[0], place_ref[1]
    lane = lax.broadcasted_iota(jnp.int32, (1, LANES), 1)
    numbers = numbers_ref[...]
    edge = HALO + 1
    for outer, inside, step in ((0, lane < edge, -1), (chans - 1, (lane >= window - edge) & (lane < window), 1)):
        other = frame + step
        exists = (other >= 0) & (other < count)
        row = came_ref[code_gap(orders, me_ref, jnp.clip(other, 0, count - 1)), rows + 32 : rows + 48].astype(F32)[0:1]
        numbers = jnp.where(inside & (chan == outer), jnp.where(exists, row, 0.0), numbers)
    after_one = pltpu.roll(numbers, LANES - 1, 1)
    after_two = pltpu.roll(numbers, LANES - 2, 1)
    masks_ref[0:1] = (numbers == after_one).astype(F32)
    masks_ref[1:2] = (after_one == after_two).astype(F32)


def unpack_small(count_zero, came_ref, at, vec_ref, pairs_ref):
    parts = [jnp.sum(came_ref[:, at + 16 * k : at + 16 * (k + 1)].astype(F32), axis=0) for k in range(2)]
    sums = parts[0] + parts[1]
    average = sums[0:1] / count_zero
    vec_ref[0:1] = average
    vec_ref[1:2] = lax.rsqrt(sums[1:2] / count_zero - average * average + norm_epsilon)
    vec_ref[2:3] = sums[2:3]
    vec_ref[3:4] = sums[9:10]
    c = lax.broadcasted_iota(jnp.int32, (LANES, 2 * LANES), 1)
    r = lax.broadcasted_iota(jnp.int32, (LANES, 2 * LANES), 0)
    for side in range(2):
        place = (c == 2 * r + side).astype(BF16)
        spread_rows = [dot(part.astype(BF16), place) for part in (parts[0], parts[1])]
        both = spread_rows[0] + spread_rows[1]
        for k in range(3):
            for kind in range(2):
                row = both[2 + 7 * kind + 1 + 2 * k + side : 2 + 7 * kind + 2 + 2 * k + side]
                pairs_ref[k, kind : kind + 1] = row if side == 0 else pairs_ref[k, kind : kind + 1] + row


def turn_first(taps, short, turned_ref):
    ins, outs = short.ref.shape
    taps.need_all()
    short.need_all()
    for kt in range(3):
        turned_ref[2 - kt, 0:ins, 0:outs] = taps.ref[kt, ins : 2 * ins]
        turned_ref[2 - kt, 0:ins, outs:] = jnp.zeros((ins, outs), BF16)
        turned_ref[2 - kt, ins:, 0:outs] = taps.ref[kt, 2 * ins :]
        turned_ref[2 - kt, ins:, outs:] = taps.ref[kt, 0:ins]


def pack_first(order, chans, shard, me_ref, raw_ref, out_ref):
    devices, rows, _ = out_ref.shape
    count = devices // chans
    outs = raw_ref.shape[0] * LANES
    per = LANES // (outs // chans)
    wide = per * LANES
    piece = LANES // per
    gather = chosen(wide, wide, lambda r: (r % LANES) // piece * LANES + r // LANES * piece + r % piece)
    for frame in range(count):
        for side in range(chans // per):
            parts = [raw_ref[side, frame * shard + slab * rows : frame * shard + (slab + 1) * rows] for slab in range(per)]
            result = dot_nt(jnp.concatenate(parts, axis=1).astype(BF16), gather).astype(BF16)
            for k in range(per):
                at = position(order, me_ref, side * per + k, frame)
                out_ref[at] = result[:, k * LANES : (k + 1) * LANES]


def packed_rows(shard, per):
    return -(-shard // (per * 16)) * 16


def frames_in(chan_ref, mains, edges_ref, total, target, body):
    parts = len(mains)
    for main in mains:
        main.need_all()
    for low, at, part in ((0, 0, 0), (total - HALO, HALO, parts - 1)):

        @pl.when(chan_ref[0] == part)
        def _():
            for d, main in enumerate(mains):
                size = main.ref.shape[1]
                main.ref[low : low + HALO] = edges_ref[d, at : at + HALO, size : 2 * size]

    def piece(at, chunk, _):
        cubes = jnp.concatenate([main.ref[pl.ds(at, chunk)] for main in mains], axis=1)
        body(cubes.reshape(chunk * cubes.shape[1], LANES), at, chunk)

    loop(0, total, target, piece, 2)


def lane_row(chan_ref, q, size):
    return (q // size ^ chan_ref[0]) * size + q % size


def frames_out(rows, count, out_ref, at):
    parts, _, size, _ = out_ref.shape
    cube = rows.reshape(count, parts * size, LANES)
    for s in range(parts):
        out_ref[s, pl.ds(at, count)] = cube[:, s * size : (s + 1) * size].astype(out_ref.dtype)


def pieces_of(total):
    return fit(total, 4)


def channels_of(ref, base, chunk, parity):
    return ref[pl.ds(base, chunk), parity].reshape(chunk * B1, ref.shape[-1])


def signal_kernel(chan_ref, main, edges_ref, x_out):
    parts, _, size, _ = main.ref.shape
    x_ref = x_out.ref
    total = x_ref.shape[0]
    channels = x_ref.shape[-1]
    half = LANES // 2
    split = chosen(LANES, LANES, lambda r: r // half * half + r % B1 * 2 + r % half // B1)
    order = chosen(channels, channels, lambda r: r // half + r % half * 2)

    def turn(values, base, chunk):
        turned = dot_nt(split, values)
        for parity in range(2):
            pairs = []
            for pair in range(chunk // 2):
                lanes = turned[:, pair * LANES : (pair + 1) * LANES]
                even = lanes[parity * B1 : (parity + 1) * B1]
                odd = lanes[half + parity * B1 : half + (parity + 1) * B1]
                pairs.extend(halves_of(even, odd))
            x = dot(jnp.concatenate(pairs, axis=0).astype(BF16), order)
            x_ref[pl.ds(base, chunk), parity] = x.reshape(chunk, B1, channels).astype(BF16)

    main.need_all()
    for low, at, part in ((0, 0, 0), (total - HALO, HALO, parts - 1)):

        @pl.when(chan_ref[0] == part)
        def _():
            for s in range(parts):
                main.ref[s, low : low + HALO] = edges_ref[s ^ part, at : at + HALO, 0:size]

    def piece(at, chunk, _):
        cubes = jnp.concatenate([main.ref[s, pl.ds(at, chunk)] for s in range(parts)], axis=1)
        turn(cubes.reshape(chunk * parts * size, LANES), at, chunk)

    loop(0, total, 48, piece, 2)
    x_out.send(0, total, 0)
    x_out.finish()


def first_kernel(own, prev_ref, next_ref, x, taps, short, vec_ref, h_out, s_out, copies_ref, cols_ref, acc_ref):
    total = x.ref.shape[0]
    channels = x.ref.shape[-1]
    norm = norm_rows(vec_ref)

    def build(base, chunk):
        acts = [activated(channels_of(x.ref, base, chunk, parity), norm) for parity in range(2)]
        below, _ = shifts(acts[1])
        put(cols_ref, base, chunk, jnp.concatenate([below, acts[0], acts[1]], axis=1))

    by_pieces([x], total, 12, build)
    acc_ref[...] = jnp.zeros_like(acc_ref)
    taps.need_all()
    short.need_all()

    def conv(base, chunk, number):
        result = taps_sum(cols_ref, taps.ref, (prev_ref, next_ref), base, chunk)
        put(h_out.ref, base, chunk, result)
        h_out.send(base, chunk, number)
        mine = own_rows(result, base, chunk, HALO, HALO + own)
        add_sums(acc_ref, mine, mine * mine)
        even = rows_of(cols_ref, base, chunk)[:, channels : 2 * channels]
        put(s_out.ref, base, chunk, dot(even, short.ref[...]))
        s_out.send(base, chunk, number)

    unrolled(1, total - 1, 12, conv)
    spread_sums(acc_ref, copies_ref)
    h_out.finish()
    s_out.finish()


def by_pieces(fetched, total, target, body):
    pieces = fetched[0].pieces
    size = total // pieces

    def piece(number, carry):
        for operand in fetched:
            operand.need(number)
        spans(number * size, size, target, lambda base, chunk, _: body(base, chunk))
        return carry

    lax.fori_loop(0, pieces, piece, 0)


def activate_into(h, norm, cols_ref):
    def build(base, chunk):
        act = activated(rows_of(h.ref, base, chunk), norm)
        below, above = shifts(act)
        put(cols_ref, base, chunk, jnp.concatenate([below, act, above], axis=1))

    by_pieces([h], cols_ref.shape[0], 24, build)


def forward_kernel(own, count, number, lead, target, with_short, prev_ref, next_ref, h, taps, *rest):
    if with_short:
        s, came_ref, pairs_ref, out, copies_ref, vec_ref, cols_ref, acc_ref = rest
    else:
        came_ref, pairs_ref, out, copies_ref, vec_ref, cols_ref, acc_ref = rest
    total = cols_ref.shape[0]
    norm = norm_of(came_ref, pairs_ref, number, count)
    for k in range(4):
        vec_ref[k : k + 1] = norm[k]
    activate_into(h, norm, cols_ref)
    acc_ref[...] = jnp.zeros_like(acc_ref)
    taps.need_all()

    def conv(base, chunk, number):
        result = taps_sum(cols_ref, taps.ref, (prev_ref, next_ref), base, chunk)
        if with_short:
            if number == 0:
                s.need_all()
            result = result + rows_of(s.ref, base, chunk).astype(F32)
        put(out.ref, base, chunk, result)
        out.send(base, chunk, number)
        mine = own_rows(result, base, chunk, HALO, HALO + own)
        add_sums(acc_ref, mine, mine * mine)

    unrolled(lead, total - lead, target, conv)
    spread_sums(acc_ref, copies_ref)
    out.finish()


def shift_into(value, base, chunk, cols_ref):
    below, above = shifts(value)
    put(cols_ref, base, chunk, jnp.concatenate([above, value, below], axis=1))


def top_kernel(parts, chan_ref, *rest):
    mains, (edges_ref, e_out) = rest[:parts], rest[parts:]
    size = mains[0].ref.shape[1]
    total, _, wide = e_out.shape
    quarter = LANES // 4
    half = LANES // 2
    order = chosen(wide, wide, lambda r: r // half + lane_row(chan_ref, r % half, size) * 4)
    eye = chosen(LANES, LANES, same)

    def turn(values, base, chunk):
        turned = dot_nt(eye, values)
        frames = []
        for pair in range(chunk // 2):
            lanes = turned[:, pair * LANES : (pair + 1) * LANES]
            sides = [
                halves_of(
                    lanes[2 * side * quarter : (2 * side + 1) * quarter],
                    lanes[(2 * side + 1) * quarter : (2 * side + 2) * quarter],
                )
                for side in range(2)
            ]
            frames.extend([jnp.concatenate([sides[0][k], sides[1][k]], axis=1) for k in range(2)])
        put(e_out.ref, base, chunk, dot(jnp.concatenate(frames, axis=0).astype(BF16), order))

    frames_in(chan_ref, mains, edges_ref, total, 48, turn)
    e_out.send(0, total, 0)
    e_out.finish()


def top_back_kernel(layer, orders, chans, me_ref, prev_ref, next_ref, e, own_ref, other_ref, q_out, taps_out, cols_ref, turned_ref, came_ref, sems):
    total = q_out.shape[0]
    wide = e.ref.shape[-1]
    fetches = fetch_wide(layer, own_ref, other_ref, came_ref, sems)

    def build(base, chunk):
        shift_into(rows_of(e.ref, base, chunk).astype(F32), base, chunk, cols_ref)

    by_pieces([e], total, 24, build)
    for fetch in fetches:
        fetch.wait()
    unpack_wide(orders, chans, me_ref, came_ref, taps_out.ref)
    taps_out.send(0, 9, 0)
    for kt in range(3):
        for kf in range(3):
            turned_ref[2 - kt, :, kf * wide : (kf + 1) * wide] = taps_out.ref[3 * kt + kf]

    def back(base, chunk, number):
        put(q_out.ref, base, chunk, taps_sum(cols_ref, turned_ref, (prev_ref, next_ref), base, chunk, dot_nt))
        q_out.send(base, chunk, number)

    unrolled(3, total - 3, 12, back)
    taps_out.finish()
    q_out.finish()


def top_norm_kernel(own, count, q, h, came_ref, pairs_ref, dz_out, copies_ref, vec_ref, acc_ref):
    total = dz_out.shape[0]
    norm = norm_of(came_ref, pairs_ref, 2, count)
    for k in range(4):
        vec_ref[k : k + 1] = norm[k]
    acc_ref[...] = jnp.zeros_like(acc_ref)

    def back(base, chunk):
        dz, xhat = back_act(rows_of(q.ref, base, chunk).astype(F32), rows_of(h.ref, base, chunk), norm)
        put(dz_out.ref, base, chunk, dz)
        mine = own_rows(dz, base, chunk, HALO, HALO + own)
        add_sums(acc_ref, mine, own_rows(dz * xhat, base, chunk, HALO, HALO + own))

    by_pieces([q, h], total, 24, back)
    dz_out.send(0, total, 0)
    spread_sums(acc_ref, copies_ref)
    dz_out.finish()


def last_kernel(own, prev_ref, next_ref, h, taps, x, vec_ref, y_ref, cols_ref):
    wide = cols_ref.shape[-1] // 3
    half = LANES // 2
    order = chosen(wide, wide, lambda r: r // half + r % half * 4)
    eye = chosen(LANES, LANES, same)
    activate_into(h, norm_rows(vec_ref), cols_ref)
    taps.need_all()
    x.need_all()

    def conv(base, chunk, _):
        result = taps_sum(cols_ref, taps.ref, (prev_ref, next_ref), base, chunk) + rows_of(x.ref, base, chunk).astype(F32)
        mixed = dot_nt(result.astype(BF16), order)
        cube = mixed.reshape(chunk, B1, wide)
        for pair in range(chunk // 2):
            stack = []
            for side in range(wide // LANES):
                lanes = slice(side * LANES, (side + 1) * LANES)
                stack.extend(halves_of(cube[2 * pair][:, lanes], cube[2 * pair + 1][:, lanes]))
            turned = dot_nt(eye, jnp.concatenate(stack, axis=0).astype(BF16))
            frames_out(turned, 2, y_ref, base - HALO + 2 * pair)

    unrolled(HALO, HALO + own, 12, conv)


def middle_kernel(own, count, lead, target, with_top, prev_ref, next_ref, dz, h, *rest):
    if with_top:
        e, *rest = rest
    taps, low, back_ref, vec_ref, low_vec_ref, d_out, dz_out, copies_ref, sums_ref, cols_ref, acc_ref, turned_ref = rest
    total = cols_ref.shape[0]
    norm, low_norm = norm_rows(vec_ref), norm_rows(low_vec_ref)
    sums = came_sums(back_ref)
    sums_ref[0:1], sums_ref[1:2] = sums

    def build(base, size):
        d = back_norm(rows_of(dz.ref, base, size), rows_of(h.ref, base, size), norm, sums, count)
        if with_top:
            d = d + rows_of(e.ref, base, size).astype(F32)
        put(d_out.ref, base, size, d)
        shift_into(d, base, size, cols_ref)

    by_pieces([dz, h, e] if with_top else [dz, h], total, 24, build)
    d_out.send(0, total, 0)
    acc_ref[...] = jnp.zeros_like(acc_ref)
    taps.need_all()
    turn_taps(taps.ref, turned_ref)

    def back(base, chunk, number):
        q = taps_sum(cols_ref, turned_ref, (prev_ref, next_ref), base, chunk, dot_nt)
        if number == 0:
            low.need_all()
        new, xhat = back_act(q, rows_of(low.ref, base, chunk), low_norm)
        put(dz_out.ref, base, chunk, new)
        dz_out.send(base, chunk, number)
        mine = own_rows(new, base, chunk, HALO, HALO + own)
        add_sums(acc_ref, mine, mine * xhat)

    unrolled(lead, total - lead, target, back)
    spread_sums(acc_ref, copies_ref)
    d_out.finish()
    dz_out.finish()


def give(buffer_ref, keep_ref, send_ref, sems):
    half = keep_ref.shape[0]
    keep = pltpu.make_async_copy(buffer_ref.at[pl.ds(0, half)], keep_ref, sems.at[0])
    send = pltpu.make_async_copy(buffer_ref.at[pl.ds(half, half)], send_ref, sems.at[1])
    keep.start()
    send.start()
    keep.wait()
    send.wait()


def weight_kernel(
    own, order, chans, me_ref, h, d, vec_ref, lanes_ref, keep_ref, send_ref,
    cols_ref, turned_ref, buffer_ref, sems,
):
    norm = norm_rows(vec_ref)
    wide = h.ref.shape[-1]

    def build(base, chunk):
        shift_into(rows_of(d.ref, base, chunk).astype(F32), base, chunk, cols_ref)

    chunk = fit(own, 28, 4)
    staged = all(HALO + chunk * (i + 1) <= h.size * (i + 2) for i in range(own // chunk)) and own // chunk + 1 == h.pieces
    if not staged:
        h.need_all()

    def turn(base, chunk, number):
        if staged:
            if number == 0:
                h.need(0)
            h.need(number + 1)
        u = activated(rows_of(h.ref, HALO + base, chunk), norm)
        columns = pl.ds(base * B1, chunk * B1)
        turned = transposed(u.astype(BF16))
        turned_ref[0, :, columns] = turned * lanes_ref[1:2, columns]
        turned_ref[1, :, columns] = turned
        turned_ref[2, :, columns] = turned * lanes_ref[0:1, columns]

    for number in range(own // chunk):
        turn(number * chunk, chunk, number)
    by_pieces([d], cols_ref.shape[0], 24, build)
    slabs = []
    for tap in range(3):
        other = cols_ref[pl.ds(HALO + 1 - tap, own)].reshape(own * B1, cols_ref.shape[-1])
        grad = dot(turned_ref[tap], other).astype(BF16)
        slabs.extend([grad[:, k * wide : (k + 1) * wide] for k in range(3)])
    pack_wide(order, chans, me_ref, slabs, buffer_ref)
    give(buffer_ref, keep_ref, send_ref, sems)


def bottom_kernel(
    own, count, prev_ref, next_ref, dz, h, taps, short, e1, x, back_ref, high_vec_ref, vec_ref,
    d_out, dz_out, copies_ref, sums_ref, cols_ref, acc_ref, turned_ref,
):
    total = cols_ref.shape[0]
    norm, low_norm = norm_rows(high_vec_ref), norm_rows(vec_ref)
    sums = came_sums(back_ref)
    sums_ref[0:1], sums_ref[1:2] = sums
    channels = x.ref.shape[-1]

    def build(base, size):
        d = back_norm(rows_of(dz.ref, base, size), rows_of(h.ref, base, size), norm, sums, count)
        put(d_out.ref, base, size, d)
        _, above = shifts(d)
        put(cols_ref, base, size, jnp.concatenate([d, above], axis=1))

    by_pieces([dz, h], total, 24, build)
    d_out.send(0, total, 0)
    acc_ref[...] = jnp.zeros_like(acc_ref)
    turn_first(taps, short, turned_ref)
    e1.need_all()
    x.need_all()

    def back(base, chunk, number):
        q = taps_sum(cols_ref, turned_ref, (prev_ref, next_ref), base, chunk, dot_nt)
        r = dot_nt(rows_of(e1.ref, base, chunk), short.ref[...])
        parts = (q[:, :channels] + r, q[:, channels:])
        for parity in range(2):
            new, xhat = back_act(parts[parity], channels_of(x.ref, base, chunk, parity), low_norm)
            dz_out.ref[pl.ds(base - HALO, chunk), parity] = new.reshape(chunk, B1, channels).astype(BF16)
            add_sums(acc_ref, new, new * xhat)
        dz_out.send(base - HALO, chunk, number)

    unrolled(HALO, HALO + own, 12, back)
    spread_sums(acc_ref, copies_ref)
    d_out.finish()
    dz_out.finish()


def first_weight_kernel(
    own, order, chans, shard, me_ref, d, x, e1, vec_ref, lanes_ref, keep_ref, send_ref,
    cols_ref, turned_ref, raw_ref, buffer_ref, sems,
):
    norm = norm_rows(vec_ref)
    channels = x.ref.shape[-1]
    wide = d.ref.shape[-1]

    def build(base, size):
        value = rows_of(d.ref, base, size)
        _, above = shifts(value.astype(F32))
        put(cols_ref, base, size, jnp.concatenate([value, above.astype(BF16)], axis=1))

    by_pieces([d], cols_ref.shape[0], 24, build)
    x.need_all()
    e1.need_all()

    def turn(base, chunk):
        columns = pl.ds(base * B1, chunk * B1)
        for parity in range(2):
            place = slice(parity * channels, (parity + 1) * channels)
            turned = transposed(activated(channels_of(x.ref, HALO + base, chunk, parity), norm).astype(BF16))
            turned_ref[0, place, columns] = turned * lanes_ref[1:2, columns]
            turned_ref[1, place, columns] = turned
            turned_ref[2, place, columns] = turned * lanes_ref[0:1, columns]

    chunk = fit(own, 28, 4)
    for number in range(own // chunk):
        turn(number * chunk, chunk)
    for tap in range(3):
        other = cols_ref[pl.ds(HALO + 1 - tap, own)].reshape(own * B1, cols_ref.shape[-1])
        grad = dot(turned_ref[tap], other)
        slabs = (grad[channels:, wide:], grad[:channels, :wide], grad[channels:, :wide])
        for kf in range(3):
            for side in range(wide // LANES):
                raw_ref[side, pl.ds(3 * tap + kf, channels, stride=9)] = slabs[kf][:, side * LANES : (side + 1) * LANES]
    short = dot(turned_ref[1, 0:channels], e1.ref[pl.ds(HALO, own)].reshape(own * B1, wide))
    rest = raw_ref.shape[1] - 10 * channels
    for side in range(wide // LANES):
        raw_ref[side, 9 * channels : 10 * channels] = short[:, side * LANES : (side + 1) * LANES]
        raw_ref[side, 10 * channels :] = jnp.zeros((rest, LANES), F32)
    pack_first(order, chans, shard, me_ref, raw_ref, buffer_ref)
    give(buffer_ref, keep_ref, send_ref, sems)


def input_kernel(own, count, dz, x, back_ref, vec_ref, out_ref, sums_ref):
    norm = norm_rows(vec_ref)
    sums = came_sums(back_ref)
    sums_ref[0:1], sums_ref[1:2] = sums
    channels = x.ref.shape[-1]
    half = LANES // 2
    order = chosen(channels, channels, lambda r: r // half + r % half * 2)
    eye = chosen(LANES, LANES, same)
    split = chosen(LANES, LANES, lambda r: r // half * half + r % 2 * B1 + r % half // 2)
    dz.need_all()
    x.need_all()

    def build(base, chunk, _):
        mixed = []
        for parity in range(2):
            g = back_norm(
                channels_of(dz.ref, base, chunk, parity), channels_of(x.ref, HALO + base, chunk, parity), norm, sums, count
            )
            mixed.append(dot_nt(g.astype(BF16), order).reshape(chunk, B1, channels))
        for pair in range(chunk // 2):
            even, odd = [], []
            for parity in range(2):
                first, second = halves_of(mixed[parity][2 * pair], mixed[parity][2 * pair + 1])
                even.append(first)
                odd.append(second)
            stack = jnp.concatenate(even + odd, axis=0).astype(BF16)
            turned = dot_nt(eye, dot(split, stack).astype(BF16))
            frames_out(turned, 2, out_ref, base + 2 * pair)

    loop(0, own, 28, build, 2)


SMEM = pl.BlockSpec(memory_space=pltpu.SMEM)
VMEM = pl.BlockSpec(memory_space=pltpu.VMEM)
HBM = pl.BlockSpec(memory_space=pl.ANY)
DMA = pltpu.SemaphoreType.DMA


def run(kernel, scalars, fetched, operands, sent, outs, scratch, micros, plain=(), loose=()):
    arrays = [array for array, _ in fetched]
    buffers = [pltpu.VMEM(array.shape, array.dtype) for array in arrays] + [pltpu.VMEM(shape, kind) for shape, kind, _ in sent]
    sems = [DMA((pieces,)) for _, pieces in fetched] + [DMA((pieces,)) for _, _, pieces in sent]
    counts = (len(scalars), len(fetched), len(loose), len(operands), len(sent), len(plain), len(outs), len(scratch), len(buffers), len(sems))

    def whole(*refs):
        groups, at = [], 0
        for count in counts:
            groups.append(refs[at : at + count])
            at += count
        small, sources, left, inputs, targets, copied, results, own, held, marks = groups
        small = [view for ref in small for view in ((ref.at[0], ref.at[1]) if len(ref.shape) == 2 else (ref,))]
        incoming = [Fetched(*triple) for triple in zip(sources, held, marks)]
        leaving = [Sent(*triple) for triple in zip(targets, held[len(incoming) :], marks[len(incoming) :])]
        for operand in incoming:
            operand.start()
        kernel(*small, *incoming, *left, *inputs, *leaving, *copied, *results, *own)

    made = [(shape, kind) for shape, kind, _ in sent] + list(plain) + list(outs)
    moved = sum(x.size * x.dtype.itemsize for x in arrays + list(operands))
    return pl.pallas_call(
        whole,
        in_specs=[SMEM] * len(scalars) + [HBM] * (len(arrays) + len(loose)) + [VMEM] * len(operands),
        out_specs=[HBM] * (len(sent) + len(plain)) + [VMEM] * len(outs),
        out_shape=[jax.ShapeDtypeStruct(shape, kind) for shape, kind in made],
        scratch_shapes=[pltpu.VMEM(*one) if isinstance(one, tuple) else one for one in scratch] + buffers + sems,
        compiler_params=pltpu.CompilerParams(vmem_limit_bytes=VMEM_BYTES),
        cost_estimate=pl.CostEstimate(flops=int(micros * 1.15e9), bytes_accessed=moved // 10, transcendentals=0),
    )(*scalars, *arrays, *loose, *operands)


def norm_pair(params, norm_index):
    if norm_index == 0:
        return jnp.stack([params[0, 0], params[1, 0]])
    row_pair = params[:, 2 * norm_index - 1 : 2 * norm_index + 1]
    return jnp.transpose(row_pair, (0, 2, 1)).reshape(2, -1)


def pack_norms(vectors):
    blocks = [vectors[0][None]]
    for vector in vectors[1:]:
        blocks.append(vector.reshape(-1, 2).T)
    return jnp.concatenate(blocks, axis=0)


def adam_step(weight, moment, square, gradient, step_rate, decay_rate):
    moment_next = beta_first * moment + (1.0 - beta_first) * gradient
    square_next = beta_second * square + (1.0 - beta_second) * gradient * gradient
    corrected = moment_next / (1.0 - beta_first**STEP)
    divisor = jnp.sqrt(square_next / (1.0 - beta_second**STEP)) + adam_epsilon
    weight_next = weight - step_rate * (corrected / divisor + decay_rate * weight)
    return (weight_next, moment_next, square_next)


def body(
    signal,
    clip_ids,
    output_grad,
    first_weight,
    first_mean,
    first_square,
    wide_weight,
    wide_mean,
    wide_square,
    norm_params,
    norm_mean,
    norm_square,
):
    chans = lax.axis_size("chan")
    groups_of_frames = lax.axis_size("frames")
    devices = chans * groups_of_frames
    chan = lax.axis_index("chan")
    me = {"chan": chan, "frames": lax.axis_index("frames")}
    group = signal.shape[0]
    own = group // chans
    total = own + 2 * HALO
    frames = group * groups_of_frames
    in_local = signal.shape[1] // B0
    ins = in_local * chans
    wide_local = output_grad.shape[1] // B1
    wide = wide_local * chans
    columns = first_weight.shape[1]
    per = LANES // columns
    count_zero = frames * B0
    count = frames * B1

    core = [("chan", 1)]
    near, far = halves("chan", chans)[:-1], halves("frames", groups_of_frames)
    gather_orders = (far + near + core, far[:-2] + far[-1:] + near + far[-2:-1] + core)
    order_grads = (far + near + core, far[:-2] + near + far[-2:] + core)
    first_order = (near + far[:-2] + far[-1:] + far[-2:-1] + core, near + far + core)
    code_first = jnp.stack([code_of(order, me) for order in first_order]).astype(jnp.int32)
    code_gather = jnp.stack([code_of(order, me) for order in gather_orders]).astype(jnp.int32)
    code_grads = jnp.stack([code_of(order, me) for order in order_grads]).astype(jnp.int32)
    last_step = len(core + near + far) - 1
    signal_rows = signal.reshape(group, -1, LANES)
    shard = first_weight.shape[0]
    packed = packed_rows(shard, per)
    first_send = jnp.pad(first_weight.astype(BF16), ((0, per * packed - shard), (0, 0)))
    first_send = jnp.transpose(first_send.reshape(per, packed, columns), (1, 0, 2)).reshape(packed, LANES)
    windows = windows_of(signal_rows)
    signal_main = lax.all_to_all(windows, "chan", 0, 0, tiled=True)
    edge = edges_of(jnp.concatenate([signal, output_grad], axis=1))

    local = signal.astype(F32)
    local_sums = jnp.stack([jnp.sum(local, axis=0), jnp.sum(local * local, axis=0)]).reshape(2, in_local, B0).sum(axis=2)
    shared = jnp.where(me["frames"] == 0, norm_params.reshape(-1, in_local), 0.0)
    small = jnp.concatenate([local_sums, shared], axis=0)
    places = jnp.arange(LANES) // in_local == chan
    small = jnp.where(places[None], jnp.tile(small, (1, LANES // in_local)), 0.0)
    big = lax.reduce_precision(small, 8, 7)
    edge_count = HALO + 1
    window = total + 2
    numbers = (clip_ids + 1).astype(F32)
    numbers = jnp.pad(numbers, (edge_count, edge_count))
    own_numbers = jnp.pad(lax.dynamic_slice_in_dim(numbers, chan * own, window, 0), (0, LANES - window))[None]
    edge_numbers = jnp.concatenate(
        [numbers[group : group + edge_count], jnp.zeros((window - 2 * edge_count,), F32), numbers[edge_count : 2 * edge_count]]
    )
    edge_numbers = jnp.pad(edge_numbers[None], ((0, 15), (0, LANES - window)))
    first_send = jnp.concatenate(
        [first_send, big.astype(BF16), (small - big).astype(BF16), edge_numbers.astype(BF16)], axis=0
    )[None]

    first_steps, block = [], first_send
    for k in range(last_step):
        if k == 1:
            block = after(block, windows)
        block = jnp.concatenate([block, exchange(block, first_order, k)], axis=0)
        first_steps.append(block)
        if k == 1:
            edges = by_distance(after(edge, block))
    edges = jnp.stack(edges)
    place = jnp.stack([chan, me["frames"]]).astype(jnp.int32)
    (x_zero,) = run(
        signal_kernel,
        (place,),
        [(signal_main, chans)],
        (edges,),
        [((total, 2, B1, ins), BF16, 1)],
        [],
        [],
        6,
    )
    first_halves = (block, exchange(after(block, x_zero), first_order, last_step))
    first_steps.append(first_halves[1])

    layers = wide_weight.shape[0]
    rows = wide_weight.shape[1] // 9
    slab_groups = -(-9 // per)
    wide_send = jnp.transpose(wide_weight.astype(BF16).reshape(layers, rows, 9, columns), (0, 2, 1, 3))
    wide_send = jnp.pad(wide_send, ((0, 0), (0, per * slab_groups - 9), (0, 0), (0, 0)))
    wide_send = jnp.transpose(wide_send.reshape(layers, per, slab_groups, rows, columns), (0, 2, 3, 1, 4))
    wide_send = wide_send.reshape(layers, slab_groups, rows, LANES)


    cube = (total, B1, wide)
    cols = (total, B1, 3 * wide)
    lane_rows = signal_rows.shape[1]
    copies = ((devices, 1, 2 * wide), F32)
    acc = ((2, 8, wide), F32)

    pieces = pieces_of(total)

    def steps(low, target):
        return steps_of(low, total - low, target)

    vec = ((4, wide), F32)
    both = ((2, wide), F32)

    slab_blocks = ((devices, slab_groups, rows, LANES), BF16)
    slabs = ((9, wide, wide), BF16, 1)

    def conv_taps(taps):
        return taps.reshape(3, 3 * wide, wide)

    taps_one, short_taps, vec_zero, pairs, both_masks = run(
        functools.partial(unpack_first, first_order, chans, shard, count_zero, window),
        (code_first, place),
        [],
        (own_numbers,),
        [],
        [((3, 3 * ins, wide), BF16), ((ins, wide), BF16), ((4, ins), F32), ((3, 2, wide), F32), ((2, LANES), F32)],
        [((wide // LANES, 10 * ins, LANES), F32), ((devices,) + first_send.shape[1:], BF16), DMA((2,))],
        4,
        loose=first_halves,
    )
    masks = (both_masks,)
    hidden_one, shortcut, sums = run(
        functools.partial(first_kernel, own),
        masks,
        [(x_zero, pieces), (taps_one, 1), (short_taps, 1)],
        (vec_zero,),
        [(cube, BF16, steps(1, 12)), (cube, BF16, steps(1, 12))],
        [copies],
        [((total, B1, 3 * ins), BF16), acc],
        8,
    )
    ties = [[first_steps[1]], [first_steps[2]], [first_steps[3], edges]] + [[first_halves[1]]] * last_step
    ties[last_step] = [hidden_one]
    wide_halves, _ = gather_halves(wide_send[None], gather_orders, ties[: last_step + 1])
    top_main = to_frames(after(output_grad, hidden_one).reshape(group, -1, LANES))
    came_one = to_all(sums)
    taps_two, taps_three = run(
        functools.partial(unpack_kernel, (0, 1), gather_orders, chans),
        (code_gather,),
        [],
        (),
        [slabs, slabs],
        [],
        [slab_blocks, slab_blocks, DMA((4,))],
        5,
        loose=wide_halves,
    )
    taps_two, taps_three = conv_taps(taps_two), conv_taps(taps_three)
    residual, sums, vec_one = run(
        functools.partial(forward_kernel, own, count, 0, 2, 12, True),
        masks,
        [(hidden_one, pieces), (taps_two, 1), (shortcut, 1)],
        (came_one, pairs),
        [(cube, BF16, steps(2, 12))],
        [copies, vec],
        [(cols, BF16), acc],
        9,
    )
    came_two = to_all(sums)
    (top,) = run(
        functools.partial(top_kernel, chans),
        (place,),
        [(main, 1) for main in top_main],
        (after(edges, residual),),
        [(cube, BF16, 1)],
        [],
        [],
        10,
    )
    hidden_two, sums, vec_two = run(
        functools.partial(forward_kernel, own, count, 1, 3, 12, False),
        masks,
        [(residual, pieces), (after(taps_three, top), 1)],
        (came_two, pairs),
        [(cube, BF16, steps(3, 12))],
        [copies, vec],
        [(cols, BF16), acc],
        9,
    )
    came_three = to_all(sums)
    top_back, taps_four = run(
        functools.partial(top_back_kernel, 2, gather_orders, chans),
        (code_gather,) + masks,
        [(after(top, hidden_two), pieces)],
        (),
        [(cube, BF16, steps(3, 12)), slabs],
        [],
        [(cols, BF16), ((3, wide, 3 * wide), BF16), slab_blocks, DMA((2,))],
        8,
        loose=wide_halves,
    )
    taps_four = conv_taps(taps_four)
    late = after(both_masks, hidden_two)[:, HALO : HALO + own]
    lanes = jnp.repeat(late, B1, axis=1).astype(BF16)
    dz_three, sums, vec_three = run(
        functools.partial(top_norm_kernel, own, count),
        (),
        [(top_back, pieces), (hidden_two, pieces)],
        (came_three, pairs),
        [(cube, BF16, 1)],
        [copies, vec],
        [acc],
        4,
    )
    back_three = to_all(sums)

    def weight_grad(vector, values, d):
        blocks = (devices, slab_groups, rows, LANES)
        kept = ((devices // 2,) + blocks[1:], BF16)
        return run(
            functools.partial(weight_kernel, own, order_grads, chans),
            (code_grads,),
            [(values, pieces), (d, pieces)],
            (vector, lanes),
            [],
            [],
            [(cols, BF16), ((3, wide, own * B1), BF16), (blocks, BF16), DMA((2,))],
            9,
            [kept, kept],
        )

    four = weight_grad(vec_three, hidden_two, after(top, dz_three))
    (block_rows,) = run(
        functools.partial(last_kernel, own),
        masks,
        [(after(hidden_two, dz_three), pieces), (taps_four, 1), (residual, 1)],
        (vec_three,),
        [],
        [((chans, own, lane_rows, LANES), BF16)],
        [(cols, BF16)],
        12,
    )

    block_came = lax.all_to_all(block_rows, "chan", 0, 0, tiled=True)
    d_three, dz_two, sums, norm_three = run(
        functools.partial(middle_kernel, own, count, 4, 12, False),
        masks,
        [(dz_three, pieces), (hidden_two, pieces), (after(taps_three, block_rows, *four), 1), (residual, 1)],
        (back_three, vec_three, vec_two),
        [(cube, BF16, 1), (cube, BF16, steps(4, 12))],
        [copies, both],
        [(cols, BF16), acc, ((3, wide, 3 * wide), BF16)],
        9,
    )
    back_two = to_all(sums)
    three = weight_grad(vec_two, residual, d_three)
    low_top, dz_one, sums, norm_two = run(
        functools.partial(middle_kernel, own, count, 5, 12, True),
        masks,
        [(dz_two, pieces), (residual, pieces), (top, pieces), (after(taps_two, block_came, *three), 1), (hidden_one, 1)],
        (back_two, vec_two, vec_one),
        [(cube, BF16, 1), (cube, BF16, steps(5, 12))],
        [copies, both],
        [(cols, BF16), acc, ((3, wide, 3 * wide), BF16)],
        9,
    )
    back_one = to_all(sums)
    two = weight_grad(vec_one, hidden_one, low_top)
    d_one, dz_zero, sums, norm_one = run(
        functools.partial(bottom_kernel, own, count),
        masks,
        [(dz_one, pieces), (hidden_one, pieces), (after(taps_one, *two), 1), (short_taps, 1), (low_top, 1), (x_zero, 1)],
        (back_one, vec_one, vec_zero),
        [(cube, BF16, 1), ((own, 2, B1, ins), BF16, steps_of(0, own, 12))],
        [((devices, 1, 2 * ins), F32), both],
        [((total, B1, 2 * wide), BF16), ((2, 8, ins), F32), ((3, 2 * ins, 2 * wide), BF16)],
        8,
    )
    back_zero = to_all(sums)
    gave = lax.optimization_barrier((*two, *three, *four, dz_zero))
    wide_keep, wide_send = scatter_step(gave[:6:2], gave[1:6:2], order_grads, last_step)
    one_blocks = (devices, packed, LANES)
    one_kept = ((devices // 2,) + one_blocks[1:], BF16)
    one = run(
        functools.partial(first_weight_kernel, own, first_order, chans, shard),
        (code_first,),
        [(after(d_one, *wide_keep, *wide_send), pieces), (x_zero, 1), (low_top, 1)],
        (vec_zero, lanes),
        [],
        [],
        [
            ((total, B1, 2 * wide), BF16),
            ((3, 2 * ins, own * B1), BF16),
            ((wide // LANES, 10 * ins + per * packed, LANES), F32),
            (one_blocks, BF16),
            DMA((2,)),
        ],
        8,
        [one_kept, one_kept],
    )
    wide_keep, wide_send = scatter_step(wide_keep, wide_send, order_grads, last_step - 1)
    input_rows, norm_zero = run(
        functools.partial(input_kernel, own, count_zero),
        (),
        [(after(dz_zero, *one), 1), (x_zero, 1)],
        (back_zero, vec_zero),
        [],
        [((chans, own, lane_rows, LANES), BF16), ((2, ins), F32)],
        [],
        8,
    )

    input_came = lax.all_to_all(input_rows, "chan", 0, 0, tiled=True)
    block_out = block_came.reshape(group, -1).astype(F32)
    input_grad = input_came.reshape(group, -1).astype(F32)

    wide_keep, wide_send = scatter_step(wide_keep, wide_send, order_grads, last_step - 2)
    wide_keep, wide_send = ([after(x[0], input_rows)] for x in (wide_keep, wide_send))
    first_keep, first_send_half = ([after(x, input_rows)] for x in one)
    wide_sum = scatter_steps(wide_keep, wide_send, order_grads, last_step - 2).astype(F32)
    wide_sum = jnp.transpose(wide_sum.reshape(3, slab_groups, rows, per, columns), (0, 3, 1, 2, 4))
    wide_sum = wide_sum.reshape(3, per * slab_groups, rows, columns)[:, :9]
    grad_wide = lax.optimization_barrier(jnp.transpose(wide_sum, (0, 2, 1, 3)).reshape(wide_weight.shape))
    first_sum = scatter_steps(first_keep, first_send_half, first_order, last_step + 1).astype(F32)
    grad_first = jnp.transpose(first_sum.reshape(packed, per, columns), (1, 0, 2)).reshape(-1, columns)[:shard]
    grad_first = lax.optimization_barrier(grad_first)

    norm_sums = [norm_zero, norm_one, norm_two, norm_three]
    grad_norms = jnp.stack([pack_norms([s[1] for s in norm_sums]), pack_norms([s[0] for s in norm_sums])], axis=1)
    grad_norms = lax.dynamic_slice_in_dim(grad_norms, chan * norm_params.shape[2], norm_params.shape[2], 2)
    own_squares = jnp.sum(grad_first * grad_first) + jnp.sum(grad_wide * grad_wide)
    own_squares = own_squares + jnp.where(lax.axis_index("frames") == 0, jnp.sum(grad_norms * grad_norms), 0.0)
    squares = jnp.sum(to_all(after(jnp.broadcast_to(own_squares, (devices, 1, LANES)), input_came))[:, 0, 0])
    grad_norm = jnp.sqrt(squares)
    factor = clip_limit / jnp.maximum(grad_norm, clip_limit)
    first_next, first_mean_next, first_square_next = adam_step(
        first_weight, first_mean, first_square, grad_first * factor, conv_rate, weight_decay
    )
    wide_next, wide_mean_next, wide_square_next = adam_step(
        wide_weight, wide_mean, wide_square, grad_wide * factor, conv_rate, weight_decay
    )
    norm_arrays = [jnp.transpose(array, (1, 0, 2)) for array in (norm_params, norm_mean, norm_square)]
    norm_next, norm_mean_next, norm_square_next = (
        jnp.transpose(array, (1, 0, 2)) for array in adam_step(*norm_arrays, grad_norms * factor, norm_rate, 0.0)
    )
    return (
        block_out,
        input_grad,
        grad_norm,
        first_next,
        first_mean_next,
        first_square_next,
        first_next.astype(BF16),
        wide_next,
        wide_mean_next,
        wide_square_next,
        wide_next.astype(BF16),
        norm_next,
        norm_mean_next,
        norm_square_next,
    )


def solution(mesh):
    rows = P("frames", "chan")
    deep = P(None, "frames", "chan")
    norms = P(None, None, "chan")
    in_specs = (rows, P("frames"), rows, rows, rows, rows, deep, deep, deep, norms, norms, norms)
    out_specs = (rows, rows, P(), rows, rows, rows, rows, deep, deep, deep, deep, norms, norms, norms)
    return jax.shard_map(body, mesh=mesh, in_specs=in_specs, out_specs=out_specs, check_vma=False)
```

```python
import functools
import math

import jax
import jax.numpy as jnp
from jax import lax
from jax.experimental import pallas as pl
from jax.experimental.pallas import tpu as pltpu
from jax.sharding import PartitionSpec as P

B0 = 64
STEP = 10
B1 = 32
HALO = 6
LANES = 128

norm_epsilon = 1e-05
clip_limit = 100.0
beta_first = 0.9
beta_second = 0.999
adam_epsilon = 1e-08
conv_rate = 0.05
norm_rate = 0.5
weight_decay = 0.01

BOTH = ("chan", "frames")
VMEM_BYTES = 58 * 1024 * 1024
F32 = jnp.float32
BF16 = jnp.bfloat16
NT = (((1,), (1,)), ((), ()))


def to_all(copies):
    return lax.all_to_all(copies, BOTH, 0, 0, tiled=True)


def edges_of(block):
    count = lax.axis_size("frames")
    forward = [(i, i + 1) for i in range(count - 1)]
    low = lax.ppermute(block[block.shape[0] - HALO :].reshape(HALO, -1, LANES), "frames", forward)
    high = lax.ppermute(block[:HALO].reshape(HALO, -1, LANES), "frames", [(b, a) for a, b in forward])
    return jnp.concatenate([low, high], axis=0)


def by_distance(edge):
    parts = lax.axis_size("chan")
    return [edge] + [lax.ppermute(edge, "chan", [(i, i ^ d) for i in range(parts)]) for d in range(1, parts)]


def windows_of(block):
    parts = lax.axis_size("chan")
    own = block.shape[0] // parts
    padded = jnp.pad(block, ((HALO, HALO), (0, 0), (0, 0)))
    return jnp.stack([padded[k * own : k * own + own + 2 * HALO] for k in range(parts)])


def to_frames(block):
    parts = lax.axis_size("chan")
    chan = lax.axis_index("chan")
    own = block.shape[0] // parts
    padded = jnp.pad(block, ((HALO, HALO), (0, 0), (0, 0)))
    windows = [lax.dynamic_slice_in_dim(padded, (chan ^ d) * own, own + 2 * HALO, 0) for d in range(parts)]
    return [windows[0]] + [lax.ppermute(windows[d], "chan", [(i, i ^ d) for i in range(parts)]) for d in range(1, parts)]


def halves(axis, size):
    steps = []
    while size > 1:
        size //= 2
        steps.append((axis, size))
    return steps


def code_of(order, place):
    return sum(((place[axis] // step) % 2) << k for k, (axis, step) in enumerate(order))


def position(orders, me_ref, chan, frame):
    core = chan % 2
    return code_of(orders[core], {"chan": chan, "frames": frame}) ^ me_ref[core]


def code_gap(orders, me_ref, frame):
    code = 0
    for k, (axis, step) in enumerate(orders[0]):
        if axis == "frames":
            code = code + ((frame // step) % 2) * (1 << k)
    return code ^ me_ref[0]


def exchange(value, orders, k):
    chans, count = lax.axis_size("chan"), lax.axis_size("frames")
    pairs = []
    for chan in range(chans):
        for frame in range(count):
            axis, step = orders[chan % 2][k]
            other = (chan ^ step, frame) if axis == "chan" else (chan, frame ^ step)
            pairs.append((chan * count + frame, other[0] * count + other[1]))
    return lax.ppermute(value, BOTH, pairs)


def gather_halves(block, orders, ties):
    blocks = []
    for k in range(len(orders[0]) - 1):
        block = jnp.concatenate([block, exchange(after(block, *ties[k]), orders, k)], axis=0)
        blocks.append(block)
    other = exchange(after(block, *ties[-1]), orders, len(orders[0]) - 1)
    return (block, other), blocks + [other]


def scatter_step(keeps, sends, orders, k):
    came = [exchange(send, orders, k) for send in sends]
    half = max(keeps[0].shape[0] // 2, 1)

    def added(part):
        return jnp.concatenate([(k[part].astype(F32) + c[part].astype(F32)).astype(BF16) for k, c in zip(keeps, came)], axis=1)

    return [added(slice(0, half))], [added(slice(half, None))]


def scatter_steps(keeps, sends, orders, count):
    for k in reversed(range(count)):
        keeps, sends = scatter_step(keeps, sends, orders, k)
    return keeps[0][0]


def after(value, *others):
    return lax.optimization_barrier((value, *others))[0]


def fit(count, target, unit=1):
    return max([k for k in range(unit, target + 1, unit) if count % k == 0], default=count)


def loop(low, high, target, body, unit=1):
    return spans(low, high - low, target, body, unit)


def spans(low, count, target, body, unit=1):
    chunk = fit(count, target, unit)

    def step(i, carry):
        body(low + i * chunk, chunk, i)
        return carry

    if chunk == count:
        body(low, chunk, 0)
    else:
        lax.fori_loop(0, count // chunk, step, 0)
    return chunk


def unrolled(low, high, target, body, unit=1):
    count = -(-(high - low) // target)
    ends = [low + (high - low) // unit * k // count * unit for k in range(count + 1)]
    for number in range(count):
        body(ends[number], ends[number + 1] - ends[number], number)


def steps_of(low, high, target):
    return -(-(high - low) // target)


class Fetched:
    def __init__(self, source, ref, sems):
        self.source, self.ref, self.sems = source, ref, sems
        self.pieces = sems.shape[0]
        self.size = ref.shape[0] // self.pieces

    def copy(self, number):
        rows = pl.ds(number * self.size, self.size)
        return pltpu.make_async_copy(self.source.at[rows], self.ref.at[rows], self.sems.at[number])

    def start(self):
        for number in range(self.pieces):
            self.copy(number).start()

    def need(self, number):
        self.copy(number).wait()

    def need_all(self):
        for number in range(self.pieces):
            self.need(number)


class Sent:
    def __init__(self, target, ref, sems):
        self.target, self.ref, self.sems = target, ref, sems
        self.shape, self.dtype = ref.shape, ref.dtype
        self.sent = []

    def copy(self, base, chunk, number):
        rows = pl.ds(base, chunk)
        return pltpu.make_async_copy(self.ref.at[rows], self.target.at[rows], self.sems.at[number])

    def send(self, base, chunk, number):
        self.sent.append((base, chunk, number))
        self.copy(base, chunk, number).start()

    def finish(self):
        for one in self.sent:
            self.copy(*one).wait()


def sigmoid(z):
    return 0.5 * jnp.tanh(0.5 * z) + 0.5


def dot(a, b):
    return jnp.dot(a, b, preferred_element_type=F32)


def dot_nt(a, b):
    return lax.dot_general(a, b, NT, preferred_element_type=F32)


def chosen(rows, columns, source):
    r = lax.broadcasted_iota(jnp.int32, (rows, columns), 0)
    c = lax.broadcasted_iota(jnp.int32, (rows, columns), 1)
    return (c == source(r)).astype(BF16)


def same(r):
    return r


def transposed(rows):
    return dot_nt(chosen(rows.shape[1], rows.shape[1], same), rows).astype(BF16)


def shifts(flat):
    rows = flat.shape[0]
    bins = lax.broadcasted_iota(jnp.int32, flat.shape, 0) % B1
    below = jnp.where(bins == 0, 0.0, pltpu.roll(flat, 1, 0))
    above = jnp.where(bins == B1 - 1, 0.0, pltpu.roll(flat, rows - 1, 0))
    return below, above


def mask_frames(partial, mask_ref, base, chunk):
    cube = partial.reshape(chunk, B1, partial.shape[-1])
    return jnp.concatenate([cube[k] * mask_ref[base + k] for k in range(chunk)], axis=0)


def rows_of(ref, base, chunk):
    return ref[pl.ds(base, chunk)].reshape(chunk * B1, ref.shape[-1])


def put(ref, base, chunk, value):
    ref[pl.ds(base, chunk)] = value.reshape(chunk, B1, value.shape[-1]).astype(ref.dtype)


def taps_sum(cols_ref, taps_ref, masks, base, chunk, product=dot):
    total = None
    for tap in (1, 0, 2):
        partial = product(rows_of(cols_ref, base + tap - 1, chunk), taps_ref[tap])
        if tap == 0:
            partial = mask_frames(partial, masks[0], base, chunk)
        if tap == 2:
            partial = mask_frames(partial, masks[1], base, chunk)
        total = partial if total is None else total + partial
    return total


def own_rows(value, base, chunk, low, high):
    if isinstance(base, int) and low <= base and base + chunk <= high:
        return value
    frame = base + lax.broadcasted_iota(jnp.int32, value.shape, 0) // B1
    return jnp.where((frame >= low) & (frame < high), value, 0.0)


def add_sums(acc_ref, first, second):
    rows, channels = first.shape
    acc_ref[0] += jnp.sum(first.reshape(rows // 8, 8, channels), axis=0)
    acc_ref[1] += jnp.sum(second.reshape(rows // 8, 8, channels), axis=0)


def spread_sums(acc_ref, copies_ref):
    channels = acc_ref.shape[-1]
    for k in range(2):
        row = jnp.sum(acc_ref[k], axis=0, keepdims=True)
        copies_ref[:, :, k * channels : (k + 1) * channels] = jnp.broadcast_to(
            row[None], (copies_ref.shape[0], 1, channels)
        )


def came_sums(came_ref):
    total = jnp.sum(came_ref[...], axis=0)
    half = total.shape[-1] // 2
    return total[:, :half], total[:, half:]


def norm_of(came_ref, pairs_ref, number, count):
    first, second = came_sums(came_ref)
    mean = first / count
    spread = lax.rsqrt(second / count - mean * mean + norm_epsilon)
    return mean, spread, pairs_ref[number, 0:1], pairs_ref[number, 1:2]


def norm_rows(vec_ref):
    return vec_ref[0:1], vec_ref[1:2], vec_ref[2:3], vec_ref[3:4]


def normal(values, norm):
    return (values.astype(F32) - norm[0]) * norm[1]


def activated(values, norm):
    z = normal(values, norm) * norm[2] + norm[3]
    return z * sigmoid(z)


def back_act(q, values, norm):
    xhat = normal(values, norm)
    z = xhat * norm[2] + norm[3]
    gate = sigmoid(z)
    return q * gate * (1.0 + z * (1.0 - gate)), xhat


def back_norm(dz, values, norm, sums, count):
    xhat = normal(values, norm)
    return norm[2] * norm[1] * (dz.astype(F32) - sums[0] / count - xhat * (sums[1] / count))


def swap_halves(value):
    return pltpu.roll(value, LANES // 2, 1)


def halves_of(first, second):
    low = lax.broadcasted_iota(jnp.int32, first.shape, 1) < LANES // 2
    return jnp.where(low, first, swap_halves(second)), jnp.where(low, swap_halves(first), second)


def fetch_wide(layer, own_ref, other_ref, came_ref, sems):
    half = own_ref.shape[0]
    fetches = [
        pltpu.make_async_copy(ref.at[:, layer], came_ref.at[pl.ds(k * half, half)], sems.at[k])
        for k, ref in enumerate((own_ref, other_ref))
    ]
    for fetch in fetches:
        fetch.start()
    return fetches


def unpack_wide(orders, chans, me_ref, came_ref, taps_ref):
    devices, groups, rows, _ = came_ref.shape
    count = devices // chans
    per = LANES // (taps_ref.shape[2] // chans)
    wide = per * LANES
    piece = LANES // per
    spread = chosen(wide, wide, lambda r: (r % LANES) // piece * LANES + r // LANES * piece + r % piece)
    for frame in range(count):
        for side in range(chans // per):
            parts = []
            for k in range(per):
                at = position(orders, me_ref, side * per + k, frame)
                parts.append(came_ref[at].reshape(groups * rows, LANES))
            result = dot_nt(jnp.concatenate(parts, axis=1), spread).astype(BF16)
            for slab in range(per):
                for group in range(groups):
                    if slab * groups + group < 9:
                        taps_ref[slab * groups + group, frame * rows : (frame + 1) * rows, side * LANES : (side + 1) * LANES] = result[
                            group * rows : (group + 1) * rows, slab * LANES : (slab + 1) * LANES
                        ]


def unpack_kernel(layers, orders, chans, me_ref, own_ref, other_ref, *rest):
    outs, came_refs, sems = rest[: len(layers)], rest[len(layers) : -1], rest[-1]
    fetches = [
        fetch_wide(layer, own_ref, other_ref, came_refs[n], sems.at[pl.ds(2 * n, 2)]) for n, layer in enumerate(layers)
    ]
    for n, out in enumerate(outs):
        for fetch in fetches[n]:
            fetch.wait()
        unpack_wide(orders, chans, me_ref, came_refs[n], out.ref)
        out.send(0, 9, 0)
    for out in outs:
        out.finish()


def turn_taps(taps_ref, turned_ref):
    wide = taps_ref.shape[-1]
    for kt in range(3):
        for kf in range(3):
            turned_ref[2 - kt, :, kf * wide : (kf + 1) * wide] = taps_ref[kt, kf * wide : (kf + 1) * wide]


def pack_wide(order, chans, me_ref, slabs, out_ref):
    devices, groups, rows, _ = out_ref.shape
    count = devices // chans
    per = LANES // (slabs[0].shape[1] // chans)
    wide = per * LANES
    piece = LANES // per
    gather = chosen(wide, wide, lambda r: (r % LANES) // piece * LANES + r // LANES * piece + r % piece)
    for group in range(groups):
        for side in range(chans // per):
            parts = []
            for slab in range(per):
                tap = slab * groups + group
                tap = tap if tap < 9 else 8
                parts.append(slabs[tap][:, side * LANES : (side + 1) * LANES])
            result = dot_nt(jnp.concatenate(parts, axis=1), gather).astype(BF16)
            for k in range(per):
                for frame in range(count):
                    at = position(order, me_ref, side * per + k, frame)
                    out_ref[at, group] = result[frame * rows : (frame + 1) * rows, k * LANES : (k + 1) * LANES]


def unpack_first(
    orders, chans, shard, count_zero, window, me_ref, place_ref, own_ref, other_ref, numbers_ref,
    taps_ref, short_ref, vec_ref, pairs_ref, masks_ref, raw_ref, came_ref, sems,
):
    half = own_ref.shape[0]
    fetches = [
        pltpu.make_async_copy(ref, came_ref.at[pl.ds(k * half, half)], sems.at[k]) for k, ref in enumerate((own_ref, other_ref))
    ]
    for fetch in fetches:
        fetch.start()
    for fetch in fetches:
        fetch.wait()
    devices = came_ref.shape[0]
    count = devices // chans
    ins, outs = short_ref.shape
    per = LANES // (outs // chans)
    rows = packed_rows(shard, per)
    wide = per * LANES
    piece = LANES // per
    spread = chosen(wide, wide, lambda r: (r % LANES) // piece * LANES + r // LANES * piece + r % piece)
    for frame in range(count):
        for side in range(chans // per):
            parts = [came_ref[position(orders, me_ref, side * per + k, frame), 0:rows] for k in range(per)]
            result = dot_nt(jnp.concatenate(parts, axis=1), spread)
            for slab in range(per):
                start = slab * rows
                size = min(rows, shard - start)
                if size > 0:
                    raw_ref[side, frame * shard + start : frame * shard + start + size] = result[
                        :size, slab * LANES : (slab + 1) * LANES
                    ]
    for tap in range(9):
        kt, kf = tap // 3, tap % 3
        for side in range(outs // LANES):
            lanes = slice(side * LANES, (side + 1) * LANES)
            taps_ref[kt, kf * ins : (kf + 1) * ins, lanes] = raw_ref[side, pl.ds(tap, ins, stride=9)].astype(BF16)
    for side in range(outs // LANES):
        short_ref[:, side * LANES : (side + 1) * LANES] = raw_ref[side, 9 * ins : 10 * ins].astype(BF16)
    unpack_small(count_zero, came_ref, rows, vec_ref, pairs_ref)
    chan, frame = place_ref[0], place_ref[1]
    lane = lax.broadcasted_iota(jnp.int32, (1, LANES), 1)
    numbers = numbers_ref[...]
    edge = HALO + 1
    for outer, inside, step in ((0, lane < edge, -1), (chans - 1, (lane >= window - edge) & (lane < window), 1)):
        other = frame + step
        exists = (other >= 0) & (other < count)
        row = came_ref[code_gap(orders, me_ref, jnp.clip(other, 0, count - 1)), rows + 32 : rows + 48].astype(F32)[0:1]
        numbers = jnp.where(inside & (chan == outer), jnp.where(exists, row, 0.0), numbers)
    after_one = pltpu.roll(numbers, LANES - 1, 1)
    after_two = pltpu.roll(numbers, LANES - 2, 1)
    masks_ref[0:1] = (numbers == after_one).astype(F32)
    masks_ref[1:2] = (after_one == after_two).astype(F32)


def unpack_small(count_zero, came_ref, at, vec_ref, pairs_ref):
    parts = [jnp.sum(came_ref[:, at + 16 * k : at + 16 * (k + 1)].astype(F32), axis=0) for k in range(2)]
    sums = parts[0] + parts[1]
    average = sums[0:1] / count_zero
    vec_ref[0:1] = average
    vec_ref[1:2] = lax.rsqrt(sums[1:2] / count_zero - average * average + norm_epsilon)
    vec_ref[2:3] = sums[2:3]
    vec_ref[3:4] = sums[9:10]
    c = lax.broadcasted_iota(jnp.int32, (LANES, 2 * LANES), 1)
    r = lax.broadcasted_iota(jnp.int32, (LANES, 2 * LANES), 0)
    for side in range(2):
        place = (c == 2 * r + side).astype(BF16)
        spread_rows = [dot(part.astype(BF16), place) for part in (parts[0], parts[1])]
        both = spread_rows[0] + spread_rows[1]
        for k in range(3):
            for kind in range(2):
                row = both[2 + 7 * kind + 1 + 2 * k + side : 2 + 7 * kind + 2 + 2 * k + side]
                pairs_ref[k, kind : kind + 1] = row if side == 0 else pairs_ref[k, kind : kind + 1] + row


def turn_first(taps, short, turned_ref):
    ins, outs = short.ref.shape
    taps.need_all()
    short.need_all()
    for kt in range(3):
        turned_ref[2 - kt, 0:ins, 0:outs] = taps.ref[kt, ins : 2 * ins]
        turned_ref[2 - kt, 0:ins, outs:] = jnp.zeros((ins, outs), BF16)
        turned_ref[2 - kt, ins:, 0:outs] = taps.ref[kt, 2 * ins :]
        turned_ref[2 - kt, ins:, outs:] = taps.ref[kt, 0:ins]


def pack_first(order, chans, shard, me_ref, raw_ref, out_ref):
    devices, rows, _ = out_ref.shape
    count = devices // chans
    outs = raw_ref.shape[0] * LANES
    per = LANES // (outs // chans)
    wide = per * LANES
    piece = LANES // per
    gather = chosen(wide, wide, lambda r: (r % LANES) // piece * LANES + r // LANES * piece + r % piece)
    for frame in range(count):
        for side in range(chans // per):
            parts = [raw_ref[side, frame * shard + slab * rows : frame * shard + (slab + 1) * rows] for slab in range(per)]
            result = dot_nt(jnp.concatenate(parts, axis=1).astype(BF16), gather).astype(BF16)
            for k in range(per):
                at = position(order, me_ref, side * per + k, frame)
                out_ref[at] = result[:, k * LANES : (k + 1) * LANES]


def packed_rows(shard, per):
    return -(-shard // (per * 16)) * 16


def frames_in(chan_ref, mains, edges_ref, total, target, body):
    parts = len(mains)
    for main in mains:
        main.need_all()
    for low, at, part in ((0, 0, 0), (total - HALO, HALO, parts - 1)):

        @pl.when(chan_ref[0] == part)
        def _():
            for d, main in enumerate(mains):
                size = main.ref.shape[1]
                main.ref[low : low + HALO] = edges_ref[d, at : at + HALO, size : 2 * size]

    def piece(at, chunk, _):
        cubes = jnp.concatenate([main.ref[pl.ds(at, chunk)] for main in mains], axis=1)
        body(cubes.reshape(chunk * cubes.shape[1], LANES), at, chunk)

    loop(0, total, target, piece, 2)


def lane_row(chan_ref, q, size):
    return (q // size ^ chan_ref[0]) * size + q % size


def frames_out(rows, count, out_ref, at):
    parts, _, size, _ = out_ref.shape
    cube = rows.reshape(count, parts * size, LANES)
    for s in range(parts):
        out_ref[s, pl.ds(at, count)] = cube[:, s * size : (s + 1) * size].astype(out_ref.dtype)


def pieces_of(total):
    return fit(total, 4)


def channels_of(ref, base, chunk, parity):
    return ref[pl.ds(base, chunk), parity].reshape(chunk * B1, ref.shape[-1])


def signal_kernel(chan_ref, main, edges_ref, x_out):
    parts, _, size, _ = main.ref.shape
    x_ref = x_out.ref
    total = x_ref.shape[0]
    channels = x_ref.shape[-1]
    half = LANES // 2
    split = chosen(LANES, LANES, lambda r: r // half * half + r % B1 * 2 + r % half // B1)
    order = chosen(channels, channels, lambda r: r // half + r % half * 2)

    def turn(values, base, chunk):
        turned = dot_nt(split, values)
        for parity in range(2):
            pairs = []
            for pair in range(chunk // 2):
                lanes = turned[:, pair * LANES : (pair + 1) * LANES]
                even = lanes[parity * B1 : (parity + 1) * B1]
                odd = lanes[half + parity * B1 : half + (parity + 1) * B1]
                pairs.extend(halves_of(even, odd))
            x = dot(jnp.concatenate(pairs, axis=0).astype(BF16), order)
            x_ref[pl.ds(base, chunk), parity] = x.reshape(chunk, B1, channels).astype(BF16)

    main.need_all()
    for low, at, part in ((0, 0, 0), (total - HALO, HALO, parts - 1)):

        @pl.when(chan_ref[0] == part)
        def _():
            for s in range(parts):
                main.ref[s, low : low + HALO] = edges_ref[s ^ part, at : at + HALO, 0:size]

    def piece(at, chunk, _):
        cubes = jnp.concatenate([main.ref[s, pl.ds(at, chunk)] for s in range(parts)], axis=1)
        turn(cubes.reshape(chunk * parts * size, LANES), at, chunk)

    loop(0, total, 48, piece, 2)
    x_out.send(0, total, 0)
    x_out.finish()


def first_kernel(own, prev_ref, next_ref, x, taps, short, vec_ref, h_out, s_out, copies_ref, cols_ref, acc_ref):
    total = x.ref.shape[0]
    channels = x.ref.shape[-1]
    norm = norm_rows(vec_ref)

    def build(base, chunk):
        acts = [activated(channels_of(x.ref, base, chunk, parity), norm) for parity in range(2)]
        below, _ = shifts(acts[1])
        put(cols_ref, base, chunk, jnp.concatenate([below, acts[0], acts[1]], axis=1))

    by_pieces([x], total, 12, build)
    acc_ref[...] = jnp.zeros_like(acc_ref)
    taps.need_all()
    short.need_all()

    def conv(base, chunk, number):
        result = taps_sum(cols_ref, taps.ref, (prev_ref, next_ref), base, chunk)
        put(h_out.ref, base, chunk, result)
        h_out.send(base, chunk, number)
        mine = own_rows(result, base, chunk, HALO, HALO + own)
        add_sums(acc_ref, mine, mine * mine)
        even = rows_of(cols_ref, base, chunk)[:, channels : 2 * channels]
        put(s_out.ref, base, chunk, dot(even, short.ref[...]))
        s_out.send(base, chunk, number)

    unrolled(1, total - 1, 12, conv)
    spread_sums(acc_ref, copies_ref)
    h_out.finish()
    s_out.finish()


def by_pieces(fetched, total, target, body):
    pieces = fetched[0].pieces
    size = total // pieces

    def piece(number, carry):
        for operand in fetched:
            operand.need(number)
        spans(number * size, size, target, lambda base, chunk, _: body(base, chunk))
        return carry

    lax.fori_loop(0, pieces, piece, 0)


def activate_into(h, norm, cols_ref):
    def build(base, chunk):
        act = activated(rows_of(h.ref, base, chunk), norm)
        below, above = shifts(act)
        put(cols_ref, base, chunk, jnp.concatenate([below, act, above], axis=1))

    by_pieces([h], cols_ref.shape[0], 24, build)


def forward_kernel(own, count, number, lead, target, with_short, prev_ref, next_ref, h, taps, *rest):
    if with_short:
        s, came_ref, pairs_ref, out, copies_ref, vec_ref, cols_ref, acc_ref = rest
    else:
        came_ref, pairs_ref, out, copies_ref, vec_ref, cols_ref, acc_ref = rest
    total = cols_ref.shape[0]
    norm = norm_of(came_ref, pairs_ref, number, count)
    for k in range(4):
        vec_ref[k : k + 1] = norm[k]
    activate_into(h, norm, cols_ref)
    acc_ref[...] = jnp.zeros_like(acc_ref)
    taps.need_all()

    def conv(base, chunk, number):
        result = taps_sum(cols_ref, taps.ref, (prev_ref, next_ref), base, chunk)
        if with_short:
            if number == 0:
                s.need_all()
            result = result + rows_of(s.ref, base, chunk).astype(F32)
        put(out.ref, base, chunk, result)
        out.send(base, chunk, number)
        mine = own_rows(result, base, chunk, HALO, HALO + own)
        add_sums(acc_ref, mine, mine * mine)

    unrolled(lead, total - lead, target, conv)
    spread_sums(acc_ref, copies_ref)
    out.finish()


def shift_into(value, base, chunk, cols_ref):
    below, above = shifts(value)
    put(cols_ref, base, chunk, jnp.concatenate([above, value, below], axis=1))


def top_kernel(parts, chan_ref, *rest):
    mains, (edges_ref, e_out) = rest[:parts], rest[parts:]
    size = mains[0].ref.shape[1]
    total, _, wide = e_out.shape
    quarter = LANES // 4
    half = LANES // 2
    order = chosen(wide, wide, lambda r: r // half + lane_row(chan_ref, r % half, size) * 4)
    eye = chosen(LANES, LANES, same)

    def turn(values, base, chunk):
        turned = dot_nt(eye, values)
        frames = []
        for pair in range(chunk // 2):
            lanes = turned[:, pair * LANES : (pair + 1) * LANES]
            sides = [
                halves_of(
                    lanes[2 * side * quarter : (2 * side + 1) * quarter],
                    lanes[(2 * side + 1) * quarter : (2 * side + 2) * quarter],
                )
                for side in range(2)
            ]
            frames.extend([jnp.concatenate([sides[0][k], sides[1][k]], axis=1) for k in range(2)])
        put(e_out.ref, base, chunk, dot(jnp.concatenate(frames, axis=0).astype(BF16), order))

    frames_in(chan_ref, mains, edges_ref, total, 48, turn)
    e_out.send(0, total, 0)
    e_out.finish()


def top_back_kernel(layer, orders, chans, me_ref, prev_ref, next_ref, e, own_ref, other_ref, q_out, taps_out, cols_ref, turned_ref, came_ref, sems):
    total = q_out.shape[0]
    wide = e.ref.shape[-1]
    fetches = fetch_wide(layer, own_ref, other_ref, came_ref, sems)

    def build(base, chunk):
        shift_into(rows_of(e.ref, base, chunk).astype(F32), base, chunk, cols_ref)

    by_pieces([e], total, 24, build)
    for fetch in fetches:
        fetch.wait()
    unpack_wide(orders, chans, me_ref, came_ref, taps_out.ref)
    taps_out.send(0, 9, 0)
    for kt in range(3):
        for kf in range(3):
            turned_ref[2 - kt, :, kf * wide : (kf + 1) * wide] = taps_out.ref[3 * kt + kf]

    def back(base, chunk, number):
        put(q_out.ref, base, chunk, taps_sum(cols_ref, turned_ref, (prev_ref, next_ref), base, chunk, dot_nt))
        q_out.send(base, chunk, number)

    unrolled(3, total - 3, 12, back)
    taps_out.finish()
    q_out.finish()


def top_norm_kernel(own, count, q, h, came_ref, pairs_ref, dz_out, copies_ref, vec_ref, acc_ref):
    total = dz_out.shape[0]
    norm = norm_of(came_ref, pairs_ref, 2, count)
    for k in range(4):
        vec_ref[k : k + 1] = norm[k]
    acc_ref[...] = jnp.zeros_like(acc_ref)

    def back(base, chunk):
        dz, xhat = back_act(rows_of(q.ref, base, chunk).astype(F32), rows_of(h.ref, base, chunk), norm)
        put(dz_out.ref, base, chunk, dz)
        mine = own_rows(dz, base, chunk, HALO, HALO + own)
        add_sums(acc_ref, mine, own_rows(dz * xhat, base, chunk, HALO, HALO + own))

    size = total // q.pieces
    for piece in range(q.pieces):
        q.need(piece)
        h.need(piece)
        unrolled(piece * size, (piece + 1) * size, 12, lambda base, chunk, _: back(base, chunk))
    dz_out.send(0, total, 0)
    spread_sums(acc_ref, copies_ref)
    dz_out.finish()


def last_kernel(own, prev_ref, next_ref, h, taps, x, vec_ref, y_ref, cols_ref):
    wide = cols_ref.shape[-1] // 3
    half = LANES // 2
    order = chosen(wide, wide, lambda r: r // half + r % half * 4)
    eye = chosen(LANES, LANES, same)
    activate_into(h, norm_rows(vec_ref), cols_ref)
    taps.need_all()
    x.need_all()

    def conv(base, chunk, _):
        result = taps_sum(cols_ref, taps.ref, (prev_ref, next_ref), base, chunk) + rows_of(x.ref, base, chunk).astype(F32)
        mixed = dot_nt(result.astype(BF16), order)
        cube = mixed.reshape(chunk, B1, wide)
        for pair in range(chunk // 2):
            stack = []
            for side in range(wide // LANES):
                lanes = slice(side * LANES, (side + 1) * LANES)
                stack.extend(halves_of(cube[2 * pair][:, lanes], cube[2 * pair + 1][:, lanes]))
            turned = dot_nt(eye, jnp.concatenate(stack, axis=0).astype(BF16))
            frames_out(turned, 2, y_ref, base - HALO + 2 * pair)

    unrolled(HALO, HALO + own, 12, conv, 2)


def middle_kernel(own, count, lead, target, with_top, prev_ref, next_ref, dz, h, *rest):
    if with_top:
        e, *rest = rest
    taps, low, back_ref, vec_ref, low_vec_ref, d_out, dz_out, copies_ref, sums_ref, cols_ref, acc_ref, turned_ref = rest
    total = cols_ref.shape[0]
    norm, low_norm = norm_rows(vec_ref), norm_rows(low_vec_ref)
    sums = came_sums(back_ref)
    sums_ref[0:1], sums_ref[1:2] = sums

    def build(base, size):
        d = back_norm(rows_of(dz.ref, base, size), rows_of(h.ref, base, size), norm, sums, count)
        if with_top:
            d = d + rows_of(e.ref, base, size).astype(F32)
        put(d_out.ref, base, size, d)
        shift_into(d, base, size, cols_ref)

    by_pieces([dz, h, e] if with_top else [dz, h], total, 24, build)
    d_out.send(0, total, 0)
    acc_ref[...] = jnp.zeros_like(acc_ref)
    taps.need_all()
    turn_taps(taps.ref, turned_ref)

    def back(base, chunk, number):
        q = taps_sum(cols_ref, turned_ref, (prev_ref, next_ref), base, chunk, dot_nt)
        if number == 0:
            low.need_all()
        new, xhat = back_act(q, rows_of(low.ref, base, chunk), low_norm)
        put(dz_out.ref, base, chunk, new)
        dz_out.send(base, chunk, number)
        mine = own_rows(new, base, chunk, HALO, HALO + own)
        add_sums(acc_ref, mine, mine * xhat)

    unrolled(lead, total - lead, target, back)
    spread_sums(acc_ref, copies_ref)
    d_out.finish()
    dz_out.finish()


def give(buffer_ref, keep_ref, send_ref, sems):
    half = keep_ref.shape[0]
    keep = pltpu.make_async_copy(buffer_ref.at[pl.ds(0, half)], keep_ref, sems.at[0])
    send = pltpu.make_async_copy(buffer_ref.at[pl.ds(half, half)], send_ref, sems.at[1])
    keep.start()
    send.start()
    keep.wait()
    send.wait()


def weight_kernel(
    own, order, chans, me_ref, h, d, vec_ref, lanes_ref, keep_ref, send_ref,
    cols_ref, turned_ref, buffer_ref, sems,
):
    norm = norm_rows(vec_ref)
    wide = h.ref.shape[-1]

    def build(base, chunk):
        shift_into(rows_of(d.ref, base, chunk).astype(F32), base, chunk, cols_ref)

    chunk = fit(own, 28, 4)
    staged = all(HALO + chunk * (i + 1) <= h.size * (i + 2) for i in range(own // chunk)) and own // chunk + 1 == h.pieces
    if not staged:
        h.need_all()

    def turn(base, chunk, number):
        if staged:
            if number == 0:
                h.need(0)
            h.need(number + 1)
        u = activated(rows_of(h.ref, HALO + base, chunk), norm)
        columns = pl.ds(base * B1, chunk * B1)
        turned = transposed(u.astype(BF16))
        turned_ref[0, :, columns] = turned * lanes_ref[1:2, columns]
        turned_ref[1, :, columns] = turned
        turned_ref[2, :, columns] = turned * lanes_ref[0:1, columns]

    for number in range(own // chunk):
        turn(number * chunk, chunk, number)
    by_pieces([d], cols_ref.shape[0], 24, build)
    slabs = []
    for tap in range(3):
        other = cols_ref[pl.ds(HALO + 1 - tap, own)].reshape(own * B1, cols_ref.shape[-1])
        grad = dot(turned_ref[tap], other).astype(BF16)
        slabs.extend([grad[:, k * wide : (k + 1) * wide] for k in range(3)])
    pack_wide(order, chans, me_ref, slabs, buffer_ref)
    give(buffer_ref, keep_ref, send_ref, sems)


def bottom_kernel(
    own, count, prev_ref, next_ref, dz, h, taps, short, e1, x, back_ref, high_vec_ref, vec_ref,
    d_out, dz_out, copies_ref, sums_ref, cols_ref, acc_ref, turned_ref,
):
    total = cols_ref.shape[0]
    norm, low_norm = norm_rows(high_vec_ref), norm_rows(vec_ref)
    sums = came_sums(back_ref)
    sums_ref[0:1], sums_ref[1:2] = sums
    channels = x.ref.shape[-1]

    def build(base, size):
        d = back_norm(rows_of(dz.ref, base, size), rows_of(h.ref, base, size), norm, sums, count)
        put(d_out.ref, base, size, d)
        _, above = shifts(d)
        put(cols_ref, base, size, jnp.concatenate([d, above], axis=1))

    by_pieces([dz, h], total, 24, build)
    d_out.send(0, total, 0)
    acc_ref[...] = jnp.zeros_like(acc_ref)
    turn_first(taps, short, turned_ref)
    e1.need_all()
    x.need_all()

    def back(base, chunk, number):
        q = taps_sum(cols_ref, turned_ref, (prev_ref, next_ref), base, chunk, dot_nt)
        r = dot_nt(rows_of(e1.ref, base, chunk), short.ref[...])
        parts = (q[:, :channels] + r, q[:, channels:])
        for parity in range(2):
            new, xhat = back_act(parts[parity], channels_of(x.ref, base, chunk, parity), low_norm)
            dz_out.ref[pl.ds(base - HALO, chunk), parity] = new.reshape(chunk, B1, channels).astype(BF16)
            add_sums(acc_ref, new, new * xhat)
        dz_out.send(base - HALO, chunk, number)

    unrolled(HALO, HALO + own, 12, back)
    spread_sums(acc_ref, copies_ref)
    d_out.finish()
    dz_out.finish()


def first_weight_kernel(
    own, order, chans, shard, me_ref, d, x, e1, vec_ref, lanes_ref, keep_ref, send_ref,
    cols_ref, turned_ref, raw_ref, buffer_ref, sems,
):
    norm = norm_rows(vec_ref)
    channels = x.ref.shape[-1]
    wide = d.ref.shape[-1]

    def build(base, size):
        value = rows_of(d.ref, base, size)
        _, above = shifts(value.astype(F32))
        put(cols_ref, base, size, jnp.concatenate([value, above.astype(BF16)], axis=1))

    by_pieces([d], cols_ref.shape[0], 24, build)
    x.need_all()
    e1.need_all()

    def turn(base, chunk):
        columns = pl.ds(base * B1, chunk * B1)
        for parity in range(2):
            place = slice(parity * channels, (parity + 1) * channels)
            turned = transposed(activated(channels_of(x.ref, HALO + base, chunk, parity), norm).astype(BF16))
            turned_ref[0, place, columns] = turned * lanes_ref[1:2, columns]
            turned_ref[1, place, columns] = turned
            turned_ref[2, place, columns] = turned * lanes_ref[0:1, columns]

    chunk = fit(own, 28, 4)
    for number in range(own // chunk):
        turn(number * chunk, chunk)
    for tap in range(3):
        other = cols_ref[pl.ds(HALO + 1 - tap, own)].reshape(own * B1, cols_ref.shape[-1])
        grad = dot(turned_ref[tap], other)
        slabs = (grad[channels:, wide:], grad[:channels, :wide], grad[channels:, :wide])
        for kf in range(3):
            for side in range(wide // LANES):
                raw_ref[side, pl.ds(3 * tap + kf, channels, stride=9)] = slabs[kf][:, side * LANES : (side + 1) * LANES]
    short = dot(turned_ref[1, 0:channels], e1.ref[pl.ds(HALO, own)].reshape(own * B1, wide))
    rest = raw_ref.shape[1] - 10 * channels
    for side in range(wide // LANES):
        raw_ref[side, 9 * channels : 10 * channels] = short[:, side * LANES : (side + 1) * LANES]
        raw_ref[side, 10 * channels :] = jnp.zeros((rest, LANES), F32)
    pack_first(order, chans, shard, me_ref, raw_ref, buffer_ref)
    give(buffer_ref, keep_ref, send_ref, sems)


def input_kernel(own, count, dz, x, back_ref, vec_ref, out_ref, sums_ref):
    norm = norm_rows(vec_ref)
    sums = came_sums(back_ref)
    sums_ref[0:1], sums_ref[1:2] = sums
    channels = x.ref.shape[-1]
    half = LANES // 2
    order = chosen(channels, channels, lambda r: r // half + r % half * 2)
    eye = chosen(LANES, LANES, same)
    split = chosen(LANES, LANES, lambda r: r // half * half + r % 2 * B1 + r % half // 2)
    dz.need_all()
    x.need_all()

    def build(base, chunk, _):
        mixed = []
        for parity in range(2):
            g = back_norm(
                channels_of(dz.ref, base, chunk, parity), channels_of(x.ref, HALO + base, chunk, parity), norm, sums, count
            )
            mixed.append(dot_nt(g.astype(BF16), order).reshape(chunk, B1, channels))
        for pair in range(chunk // 2):
            even, odd = [], []
            for parity in range(2):
                first, second = halves_of(mixed[parity][2 * pair], mixed[parity][2 * pair + 1])
                even.append(first)
                odd.append(second)
            stack = jnp.concatenate(even + odd, axis=0).astype(BF16)
            turned = dot_nt(eye, dot(split, stack).astype(BF16))
            frames_out(turned, 2, out_ref, base + 2 * pair)

    loop(0, own, 28, build, 2)


SMEM = pl.BlockSpec(memory_space=pltpu.SMEM)
VMEM = pl.BlockSpec(memory_space=pltpu.VMEM)
HBM = pl.BlockSpec(memory_space=pl.ANY)
DMA = pltpu.SemaphoreType.DMA


def run(kernel, scalars, fetched, operands, sent, outs, scratch, micros, plain=(), loose=()):
    arrays = [array for array, _ in fetched]
    buffers = [pltpu.VMEM(array.shape, array.dtype) for array in arrays] + [pltpu.VMEM(shape, kind) for shape, kind, _ in sent]
    sems = [DMA((pieces,)) for _, pieces in fetched] + [DMA((pieces,)) for _, _, pieces in sent]
    counts = (len(scalars), len(fetched), len(loose), len(operands), len(sent), len(plain), len(outs), len(scratch), len(buffers), len(sems))

    def whole(*refs):
        groups, at = [], 0
        for count in counts:
            groups.append(refs[at : at + count])
            at += count
        small, sources, left, inputs, targets, copied, results, own, held, marks = groups
        small = [view for ref in small for view in ((ref.at[0], ref.at[1]) if len(ref.shape) == 2 else (ref,))]
        incoming = [Fetched(*triple) for triple in zip(sources, held, marks)]
        leaving = [Sent(*triple) for triple in zip(targets, held[len(incoming) :], marks[len(incoming) :])]
        for operand in incoming:
            operand.start()
        kernel(*small, *incoming, *left, *inputs, *leaving, *copied, *results, *own)

    made = [(shape, kind) for shape, kind, _ in sent] + list(plain) + list(outs)
    moved = sum(x.size * x.dtype.itemsize for x in arrays + list(operands))
    return pl.pallas_call(
        whole,
        in_specs=[SMEM] * len(scalars) + [HBM] * (len(arrays) + len(loose)) + [VMEM] * len(operands),
        out_specs=[HBM] * (len(sent) + len(plain)) + [VMEM] * len(outs),
        out_shape=[jax.ShapeDtypeStruct(shape, kind) for shape, kind in made],
        scratch_shapes=[pltpu.VMEM(*one) if isinstance(one, tuple) else one for one in scratch] + buffers + sems,
        compiler_params=pltpu.CompilerParams(vmem_limit_bytes=VMEM_BYTES),
        cost_estimate=pl.CostEstimate(flops=int(micros * 1.15e9), bytes_accessed=moved // 10, transcendentals=0),
    )(*scalars, *arrays, *loose, *operands)


def norm_pair(params, norm_index):
    if norm_index == 0:
        return jnp.stack([params[0, 0], params[1, 0]])
    row_pair = params[:, 2 * norm_index - 1 : 2 * norm_index + 1]
    return jnp.transpose(row_pair, (0, 2, 1)).reshape(2, -1)


def pack_norms(vectors):
    blocks = [vectors[0][None]]
    for vector in vectors[1:]:
        blocks.append(vector.reshape(-1, 2).T)
    return jnp.concatenate(blocks, axis=0)


def adam_step(weight, moment, square, gradient, step_rate, decay_rate):
    moment_next = beta_first * moment + (1.0 - beta_first) * gradient
    square_next = beta_second * square + (1.0 - beta_second) * gradient * gradient
    corrected = moment_next / (1.0 - beta_first**STEP)
    divisor = jnp.sqrt(square_next / (1.0 - beta_second**STEP)) + adam_epsilon
    weight_next = weight - step_rate * (corrected / divisor + decay_rate * weight)
    return (weight_next, moment_next, square_next)


def body(
    signal,
    clip_ids,
    output_grad,
    first_weight,
    first_mean,
    first_square,
    wide_weight,
    wide_mean,
    wide_square,
    norm_params,
    norm_mean,
    norm_square,
):
    chans = lax.axis_size("chan")
    groups_of_frames = lax.axis_size("frames")
    devices = chans * groups_of_frames
    chan = lax.axis_index("chan")
    me = {"chan": chan, "frames": lax.axis_index("frames")}
    group = signal.shape[0]
    own = group // chans
    total = own + 2 * HALO
    frames = group * groups_of_frames
    in_local = signal.shape[1] // B0
    ins = in_local * chans
    wide_local = output_grad.shape[1] // B1
    wide = wide_local * chans
    columns = first_weight.shape[1]
    per = LANES // columns
    count_zero = frames * B0
    count = frames * B1

    core = [("chan", 1)]
    near, far = halves("chan", chans)[:-1], halves("frames", groups_of_frames)
    gather_orders = (far + near + core, far[:-2] + far[-1:] + near + far[-2:-1] + core)
    order_grads = (far + near + core, far[:-2] + near + far[-2:] + core)
    first_order = (near + far[:-2] + far[-1:] + far[-2:-1] + core, near + far + core)
    code_first = jnp.stack([code_of(order, me) for order in first_order]).astype(jnp.int32)
    code_gather = jnp.stack([code_of(order, me) for order in gather_orders]).astype(jnp.int32)
    code_grads = jnp.stack([code_of(order, me) for order in order_grads]).astype(jnp.int32)
    last_step = len(core + near + far) - 1
    signal_rows = signal.reshape(group, -1, LANES)
    shard = first_weight.shape[0]
    packed = packed_rows(shard, per)
    first_send = jnp.pad(first_weight.astype(BF16), ((0, per * packed - shard), (0, 0)))
    first_send = jnp.transpose(first_send.reshape(per, packed, columns), (1, 0, 2)).reshape(packed, LANES)
    windows = windows_of(signal_rows)
    signal_main = lax.all_to_all(windows, "chan", 0, 0, tiled=True)
    edge = edges_of(jnp.concatenate([signal, output_grad], axis=1))

    local = signal.astype(F32)
    local_sums = jnp.stack([jnp.sum(local, axis=0), jnp.sum(local * local, axis=0)]).reshape(2, in_local, B0).sum(axis=2)
    shared = jnp.where(me["frames"] == 0, norm_params.reshape(-1, in_local), 0.0)
    small = jnp.concatenate([local_sums, shared], axis=0)
    places = jnp.arange(LANES) // in_local == chan
    small = jnp.where(places[None], jnp.tile(small, (1, LANES // in_local)), 0.0)
    big = lax.reduce_precision(small, 8, 7)
    edge_count = HALO + 1
    window = total + 2
    numbers = (clip_ids + 1).astype(F32)
    numbers = jnp.pad(numbers, (edge_count, edge_count))
    own_numbers = jnp.pad(lax.dynamic_slice_in_dim(numbers, chan * own, window, 0), (0, LANES - window))[None]
    edge_numbers = jnp.concatenate(
        [numbers[group : group + edge_count], jnp.zeros((window - 2 * edge_count,), F32), numbers[edge_count : 2 * edge_count]]
    )
    edge_numbers = jnp.pad(edge_numbers[None], ((0, 15), (0, LANES - window)))
    first_send = jnp.concatenate(
        [first_send, big.astype(BF16), (small - big).astype(BF16), edge_numbers.astype(BF16)], axis=0
    )[None]

    first_steps, block = [], first_send
    for k in range(last_step):
        if k == 1:
            block = after(block, windows)
        block = jnp.concatenate([block, exchange(block, first_order, k)], axis=0)
        first_steps.append(block)
        if k == 1:
            edges = by_distance(after(edge, block))
    edges = jnp.stack(edges)
    place = jnp.stack([chan, me["frames"]]).astype(jnp.int32)
    (x_zero,) = run(
        signal_kernel,
        (place,),
        [(signal_main, chans)],
        (edges,),
        [((total, 2, B1, ins), BF16, 1)],
        [],
        [],
        6,
    )
    first_halves = (block, exchange(after(block, x_zero), first_order, last_step))
    first_steps.append(first_halves[1])

    layers = wide_weight.shape[0]
    rows = wide_weight.shape[1] // 9
    slab_groups = -(-9 // per)
    wide_send = jnp.transpose(wide_weight.astype(BF16).reshape(layers, rows, 9, columns), (0, 2, 1, 3))
    wide_send = jnp.pad(wide_send, ((0, 0), (0, per * slab_groups - 9), (0, 0), (0, 0)))
    wide_send = jnp.transpose(wide_send.reshape(layers, per, slab_groups, rows, columns), (0, 2, 3, 1, 4))
    wide_send = wide_send.reshape(layers, slab_groups, rows, LANES)


    cube = (total, B1, wide)
    cols = (total, B1, 3 * wide)
    lane_rows = signal_rows.shape[1]
    copies = ((devices, 1, 2 * wide), F32)
    acc = ((2, 8, wide), F32)

    pieces = pieces_of(total)

    def steps(low, target):
        return steps_of(low, total - low, target)

    vec = ((4, wide), F32)
    both = ((2, wide), F32)

    slab_blocks = ((devices, slab_groups, rows, LANES), BF16)
    slabs = ((9, wide, wide), BF16, 1)

    def conv_taps(taps):
        return taps.reshape(3, 3 * wide, wide)

    taps_one, short_taps, vec_zero, pairs, both_masks = run(
        functools.partial(unpack_first, first_order, chans, shard, count_zero, window),
        (code_first, place),
        [],
        (own_numbers,),
        [],
        [((3, 3 * ins, wide), BF16), ((ins, wide), BF16), ((4, ins), F32), ((3, 2, wide), F32), ((2, LANES), F32)],
        [((wide // LANES, 10 * ins, LANES), F32), ((devices,) + first_send.shape[1:], BF16), DMA((2,))],
        4,
        loose=first_halves,
    )
    masks = (both_masks,)
    hidden_one, shortcut, sums = run(
        functools.partial(first_kernel, own),
        masks,
        [(x_zero, pieces), (taps_one, 1), (short_taps, 1)],
        (vec_zero,),
        [(cube, BF16, steps(1, 12)), (cube, BF16, steps(1, 12))],
        [copies],
        [((total, B1, 3 * ins), BF16), acc],
        8,
    )
    ties = [[first_steps[1]], [first_steps[2]], [first_steps[3], edges]] + [[first_halves[1]]] * last_step
    ties[last_step] = [hidden_one]
    wide_halves, _ = gather_halves(wide_send[None], gather_orders, ties[: last_step + 1])
    top_main = to_frames(after(output_grad, hidden_one).reshape(group, -1, LANES))
    came_one = to_all(sums)
    taps_two, taps_three = run(
        functools.partial(unpack_kernel, (0, 1), gather_orders, chans),
        (code_gather,),
        [],
        (),
        [slabs, slabs],
        [],
        [slab_blocks, slab_blocks, DMA((4,))],
        5,
        loose=wide_halves,
    )
    taps_two, taps_three = conv_taps(taps_two), conv_taps(taps_three)
    residual, sums, vec_one = run(
        functools.partial(forward_kernel, own, count, 0, 2, 12, True),
        masks,
        [(hidden_one, pieces), (taps_two, 1), (shortcut, 1)],
        (came_one, pairs),
        [(cube, BF16, steps(2, 12))],
        [copies, vec],
        [(cols, BF16), acc],
        9,
    )
    came_two = to_all(sums)
    (top,) = run(
        functools.partial(top_kernel, chans),
        (place,),
        [(main, 1) for main in top_main],
        (after(edges, residual),),
        [(cube, BF16, 1)],
        [],
        [],
        10,
    )
    hidden_two, sums, vec_two = run(
        functools.partial(forward_kernel, own, count, 1, 3, 12, False),
        masks,
        [(residual, pieces), (after(taps_three, top), 1)],
        (came_two, pairs),
        [(cube, BF16, steps(3, 12))],
        [copies, vec],
        [(cols, BF16), acc],
        9,
    )
    came_three = to_all(sums)
    top_back, taps_four = run(
        functools.partial(top_back_kernel, 2, gather_orders, chans),
        (code_gather,) + masks,
        [(after(top, hidden_two), pieces)],
        (),
        [(cube, BF16, steps(3, 12)), slabs],
        [],
        [(cols, BF16), ((3, wide, 3 * wide), BF16), slab_blocks, DMA((2,))],
        8,
        loose=wide_halves,
    )
    taps_four = conv_taps(taps_four)
    late = after(both_masks, hidden_two)[:, HALO : HALO + own]
    lanes = jnp.repeat(late, B1, axis=1).astype(BF16)
    dz_three, sums, vec_three = run(
        functools.partial(top_norm_kernel, own, count),
        (),
        [(top_back, pieces), (hidden_two, pieces)],
        (came_three, pairs),
        [(cube, BF16, 1)],
        [copies, vec],
        [acc],
        4,
    )
    back_three = to_all(sums)

    def weight_grad(vector, values, d):
        blocks = (devices, slab_groups, rows, LANES)
        kept = ((devices // 2,) + blocks[1:], BF16)
        return run(
            functools.partial(weight_kernel, own, order_grads, chans),
            (code_grads,),
            [(values, pieces), (d, pieces)],
            (vector, lanes),
            [],
            [],
            [(cols, BF16), ((3, wide, own * B1), BF16), (blocks, BF16), DMA((2,))],
            9,
            [kept, kept],
        )

    four = weight_grad(vec_three, hidden_two, after(top, dz_three))
    (block_rows,) = run(
        functools.partial(last_kernel, own),
        masks,
        [(after(hidden_two, dz_three), pieces), (taps_four, 1), (residual, 1)],
        (vec_three,),
        [],
        [((chans, own, lane_rows, LANES), BF16)],
        [(cols, BF16)],
        12,
    )

    block_came = lax.all_to_all(block_rows, "chan", 0, 0, tiled=True)
    d_three, dz_two, sums, norm_three = run(
        functools.partial(middle_kernel, own, count, 4, 12, False),
        masks,
        [(dz_three, pieces), (hidden_two, pieces), (after(taps_three, block_rows, *four), 1), (residual, 1)],
        (back_three, vec_three, vec_two),
        [(cube, BF16, 1), (cube, BF16, steps(4, 12))],
        [copies, both],
        [(cols, BF16), acc, ((3, wide, 3 * wide), BF16)],
        9,
    )
    back_two = to_all(sums)
    three = weight_grad(vec_two, residual, d_three)
    low_top, dz_one, sums, norm_two = run(
        functools.partial(middle_kernel, own, count, 5, 12, True),
        masks,
        [(dz_two, pieces), (residual, pieces), (top, pieces), (after(taps_two, block_came, *three), 1), (hidden_one, 1)],
        (back_two, vec_two, vec_one),
        [(cube, BF16, 1), (cube, BF16, steps(5, 12))],
        [copies, both],
        [(cols, BF16), acc, ((3, wide, 3 * wide), BF16)],
        9,
    )
    back_one = to_all(sums)
    two = weight_grad(vec_one, hidden_one, low_top)
    d_one, dz_zero, sums, norm_one = run(
        functools.partial(bottom_kernel, own, count),
        masks,
        [(dz_one, pieces), (hidden_one, pieces), (after(taps_one, *two), 1), (short_taps, 1), (low_top, 1), (x_zero, 1)],
        (back_one, vec_one, vec_zero),
        [(cube, BF16, 1), ((own, 2, B1, ins), BF16, steps_of(0, own, 12))],
        [((devices, 1, 2 * ins), F32), both],
        [((total, B1, 2 * wide), BF16), ((2, 8, ins), F32), ((3, 2 * ins, 2 * wide), BF16)],
        8,
    )
    back_zero = to_all(sums)
    gave = lax.optimization_barrier((*two, *three, *four, dz_zero))
    wide_keep, wide_send = scatter_step(gave[:6:2], gave[1:6:2], order_grads, last_step)
    one_blocks = (devices, packed, LANES)
    one_kept = ((devices // 2,) + one_blocks[1:], BF16)
    one = run(
        functools.partial(first_weight_kernel, own, first_order, chans, shard),
        (code_first,),
        [(after(d_one, *wide_keep, *wide_send), pieces), (x_zero, 1), (low_top, 1)],
        (vec_zero, lanes),
        [],
        [],
        [
            ((total, B1, 2 * wide), BF16),
            ((3, 2 * ins, own * B1), BF16),
            ((wide // LANES, 10 * ins + per * packed, LANES), F32),
            (one_blocks, BF16),
            DMA((2,)),
        ],
        8,
        [one_kept, one_kept],
    )
    wide_keep, wide_send = scatter_step(wide_keep, wide_send, order_grads, last_step - 1)
    input_rows, norm_zero = run(
        functools.partial(input_kernel, own, count_zero),
        (),
        [(after(dz_zero, *one), 1), (x_zero, 1)],
        (back_zero, vec_zero),
        [],
        [((chans, own, lane_rows, LANES), BF16), ((2, ins), F32)],
        [],
        8,
    )

    input_came = lax.all_to_all(input_rows, "chan", 0, 0, tiled=True)
    block_out = block_came.reshape(group, -1).astype(F32)
    input_grad = input_came.reshape(group, -1).astype(F32)

    wide_keep, wide_send = scatter_step(wide_keep, wide_send, order_grads, last_step - 2)
    wide_keep, wide_send = ([after(x[0], input_rows)] for x in (wide_keep, wide_send))
    first_keep, first_send_half = ([after(x, input_rows)] for x in one)
    wide_sum = scatter_steps(wide_keep, wide_send, order_grads, last_step - 2).astype(F32)
    wide_sum = jnp.transpose(wide_sum.reshape(3, slab_groups, rows, per, columns), (0, 3, 1, 2, 4))
    wide_sum = wide_sum.reshape(3, per * slab_groups, rows, columns)[:, :9]
    grad_wide = lax.optimization_barrier(jnp.transpose(wide_sum, (0, 2, 1, 3)).reshape(wide_weight.shape))
    first_sum = scatter_steps(first_keep, first_send_half, first_order, last_step + 1).astype(F32)
    grad_first = jnp.transpose(first_sum.reshape(packed, per, columns), (1, 0, 2)).reshape(-1, columns)[:shard]
    grad_first = lax.optimization_barrier(grad_first)

    norm_sums = [norm_zero, norm_one, norm_two, norm_three]
    grad_norms = jnp.stack([pack_norms([s[1] for s in norm_sums]), pack_norms([s[0] for s in norm_sums])], axis=1)
    grad_norms = lax.dynamic_slice_in_dim(grad_norms, chan * norm_params.shape[2], norm_params.shape[2], 2)
    own_squares = jnp.sum(grad_first * grad_first) + jnp.sum(grad_wide * grad_wide)
    own_squares = own_squares + jnp.where(lax.axis_index("frames") == 0, jnp.sum(grad_norms * grad_norms), 0.0)
    squares = jnp.sum(to_all(after(jnp.broadcast_to(own_squares, (devices, 1, LANES)), input_came))[:, 0, 0])
    grad_norm = jnp.sqrt(squares)
    factor = clip_limit / jnp.maximum(grad_norm, clip_limit)
    first_next, first_mean_next, first_square_next = adam_step(
        first_weight, first_mean, first_square, grad_first * factor, conv_rate, weight_decay
    )
    wide_next, wide_mean_next, wide_square_next = adam_step(
        wide_weight, wide_mean, wide_square, grad_wide * factor, conv_rate, weight_decay
    )
    norm_arrays = [jnp.transpose(array, (1, 0, 2)) for array in (norm_params, norm_mean, norm_square)]
    norm_next, norm_mean_next, norm_square_next = (
        jnp.transpose(array, (1, 0, 2)) for array in adam_step(*norm_arrays, grad_norms * factor, norm_rate, 0.0)
    )
    return (
        block_out,
        input_grad,
        grad_norm,
        first_next,
        first_mean_next,
        first_square_next,
        first_next.astype(BF16),
        wide_next,
        wide_mean_next,
        wide_square_next,
        wide_next.astype(BF16),
        norm_next,
        norm_mean_next,
        norm_square_next,
    )


def solution(mesh):
    rows = P("frames", "chan")
    deep = P(None, "frames", "chan")
    norms = P(None, None, "chan")
    in_specs = (rows, P("frames"), rows, rows, rows, rows, deep, deep, deep, norms, norms, norms)
    out_specs = (rows, rows, P(), rows, rows, rows, rows, deep, deep, deep, deep, norms, norms, norms)
    return jax.shard_map(body, mesh=mesh, in_specs=in_specs, out_specs=out_specs, check_vma=False)
```

```python
import functools
import math

import jax
import jax.numpy as jnp
from jax import lax
from jax.experimental import pallas as pl
from jax.experimental.pallas import tpu as pltpu
from jax.sharding import PartitionSpec as P

B0 = 64
STEP = 10
B1 = 32
HALO = 6
LANES = 128

norm_epsilon = 1e-05
clip_limit = 100.0
beta_first = 0.9
beta_second = 0.999
adam_epsilon = 1e-08
conv_rate = 0.05
norm_rate = 0.5
weight_decay = 0.01

BOTH = ("chan", "frames")
VMEM_BYTES = 58 * 1024 * 1024
F32 = jnp.float32
BF16 = jnp.bfloat16
NT = (((1,), (1,)), ((), ()))


def to_all(copies):
    return lax.all_to_all(copies, BOTH, 0, 0, tiled=True)


def edges_of(block):
    count = lax.axis_size("frames")
    forward = [(i, i + 1) for i in range(count - 1)]
    low = lax.ppermute(block[block.shape[0] - HALO :].reshape(HALO, -1, LANES), "frames", forward)
    high = lax.ppermute(block[:HALO].reshape(HALO, -1, LANES), "frames", [(b, a) for a, b in forward])
    return jnp.concatenate([low, high], axis=0)


def by_distance(edge):
    parts = lax.axis_size("chan")
    return [edge] + [lax.ppermute(edge, "chan", [(i, i ^ d) for i in range(parts)]) for d in range(1, parts)]


def windows_of(block):
    parts = lax.axis_size("chan")
    own = block.shape[0] // parts
    padded = jnp.pad(block, ((HALO, HALO), (0, 0), (0, 0)))
    return jnp.stack([padded[k * own : k * own + own + 2 * HALO] for k in range(parts)])


def to_frames(block):
    parts = lax.axis_size("chan")
    chan = lax.axis_index("chan")
    own = block.shape[0] // parts
    padded = jnp.pad(block, ((HALO, HALO), (0, 0), (0, 0)))
    windows = [lax.dynamic_slice_in_dim(padded, (chan ^ d) * own, own + 2 * HALO, 0) for d in range(parts)]
    return [windows[0]] + [lax.ppermute(windows[d], "chan", [(i, i ^ d) for i in range(parts)]) for d in range(1, parts)]


def halves(axis, size):
    steps = []
    while size > 1:
        size //= 2
        steps.append((axis, size))
    return steps


def code_of(order, place):
    return sum(((place[axis] // step) % 2) << k for k, (axis, step) in enumerate(order))


def position(orders, me_ref, chan, frame):
    core = chan % 2
    return code_of(orders[core], {"chan": chan, "frames": frame}) ^ me_ref[core]


def code_gap(orders, me_ref, frame):
    code = 0
    for k, (axis, step) in enumerate(orders[0]):
        if axis == "frames":
            code = code + ((frame // step) % 2) * (1 << k)
    return code ^ me_ref[0]


def exchange(value, orders, k):
    chans, count = lax.axis_size("chan"), lax.axis_size("frames")
    pairs = []
    for chan in range(chans):
        for frame in range(count):
            axis, step = orders[chan % 2][k]
            other = (chan ^ step, frame) if axis == "chan" else (chan, frame ^ step)
            pairs.append((chan * count + frame, other[0] * count + other[1]))
    return lax.ppermute(value, BOTH, pairs)


def gather_halves(block, orders, ties):
    blocks = []
    for k in range(len(orders[0]) - 1):
        block = jnp.concatenate([block, exchange(after(block, *ties[k]), orders, k)], axis=0)
        blocks.append(block)
    other = exchange(after(block, *ties[-1]), orders, len(orders[0]) - 1)
    return (block, other), blocks + [other]


def scatter_step(keeps, sends, orders, k):
    came = [exchange(send, orders, k) for send in sends]
    half = max(keeps[0].shape[0] // 2, 1)

    def added(part):
        return jnp.concatenate([(k[part].astype(F32) + c[part].astype(F32)).astype(BF16) for k, c in zip(keeps, came)], axis=1)

    return [added(slice(0, half))], [added(slice(half, None))]


def scatter_steps(keeps, sends, orders, count):
    for k in reversed(range(count)):
        keeps, sends = scatter_step(keeps, sends, orders, k)
    return keeps[0][0]


def after(value, *others):
    return lax.optimization_barrier((value, *others))[0]


def fit(count, target, unit=1):
    return max([k for k in range(unit, target + 1, unit) if count % k == 0], default=count)


def loop(low, high, target, body, unit=1):
    return spans(low, high - low, target, body, unit)


def spans(low, count, target, body, unit=1):
    chunk = fit(count, target, unit)

    def step(i, carry):
        body(low + i * chunk, chunk, i)
        return carry

    if chunk == count:
        body(low, chunk, 0)
    else:
        lax.fori_loop(0, count // chunk, step, 0)
    return chunk


def unrolled(low, high, target, body, unit=1):
    count = -(-(high - low) // target)
    ends = [low + (high - low) // unit * k // count * unit for k in range(count + 1)]
    for number in range(count):
        body(ends[number], ends[number + 1] - ends[number], number)


def steps_of(low, high, target):
    return -(-(high - low) // target)


class Fetched:
    def __init__(self, source, ref, sems):
        self.source, self.ref, self.sems = source, ref, sems
        self.pieces = sems.shape[0]
        self.size = ref.shape[0] // self.pieces

    def copy(self, number):
        rows = pl.ds(number * self.size, self.size)
        return pltpu.make_async_copy(self.source.at[rows], self.ref.at[rows], self.sems.at[number])

    def start(self):
        for number in range(self.pieces):
            self.copy(number).start()

    def need(self, number):
        self.copy(number).wait()

    def need_all(self):
        for number in range(self.pieces):
            self.need(number)


class Sent:
    def __init__(self, target, ref, sems):
        self.target, self.ref, self.sems = target, ref, sems
        self.shape, self.dtype = ref.shape, ref.dtype
        self.sent = []

    def copy(self, base, chunk, number):
        rows = pl.ds(base, chunk)
        return pltpu.make_async_copy(self.ref.at[rows], self.target.at[rows], self.sems.at[number])

    def send(self, base, chunk, number):
        self.sent.append((base, chunk, number))
        self.copy(base, chunk, number).start()

    def finish(self):
        for one in self.sent:
            self.copy(*one).wait()


def sigmoid(z):
    return 0.5 * jnp.tanh(0.5 * z) + 0.5


def dot(a, b):
    return jnp.dot(a, b, preferred_element_type=F32)


def dot_nt(a, b):
    return lax.dot_general(a, b, NT, preferred_element_type=F32)


def chosen(rows, columns, source):
    r = lax.broadcasted_iota(jnp.int32, (rows, columns), 0)
    c = lax.broadcasted_iota(jnp.int32, (rows, columns), 1)
    return (c == source(r)).astype(BF16)


def same(r):
    return r


def transposed(rows):
    return dot_nt(chosen(rows.shape[1], rows.shape[1], same), rows).astype(BF16)


def shifts(flat):
    rows = flat.shape[0]
    bins = lax.broadcasted_iota(jnp.int32, flat.shape, 0) % B1
    below = jnp.where(bins == 0, 0.0, pltpu.roll(flat, 1, 0))
    above = jnp.where(bins == B1 - 1, 0.0, pltpu.roll(flat, rows - 1, 0))
    return below, above


def mask_frames(partial, mask_ref, base, chunk):
    cube = partial.reshape(chunk, B1, partial.shape[-1])
    return jnp.concatenate([cube[k] * mask_ref[base + k] for k in range(chunk)], axis=0)


def rows_of(ref, base, chunk):
    return ref[pl.ds(base, chunk)].reshape(chunk * B1, ref.shape[-1])


def put(ref, base, chunk, value):
    ref[pl.ds(base, chunk)] = value.reshape(chunk, B1, value.shape[-1]).astype(ref.dtype)


def taps_sum(cols_ref, taps_ref, masks, base, chunk, product=dot):
    total = None
    for tap in (1, 0, 2):
        partial = product(rows_of(cols_ref, base + tap - 1, chunk), taps_ref[tap])
        if tap == 0:
            partial = mask_frames(partial, masks[0], base, chunk)
        if tap == 2:
            partial = mask_frames(partial, masks[1], base, chunk)
        total = partial if total is None else total + partial
    return total


def own_rows(value, base, chunk, low, high):
    if isinstance(base, int) and low <= base and base + chunk <= high:
        return value
    frame = base + lax.broadcasted_iota(jnp.int32, value.shape, 0) // B1
    return jnp.where((frame >= low) & (frame < high), value, 0.0)


def add_sums(acc_ref, first, second):
    rows, channels = first.shape
    acc_ref[0] += jnp.sum(first.reshape(rows // 8, 8, channels), axis=0)
    acc_ref[1] += jnp.sum(second.reshape(rows // 8, 8, channels), axis=0)


def spread_sums(acc_ref, copies_ref):
    channels = acc_ref.shape[-1]
    for k in range(2):
        row = jnp.sum(acc_ref[k], axis=0, keepdims=True)
        copies_ref[:, :, k * channels : (k + 1) * channels] = jnp.broadcast_to(
            row[None], (copies_ref.shape[0], 1, channels)
        )


def came_sums(came_ref):
    total = jnp.sum(came_ref[...], axis=0)
    half = total.shape[-1] // 2
    return total[:, :half], total[:, half:]


def norm_of(came_ref, pairs_ref, number, count):
    first, second = came_sums(came_ref)
    mean = first / count
    spread = lax.rsqrt(second / count - mean * mean + norm_epsilon)
    return mean, spread, pairs_ref[number, 0:1], pairs_ref[number, 1:2]


def norm_rows(vec_ref):
    return vec_ref[0:1], vec_ref[1:2], vec_ref[2:3], vec_ref[3:4]


def normal(values, norm):
    return (values.astype(F32) - norm[0]) * norm[1]


def activated(values, norm):
    z = normal(values, norm) * norm[2] + norm[3]
    return z * sigmoid(z)


def back_act(q, values, norm):
    xhat = normal(values, norm)
    z = xhat * norm[2] + norm[3]
    gate = sigmoid(z)
    return q * gate * (1.0 + z * (1.0 - gate)), xhat


def back_norm(dz, values, norm, sums, count):
    xhat = normal(values, norm)
    return norm[2] * norm[1] * (dz.astype(F32) - sums[0] / count - xhat * (sums[1] / count))


def swap_halves(value):
    return pltpu.roll(value, LANES // 2, 1)


def halves_of(first, second):
    low = lax.broadcasted_iota(jnp.int32, first.shape, 1) < LANES // 2
    return jnp.where(low, first, swap_halves(second)), jnp.where(low, swap_halves(first), second)


def fetch_wide(layer, own_ref, other_ref, came_ref, sems):
    half = own_ref.shape[0]
    fetches = [
        pltpu.make_async_copy(ref.at[:, layer], came_ref.at[pl.ds(k * half, half)], sems.at[k])
        for k, ref in enumerate((own_ref, other_ref))
    ]
    for fetch in fetches:
        fetch.start()
    return fetches


def unpack_wide(orders, chans, me_ref, came_ref, taps_ref):
    devices, groups, rows, _ = came_ref.shape
    count = devices // chans
    per = LANES // (taps_ref.shape[2] // chans)
    wide = per * LANES
    piece = LANES // per
    spread = chosen(wide, wide, lambda r: (r % LANES) // piece * LANES + r // LANES * piece + r % piece)
    for frame in range(count):
        for side in range(chans // per):
            parts = []
            for k in range(per):
                at = position(orders, me_ref, side * per + k, frame)
                parts.append(came_ref[at].reshape(groups * rows, LANES))
            result = dot_nt(jnp.concatenate(parts, axis=1), spread).astype(BF16)
            for slab in range(per):
                for group in range(groups):
                    if slab * groups + group < 9:
                        taps_ref[slab * groups + group, frame * rows : (frame + 1) * rows, side * LANES : (side + 1) * LANES] = result[
                            group * rows : (group + 1) * rows, slab * LANES : (slab + 1) * LANES
                        ]


def unpack_kernel(layers, orders, chans, me_ref, own_ref, other_ref, *rest):
    outs, came_refs, sems = rest[: len(layers)], rest[len(layers) : -1], rest[-1]
    fetches = [
        fetch_wide(layer, own_ref, other_ref, came_refs[n], sems.at[pl.ds(2 * n, 2)]) for n, layer in enumerate(layers)
    ]
    for n, out in enumerate(outs):
        for fetch in fetches[n]:
            fetch.wait()
        unpack_wide(orders, chans, me_ref, came_refs[n], out.ref)
        out.send(0, 9, 0)
    for out in outs:
        out.finish()


def turn_taps(taps_ref, turned_ref):
    wide = taps_ref.shape[-1]
    for kt in range(3):
        for kf in range(3):
            turned_ref[2 - kt, :, kf * wide : (kf + 1) * wide] = taps_ref[kt, kf * wide : (kf + 1) * wide]


def pack_wide(order, chans, me_ref, slabs, out_ref):
    devices, groups, rows, _ = out_ref.shape
    count = devices // chans
    per = LANES // (slabs[0].shape[1] // chans)
    wide = per * LANES
    piece = LANES // per
    gather = chosen(wide, wide, lambda r: (r % LANES) // piece * LANES + r // LANES * piece + r % piece)
    for group in range(groups):
        for side in range(chans // per):
            parts = []
            for slab in range(per):
                tap = slab * groups + group
                tap = tap if tap < 9 else 8
                parts.append(slabs[tap][:, side * LANES : (side + 1) * LANES])
            result = dot_nt(jnp.concatenate(parts, axis=1), gather).astype(BF16)
            for k in range(per):
                for frame in range(count):
                    at = position(order, me_ref, side * per + k, frame)
                    out_ref[at, group] = result[frame * rows : (frame + 1) * rows, k * LANES : (k + 1) * LANES]


def unpack_first(
    orders, chans, shard, count_zero, window, me_ref, place_ref, own_ref, other_ref, numbers_ref,
    taps_ref, short_ref, vec_ref, pairs_ref, masks_ref, raw_ref, came_ref, sems,
):
    half = own_ref.shape[0]
    fetches = [
        pltpu.make_async_copy(ref, came_ref.at[pl.ds(k * half, half)], sems.at[k]) for k, ref in enumerate((own_ref, other_ref))
    ]
    for fetch in fetches:
        fetch.start()
    for fetch in fetches:
        fetch.wait()
    devices = came_ref.shape[0]
    count = devices // chans
    ins, outs = short_ref.shape
    per = LANES // (outs // chans)
    rows = packed_rows(shard, per)
    wide = per * LANES
    piece = LANES // per
    spread = chosen(wide, wide, lambda r: (r % LANES) // piece * LANES + r // LANES * piece + r % piece)
    for frame in range(count):
        for side in range(chans // per):
            parts = [came_ref[position(orders, me_ref, side * per + k, frame), 0:rows] for k in range(per)]
            result = dot_nt(jnp.concatenate(parts, axis=1), spread)
            for slab in range(per):
                start = slab * rows
                size = min(rows, shard - start)
                if size > 0:
                    raw_ref[side, frame * shard + start : frame * shard + start + size] = result[
                        :size, slab * LANES : (slab + 1) * LANES
                    ]
    for tap in range(9):
        kt, kf = tap // 3, tap % 3
        for side in range(outs // LANES):
            lanes = slice(side * LANES, (side + 1) * LANES)
            taps_ref[kt, kf * ins : (kf + 1) * ins, lanes] = raw_ref[side, pl.ds(tap, ins, stride=9)].astype(BF16)
    for side in range(outs // LANES):
        short_ref[:, side * LANES : (side + 1) * LANES] = raw_ref[side, 9 * ins : 10 * ins].astype(BF16)
    unpack_small(count_zero, came_ref, rows, vec_ref, pairs_ref)
    chan, frame = place_ref[0], place_ref[1]
    lane = lax.broadcasted_iota(jnp.int32, (1, LANES), 1)
    numbers = numbers_ref[...]
    edge = HALO + 1
    for outer, inside, step in ((0, lane < edge, -1), (chans - 1, (lane >= window - edge) & (lane < window), 1)):
        other = frame + step
        exists = (other >= 0) & (other < count)
        row = came_ref[code_gap(orders, me_ref, jnp.clip(other, 0, count - 1)), rows + 32 : rows + 48].astype(F32)[0:1]
        numbers = jnp.where(inside & (chan == outer), jnp.where(exists, row, 0.0), numbers)
    after_one = pltpu.roll(numbers, LANES - 1, 1)
    after_two = pltpu.roll(numbers, LANES - 2, 1)
    masks_ref[0:1] = (numbers == after_one).astype(F32)
    masks_ref[1:2] = (after_one == after_two).astype(F32)


def unpack_small(count_zero, came_ref, at, vec_ref, pairs_ref):
    parts = [jnp.sum(came_ref[:, at + 16 * k : at + 16 * (k + 1)].astype(F32), axis=0) for k in range(2)]
    sums = parts[0] + parts[1]
    average = sums[0:1] / count_zero
    vec_ref[0:1] = average
    vec_ref[1:2] = lax.rsqrt(sums[1:2] / count_zero - average * average + norm_epsilon)
    vec_ref[2:3] = sums[2:3]
    vec_ref[3:4] = sums[9:10]
    c = lax.broadcasted_iota(jnp.int32, (LANES, 2 * LANES), 1)
    r = lax.broadcasted_iota(jnp.int32, (LANES, 2 * LANES), 0)
    for side in range(2):
        place = (c == 2 * r + side).astype(BF16)
        spread_rows = [dot(part.astype(BF16), place) for part in (parts[0], parts[1])]
        both = spread_rows[0] + spread_rows[1]
        for k in range(3):
            for kind in range(2):
                row = both[2 + 7 * kind + 1 + 2 * k + side : 2 + 7 * kind + 2 + 2 * k + side]
                pairs_ref[k, kind : kind + 1] = row if side == 0 else pairs_ref[k, kind : kind + 1] + row


def turn_first(taps, short, turned_ref):
    ins, outs = short.ref.shape
    taps.need_all()
    short.need_all()
    for kt in range(3):
        turned_ref[2 - kt, 0:ins, 0:outs] = taps.ref[kt, ins : 2 * ins]
        turned_ref[2 - kt, 0:ins, outs:] = jnp.zeros((ins, outs), BF16)
        turned_ref[2 - kt, ins:, 0:outs] = taps.ref[kt, 2 * ins :]
        turned_ref[2 - kt, ins:, outs:] = taps.ref[kt, 0:ins]


def pack_first(order, chans, shard, me_ref, raw_ref, out_ref):
    devices, rows, _ = out_ref.shape
    count = devices // chans
    outs = raw_ref.shape[0] * LANES
    per = LANES // (outs // chans)
    wide = per * LANES
    piece = LANES // per
    gather = chosen(wide, wide, lambda r: (r % LANES) // piece * LANES + r // LANES * piece + r % piece)
    for frame in range(count):
        for side in range(chans // per):
            parts = [raw_ref[side, frame * shard + slab * rows : frame * shard + (slab + 1) * rows] for slab in range(per)]
            result = dot_nt(jnp.concatenate(parts, axis=1).astype(BF16), gather).astype(BF16)
            for k in range(per):
                at = position(order, me_ref, side * per + k, frame)
                out_ref[at] = result[:, k * LANES : (k + 1) * LANES]


def packed_rows(shard, per):
    return -(-shard // (per * 16)) * 16


def frames_in(chan_ref, mains, edges_ref, total, target, body):
    parts = len(mains)
    for main in mains:
        main.need_all()
    for low, at, part in ((0, 0, 0), (total - HALO, HALO, parts - 1)):

        @pl.when(chan_ref[0] == part)
        def _():
            for d, main in enumerate(mains):
                size = main.ref.shape[1]
                main.ref[low : low + HALO] = edges_ref[d, at : at + HALO, size : 2 * size]

    def piece(at, chunk, _):
        cubes = jnp.concatenate([main.ref[pl.ds(at, chunk)] for main in mains], axis=1)
        body(cubes.reshape(chunk * cubes.shape[1], LANES), at, chunk)

    loop(0, total, target, piece, 2)


def lane_row(chan_ref, q, size):
    return (q // size ^ chan_ref[0]) * size + q % size


def frames_out(rows, count, out_ref, at):
    parts, _, size, _ = out_ref.shape
    cube = rows.reshape(count, parts * size, LANES)
    for s in range(parts):
        out_ref[s, pl.ds(at, count)] = cube[:, s * size : (s + 1) * size].astype(out_ref.dtype)


def pieces_of(total):
    return fit(total, 4)


def channels_of(ref, base, chunk, parity):
    return ref[pl.ds(base, chunk), parity].reshape(chunk * B1, ref.shape[-1])


def signal_kernel(chan_ref, main, edges_ref, x_out):
    parts, _, size, _ = main.ref.shape
    x_ref = x_out.ref
    total = x_ref.shape[0]
    channels = x_ref.shape[-1]
    half = LANES // 2
    split = chosen(LANES, LANES, lambda r: r // half * half + r % B1 * 2 + r % half // B1)
    order = chosen(channels, channels, lambda r: r // half + r % half * 2)

    def turn(values, base, chunk):
        turned = dot_nt(split, values)
        for parity in range(2):
            pairs = []
            for pair in range(chunk // 2):
                lanes = turned[:, pair * LANES : (pair + 1) * LANES]
                even = lanes[parity * B1 : (parity + 1) * B1]
                odd = lanes[half + parity * B1 : half + (parity + 1) * B1]
                pairs.extend(halves_of(even, odd))
            x = dot(jnp.concatenate(pairs, axis=0).astype(BF16), order)
            x_ref[pl.ds(base, chunk), parity] = x.reshape(chunk, B1, channels).astype(BF16)

    main.need_all()
    for low, at, part in ((0, 0, 0), (total - HALO, HALO, parts - 1)):

        @pl.when(chan_ref[0] == part)
        def _():
            for s in range(parts):
                main.ref[s, low : low + HALO] = edges_ref[s ^ part, at : at + HALO, 0:size]

    def piece(at, chunk, _):
        cubes = jnp.concatenate([main.ref[s, pl.ds(at, chunk)] for s in range(parts)], axis=1)
        turn(cubes.reshape(chunk * parts * size, LANES), at, chunk)

    loop(0, total, 48, piece, 2)
    x_out.send(0, total, 0)
    x_out.finish()


def first_kernel(own, prev_ref, next_ref, x, taps, short, vec_ref, h_out, s_out, copies_ref, cols_ref, acc_ref):
    total = x.ref.shape[0]
    channels = x.ref.shape[-1]
    norm = norm_rows(vec_ref)

    def build(base, chunk):
        acts = [activated(channels_of(x.ref, base, chunk, parity), norm) for parity in range(2)]
        below, _ = shifts(acts[1])
        put(cols_ref, base, chunk, jnp.concatenate([below, acts[0], acts[1]], axis=1))

    by_pieces([x], total, 12, build)
    acc_ref[...] = jnp.zeros_like(acc_ref)
    taps.need_all()
    short.need_all()

    def conv(base, chunk, number):
        result = taps_sum(cols_ref, taps.ref, (prev_ref, next_ref), base, chunk)
        put(h_out.ref, base, chunk, result)
        h_out.send(base, chunk, number)
        mine = own_rows(result, base, chunk, HALO, HALO + own)
        add_sums(acc_ref, mine, mine * mine)
        even = rows_of(cols_ref, base, chunk)[:, channels : 2 * channels]
        put(s_out.ref, base, chunk, dot(even, short.ref[...]))
        s_out.send(base, chunk, number)

    unrolled(1, total - 1, 12, conv)
    spread_sums(acc_ref, copies_ref)
    h_out.finish()
    s_out.finish()


def by_pieces(fetched, total, target, body):
    pieces = fetched[0].pieces
    size = total // pieces

    def piece(number, carry):
        for operand in fetched:
            operand.need(number)
        spans(number * size, size, target, lambda base, chunk, _: body(base, chunk))
        return carry

    lax.fori_loop(0, pieces, piece, 0)


def activate_into(h, norm, cols_ref):
    def build(base, chunk):
        act = activated(rows_of(h.ref, base, chunk), norm)
        below, above = shifts(act)
        put(cols_ref, base, chunk, jnp.concatenate([below, act, above], axis=1))

    by_pieces([h], cols_ref.shape[0], 24, build)


def forward_kernel(own, count, number, lead, target, with_short, prev_ref, next_ref, h, taps, *rest):
    if with_short:
        s, came_ref, pairs_ref, out, copies_ref, vec_ref, cols_ref, acc_ref = rest
    else:
        came_ref, pairs_ref, out, copies_ref, vec_ref, cols_ref, acc_ref = rest
    total = cols_ref.shape[0]
    norm = norm_of(came_ref, pairs_ref, number, count)
    for k in range(4):
        vec_ref[k : k + 1] = norm[k]
    activate_into(h, norm, cols_ref)
    acc_ref[...] = jnp.zeros_like(acc_ref)
    taps.need_all()

    def conv(base, chunk, number):
        result = taps_sum(cols_ref, taps.ref, (prev_ref, next_ref), base, chunk)
        if with_short:
            if number == 0:
                s.need_all()
            result = result + rows_of(s.ref, base, chunk).astype(F32)
        put(out.ref, base, chunk, result)
        out.send(base, chunk, number)
        mine = own_rows(result, base, chunk, HALO, HALO + own)
        add_sums(acc_ref, mine, mine * mine)

    unrolled(lead, total - lead, target, conv)
    spread_sums(acc_ref, copies_ref)
    out.finish()


def shift_into(value, base, chunk, cols_ref):
    below, above = shifts(value)
    put(cols_ref, base, chunk, jnp.concatenate([above, value, below], axis=1))


def top_kernel(parts, chan_ref, *rest):
    mains, (edges_ref, e_out) = rest[:parts], rest[parts:]
    size = mains[0].ref.shape[1]
    total, _, wide = e_out.shape
    quarter = LANES // 4
    half = LANES // 2
    order = chosen(wide, wide, lambda r: r // half + lane_row(chan_ref, r % half, size) * 4)
    eye = chosen(LANES, LANES, same)

    def turn(values, base, chunk):
        turned = dot_nt(eye, values)
        frames = []
        for pair in range(chunk // 2):
            lanes = turned[:, pair * LANES : (pair + 1) * LANES]
            sides = [
                halves_of(
                    lanes[2 * side * quarter : (2 * side + 1) * quarter],
                    lanes[(2 * side + 1) * quarter : (2 * side + 2) * quarter],
                )
                for side in range(2)
            ]
            frames.extend([jnp.concatenate([sides[0][k], sides[1][k]], axis=1) for k in range(2)])
        put(e_out.ref, base, chunk, dot(jnp.concatenate(frames, axis=0).astype(BF16), order))

    frames_in(chan_ref, mains, edges_ref, total, 48, turn)
    e_out.send(0, total, 0)
    e_out.finish()


def top_back_kernel(layer, orders, chans, me_ref, prev_ref, next_ref, e, own_ref, other_ref, q_out, taps_out, cols_ref, turned_ref, came_ref, sems):
    total = q_out.shape[0]
    wide = e.ref.shape[-1]
    fetches = fetch_wide(layer, own_ref, other_ref, came_ref, sems)

    def build(base, chunk):
        shift_into(rows_of(e.ref, base, chunk).astype(F32), base, chunk, cols_ref)

    by_pieces([e], total, 24, build)
    for fetch in fetches:
        fetch.wait()
    unpack_wide(orders, chans, me_ref, came_ref, taps_out.ref)
    taps_out.send(0, 9, 0)
    for kt in range(3):
        for kf in range(3):
            turned_ref[2 - kt, :, kf * wide : (kf + 1) * wide] = taps_out.ref[3 * kt + kf]

    def back(base, chunk, number):
        put(q_out.ref, base, chunk, taps_sum(cols_ref, turned_ref, (prev_ref, next_ref), base, chunk, dot_nt))
        q_out.send(base, chunk, number)

    unrolled(3, total - 3, 12, back)
    taps_out.finish()
    q_out.finish()


def top_norm_kernel(own, count, q, h, came_ref, pairs_ref, dz_out, copies_ref, vec_ref, acc_ref):
    total = dz_out.shape[0]
    norm = norm_of(came_ref, pairs_ref, 2, count)
    for k in range(4):
        vec_ref[k : k + 1] = norm[k]
    acc_ref[...] = jnp.zeros_like(acc_ref)

    def back(base, chunk):
        dz, xhat = back_act(rows_of(q.ref, base, chunk).astype(F32), rows_of(h.ref, base, chunk), norm)
        put(dz_out.ref, base, chunk, dz)
        mine = own_rows(dz, base, chunk, HALO, HALO + own)
        add_sums(acc_ref, mine, own_rows(dz * xhat, base, chunk, HALO, HALO + own))

    size = total // q.pieces
    for piece in range(q.pieces):
        q.need(piece)
        h.need(piece)
        unrolled(piece * size, (piece + 1) * size, 12, lambda base, chunk, _: back(base, chunk))
    dz_out.send(0, total, 0)
    spread_sums(acc_ref, copies_ref)
    dz_out.finish()


def last_kernel(own, prev_ref, next_ref, h, taps, x, vec_ref, y_ref, cols_ref):
    wide = cols_ref.shape[-1] // 3
    half = LANES // 2
    order = chosen(wide, wide, lambda r: r // half + r % half * 4)
    eye = chosen(LANES, LANES, same)
    activate_into(h, norm_rows(vec_ref), cols_ref)
    taps.need_all()
    x.need_all()

    def conv(base, chunk, _):
        result = taps_sum(cols_ref, taps.ref, (prev_ref, next_ref), base, chunk) + rows_of(x.ref, base, chunk).astype(F32)
        mixed = dot_nt(result.astype(BF16), order)
        cube = mixed.reshape(chunk, B1, wide)
        for pair in range(chunk // 2):
            stack = []
            for side in range(wide // LANES):
                lanes = slice(side * LANES, (side + 1) * LANES)
                stack.extend(halves_of(cube[2 * pair][:, lanes], cube[2 * pair + 1][:, lanes]))
            turned = dot_nt(eye, jnp.concatenate(stack, axis=0).astype(BF16))
            frames_out(turned, 2, y_ref, base - HALO + 2 * pair)

    unrolled(HALO, HALO + own, 12, conv, 2)


def middle_kernel(own, count, lead, target, with_top, prev_ref, next_ref, dz, h, *rest):
    if with_top:
        e, *rest = rest
    taps, low, back_ref, vec_ref, low_vec_ref, d_out, dz_out, copies_ref, sums_ref, cols_ref, acc_ref, turned_ref = rest
    total = cols_ref.shape[0]
    norm, low_norm = norm_rows(vec_ref), norm_rows(low_vec_ref)
    sums = came_sums(back_ref)
    sums_ref[0:1], sums_ref[1:2] = sums

    def build(base, size):
        d = back_norm(rows_of(dz.ref, base, size), rows_of(h.ref, base, size), norm, sums, count)
        if with_top:
            d = d + rows_of(e.ref, base, size).astype(F32)
        put(d_out.ref, base, size, d)
        shift_into(d, base, size, cols_ref)

    by_pieces([dz, h, e] if with_top else [dz, h], total, 24, build)
    d_out.send(0, total, 0)
    acc_ref[...] = jnp.zeros_like(acc_ref)
    taps.need_all()
    turn_taps(taps.ref, turned_ref)

    def back(base, chunk, number):
        q = taps_sum(cols_ref, turned_ref, (prev_ref, next_ref), base, chunk, dot_nt)
        if number == 0:
            low.need_all()
        new, xhat = back_act(q, rows_of(low.ref, base, chunk), low_norm)
        put(dz_out.ref, base, chunk, new)
        dz_out.send(base, chunk, number)
        mine = own_rows(new, base, chunk, HALO, HALO + own)
        add_sums(acc_ref, mine, mine * xhat)

    unrolled(lead, total - lead, target, back)
    spread_sums(acc_ref, copies_ref)
    d_out.finish()
    dz_out.finish()


def give(buffer_ref, keep_ref, send_ref, sems):
    half = keep_ref.shape[0]
    keep = pltpu.make_async_copy(buffer_ref.at[pl.ds(0, half)], keep_ref, sems.at[0])
    send = pltpu.make_async_copy(buffer_ref.at[pl.ds(half, half)], send_ref, sems.at[1])
    keep.start()
    send.start()
    keep.wait()
    send.wait()


def weight_kernel(
    own, order, chans, me_ref, h, d, vec_ref, lanes_ref, keep_ref, send_ref,
    cols_ref, turned_ref, buffer_ref, sems,
):
    norm = norm_rows(vec_ref)
    wide = h.ref.shape[-1]

    def build(base, chunk):
        shift_into(rows_of(d.ref, base, chunk).astype(F32), base, chunk, cols_ref)

    chunk = fit(own, 28, 4)
    staged = all(HALO + chunk * (i + 1) <= h.size * (i + 2) for i in range(own // chunk)) and own // chunk + 1 == h.pieces
    if not staged:
        h.need_all()

    def turn(base, chunk, number):
        if staged:
            if number == 0:
                h.need(0)
            h.need(number + 1)
        u = activated(rows_of(h.ref, HALO + base, chunk), norm)
        columns = pl.ds(base * B1, chunk * B1)
        turned = transposed(u.astype(BF16))
        turned_ref[0, :, columns] = turned * lanes_ref[1:2, columns]
        turned_ref[1, :, columns] = turned
        turned_ref[2, :, columns] = turned * lanes_ref[0:1, columns]

    for number in range(own // chunk):
        turn(number * chunk, chunk, number)
    by_pieces([d], cols_ref.shape[0], 24, build)
    slabs = []
    for tap in range(3):
        other = cols_ref[pl.ds(HALO + 1 - tap, own)].reshape(own * B1, cols_ref.shape[-1])
        grad = dot(turned_ref[tap], other).astype(BF16)
        slabs.extend([grad[:, k * wide : (k + 1) * wide] for k in range(3)])
    pack_wide(order, chans, me_ref, slabs, buffer_ref)
    give(buffer_ref, keep_ref, send_ref, sems)


def bottom_kernel(
    own, count, prev_ref, next_ref, dz, h, taps, short, e1, x, back_ref, high_vec_ref, vec_ref,
    d_out, dz_out, copies_ref, sums_ref, cols_ref, acc_ref, turned_ref,
):
    total = cols_ref.shape[0]
    norm, low_norm = norm_rows(high_vec_ref), norm_rows(vec_ref)
    sums = came_sums(back_ref)
    sums_ref[0:1], sums_ref[1:2] = sums
    channels = x.ref.shape[-1]

    def build(base, size):
        d = back_norm(rows_of(dz.ref, base, size), rows_of(h.ref, base, size), norm, sums, count)
        put(d_out.ref, base, size, d)
        _, above = shifts(d)
        put(cols_ref, base, size, jnp.concatenate([d, above], axis=1))

    by_pieces([dz, h], total, 24, build)
    d_out.send(0, total, 0)
    acc_ref[...] = jnp.zeros_like(acc_ref)
    turn_first(taps, short, turned_ref)
    e1.need_all()
    x.need_all()

    def back(base, chunk, number):
        q = taps_sum(cols_ref, turned_ref, (prev_ref, next_ref), base, chunk, dot_nt)
        r = dot_nt(rows_of(e1.ref, base, chunk), short.ref[...])
        parts = (q[:, :channels] + r, q[:, channels:])
        for parity in range(2):
            new, xhat = back_act(parts[parity], channels_of(x.ref, base, chunk, parity), low_norm)
            dz_out.ref[pl.ds(base - HALO, chunk), parity] = new.reshape(chunk, B1, channels).astype(BF16)
            add_sums(acc_ref, new, new * xhat)
        dz_out.send(base - HALO, chunk, number)

    unrolled(HALO, HALO + own, 12, back)
    spread_sums(acc_ref, copies_ref)
    d_out.finish()
    dz_out.finish()


def first_weight_kernel(
    own, order, chans, shard, me_ref, d, x, e1, vec_ref, lanes_ref, keep_ref, send_ref,
    cols_ref, turned_ref, raw_ref, buffer_ref, sems,
):
    norm = norm_rows(vec_ref)
    channels = x.ref.shape[-1]
    wide = d.ref.shape[-1]

    def build(base, size):
        value = rows_of(d.ref, base, size)
        _, above = shifts(value.astype(F32))
        put(cols_ref, base, size, jnp.concatenate([value, above.astype(BF16)], axis=1))

    by_pieces([d], cols_ref.shape[0], 24, build)
    x.need_all()
    e1.need_all()

    def turn(base, chunk):
        columns = pl.ds(base * B1, chunk * B1)
        for parity in range(2):
            place = slice(parity * channels, (parity + 1) * channels)
            turned = transposed(activated(channels_of(x.ref, HALO + base, chunk, parity), norm).astype(BF16))
            turned_ref[0, place, columns] = turned * lanes_ref[1:2, columns]
            turned_ref[1, place, columns] = turned
            turned_ref[2, place, columns] = turned * lanes_ref[0:1, columns]

    chunk = fit(own, 28, 4)
    for number in range(own // chunk):
        turn(number * chunk, chunk)
    for tap in range(3):
        other = cols_ref[pl.ds(HALO + 1 - tap, own)].reshape(own * B1, cols_ref.shape[-1])
        grad = dot(turned_ref[tap], other)
        slabs = (grad[channels:, wide:], grad[:channels, :wide], grad[channels:, :wide])
        for kf in range(3):
            for side in range(wide // LANES):
                raw_ref[side, pl.ds(3 * tap + kf, channels, stride=9)] = slabs[kf][:, side * LANES : (side + 1) * LANES]
    short = dot(turned_ref[1, 0:channels], e1.ref[pl.ds(HALO, own)].reshape(own * B1, wide))
    rest = raw_ref.shape[1] - 10 * channels
    for side in range(wide // LANES):
        raw_ref[side, 9 * channels : 10 * channels] = short[:, side * LANES : (side + 1) * LANES]
        raw_ref[side, 10 * channels :] = jnp.zeros((rest, LANES), F32)
    pack_first(order, chans, shard, me_ref, raw_ref, buffer_ref)
    give(buffer_ref, keep_ref, send_ref, sems)


def input_kernel(own, count, dz, x, back_ref, vec_ref, out_ref, sums_ref):
    norm = norm_rows(vec_ref)
    sums = came_sums(back_ref)
    sums_ref[0:1], sums_ref[1:2] = sums
    channels = x.ref.shape[-1]
    half = LANES // 2
    order = chosen(channels, channels, lambda r: r // half + r % half * 2)
    eye = chosen(LANES, LANES, same)
    split = chosen(LANES, LANES, lambda r: r // half * half + r % 2 * B1 + r % half // 2)
    dz.need_all()
    x.need_all()

    def build(base, chunk, _):
        mixed = []
        for parity in range(2):
            g = back_norm(
                channels_of(dz.ref, base, chunk, parity), channels_of(x.ref, HALO + base, chunk, parity), norm, sums, count
            )
            mixed.append(dot_nt(g.astype(BF16), order).reshape(chunk, B1, channels))
        for pair in range(chunk // 2):
            even, odd = [], []
            for parity in range(2):
                first, second = halves_of(mixed[parity][2 * pair], mixed[parity][2 * pair + 1])
                even.append(first)
                odd.append(second)
            stack = jnp.concatenate(even + odd, axis=0).astype(BF16)
            turned = dot_nt(eye, dot(split, stack).astype(BF16))
            frames_out(turned, 2, out_ref, base + 2 * pair)

    loop(0, own, 28, build, 2)


SMEM = pl.BlockSpec(memory_space=pltpu.SMEM)
VMEM = pl.BlockSpec(memory_space=pltpu.VMEM)
HBM = pl.BlockSpec(memory_space=pl.ANY)
DMA = pltpu.SemaphoreType.DMA


def run(kernel, scalars, fetched, operands, sent, outs, scratch, micros, plain=(), loose=()):
    arrays = [array for array, _ in fetched]
    buffers = [pltpu.VMEM(array.shape, array.dtype) for array in arrays] + [pltpu.VMEM(shape, kind) for shape, kind, _ in sent]
    sems = [DMA((pieces,)) for _, pieces in fetched] + [DMA((pieces,)) for _, _, pieces in sent]
    counts = (len(scalars), len(fetched), len(loose), len(operands), len(sent), len(plain), len(outs), len(scratch), len(buffers), len(sems))

    def whole(*refs):
        groups, at = [], 0
        for count in counts:
            groups.append(refs[at : at + count])
            at += count
        small, sources, left, inputs, targets, copied, results, own, held, marks = groups
        small = [view for ref in small for view in ((ref.at[0], ref.at[1]) if len(ref.shape) == 2 else (ref,))]
        incoming = [Fetched(*triple) for triple in zip(sources, held, marks)]
        leaving = [Sent(*triple) for triple in zip(targets, held[len(incoming) :], marks[len(incoming) :])]
        for operand in incoming:
            operand.start()
        kernel(*small, *incoming, *left, *inputs, *leaving, *copied, *results, *own)

    made = [(shape, kind) for shape, kind, _ in sent] + list(plain) + list(outs)
    moved = sum(x.size * x.dtype.itemsize for x in arrays + list(operands))
    return pl.pallas_call(
        whole,
        in_specs=[SMEM] * len(scalars) + [HBM] * (len(arrays) + len(loose)) + [VMEM] * len(operands),
        out_specs=[HBM] * (len(sent) + len(plain)) + [VMEM] * len(outs),
        out_shape=[jax.ShapeDtypeStruct(shape, kind) for shape, kind in made],
        scratch_shapes=[pltpu.VMEM(*one) if isinstance(one, tuple) else one for one in scratch] + buffers + sems,
        compiler_params=pltpu.CompilerParams(vmem_limit_bytes=VMEM_BYTES),
        cost_estimate=pl.CostEstimate(flops=int(micros * 1.15e9), bytes_accessed=moved // 10, transcendentals=0),
    )(*scalars, *arrays, *loose, *operands)


def norm_pair(params, norm_index):
    if norm_index == 0:
        return jnp.stack([params[0, 0], params[1, 0]])
    row_pair = params[:, 2 * norm_index - 1 : 2 * norm_index + 1]
    return jnp.transpose(row_pair, (0, 2, 1)).reshape(2, -1)


def pack_norms(vectors):
    blocks = [vectors[0][None]]
    for vector in vectors[1:]:
        blocks.append(vector.reshape(-1, 2).T)
    return jnp.concatenate(blocks, axis=0)


def adam_step(weight, moment, square, gradient, step_rate, decay_rate):
    moment_next = beta_first * moment + (1.0 - beta_first) * gradient
    square_next = beta_second * square + (1.0 - beta_second) * gradient * gradient
    corrected = moment_next / (1.0 - beta_first**STEP)
    divisor = jnp.sqrt(square_next / (1.0 - beta_second**STEP)) + adam_epsilon
    weight_next = weight - step_rate * (corrected / divisor + decay_rate * weight)
    return (weight_next, moment_next, square_next)


def body(
    signal,
    clip_ids,
    output_grad,
    first_weight,
    first_mean,
    first_square,
    wide_weight,
    wide_mean,
    wide_square,
    norm_params,
    norm_mean,
    norm_square,
):
    chans = lax.axis_size("chan")
    groups_of_frames = lax.axis_size("frames")
    devices = chans * groups_of_frames
    chan = lax.axis_index("chan")
    me = {"chan": chan, "frames": lax.axis_index("frames")}
    group = signal.shape[0]
    own = group // chans
    total = own + 2 * HALO
    frames = group * groups_of_frames
    in_local = signal.shape[1] // B0
    ins = in_local * chans
    wide_local = output_grad.shape[1] // B1
    wide = wide_local * chans
    columns = first_weight.shape[1]
    per = LANES // columns
    count_zero = frames * B0
    count = frames * B1

    core = [("chan", 1)]
    near, far = halves("chan", chans)[:-1], halves("frames", groups_of_frames)
    gather_orders = (far + near + core, far[:-2] + far[-1:] + near + far[-2:-1] + core)
    order_grads = (far + near + core, far[:-2] + near + far[-2:] + core)
    first_order = (near + far[:-2] + far[-1:] + far[-2:-1] + core, near + far + core)
    code_first = jnp.stack([code_of(order, me) for order in first_order]).astype(jnp.int32)
    code_gather = jnp.stack([code_of(order, me) for order in gather_orders]).astype(jnp.int32)
    code_grads = jnp.stack([code_of(order, me) for order in order_grads]).astype(jnp.int32)
    last_step = len(core + near + far) - 1
    signal_rows = signal.reshape(group, -1, LANES)
    shard = first_weight.shape[0]
    packed = packed_rows(shard, per)
    first_send = jnp.pad(first_weight.astype(BF16), ((0, per * packed - shard), (0, 0)))
    first_send = jnp.transpose(first_send.reshape(per, packed, columns), (1, 0, 2)).reshape(packed, LANES)
    windows = windows_of(signal_rows)
    signal_main = lax.all_to_all(windows, "chan", 0, 0, tiled=True)
    edge = edges_of(jnp.concatenate([signal, output_grad], axis=1))

    local = signal.astype(F32)
    local_sums = jnp.stack([jnp.sum(local, axis=0), jnp.sum(local * local, axis=0)]).reshape(2, in_local, B0).sum(axis=2)
    shared = jnp.where(me["frames"] == 0, norm_params.reshape(-1, in_local), 0.0)
    small = jnp.concatenate([local_sums, shared], axis=0)
    places = jnp.arange(LANES) // in_local == chan
    small = jnp.where(places[None], jnp.tile(small, (1, LANES // in_local)), 0.0)
    big = lax.reduce_precision(small, 8, 7)
    edge_count = HALO + 1
    window = total + 2
    numbers = (clip_ids + 1).astype(F32)
    numbers = jnp.pad(numbers, (edge_count, edge_count))
    own_numbers = jnp.pad(lax.dynamic_slice_in_dim(numbers, chan * own, window, 0), (0, LANES - window))[None]
    edge_numbers = jnp.concatenate(
        [numbers[group : group + edge_count], jnp.zeros((window - 2 * edge_count,), F32), numbers[edge_count : 2 * edge_count]]
    )
    edge_numbers = jnp.pad(edge_numbers[None], ((0, 15), (0, LANES - window)))
    first_send = jnp.concatenate(
        [first_send, big.astype(BF16), (small - big).astype(BF16), edge_numbers.astype(BF16)], axis=0
    )[None]

    first_steps, block = [], first_send
    for k in range(last_step):
        if k == 1:
            block = after(block, windows)
        block = jnp.concatenate([block, exchange(block, first_order, k)], axis=0)
        first_steps.append(block)
        if k == 1:
            edges = by_distance(after(edge, block))
    edges = jnp.stack(edges)
    place = jnp.stack([chan, me["frames"]]).astype(jnp.int32)
    (x_zero,) = run(
        signal_kernel,
        (place,),
        [(signal_main, chans)],
        (edges,),
        [((total, 2, B1, ins), BF16, 1)],
        [],
        [],
        6,
    )
    first_halves = (block, exchange(after(block, x_zero), first_order, last_step))
    first_steps.append(first_halves[1])

    layers = wide_weight.shape[0]
    rows = wide_weight.shape[1] // 9
    slab_groups = -(-9 // per)
    wide_send = jnp.transpose(wide_weight.astype(BF16).reshape(layers, rows, 9, columns), (0, 2, 1, 3))
    wide_send = jnp.pad(wide_send, ((0, 0), (0, per * slab_groups - 9), (0, 0), (0, 0)))
    wide_send = jnp.transpose(wide_send.reshape(layers, per, slab_groups, rows, columns), (0, 2, 3, 1, 4))
    wide_send = wide_send.reshape(layers, slab_groups, rows, LANES)


    cube = (total, B1, wide)
    cols = (total, B1, 3 * wide)
    lane_rows = signal_rows.shape[1]
    copies = ((devices, 1, 2 * wide), F32)
    acc = ((2, 8, wide), F32)

    pieces = pieces_of(total)

    def steps(low, target):
        return steps_of(low, total - low, target)

    vec = ((4, wide), F32)
    both = ((2, wide), F32)

    slab_blocks = ((devices, slab_groups, rows, LANES), BF16)
    slabs = ((9, wide, wide), BF16, 1)

    def conv_taps(taps):
        return taps.reshape(3, 3 * wide, wide)

    taps_one, short_taps, vec_zero, pairs, both_masks = run(
        functools.partial(unpack_first, first_order, chans, shard, count_zero, window),
        (code_first, place),
        [],
        (own_numbers,),
        [],
        [((3, 3 * ins, wide), BF16), ((ins, wide), BF16), ((4, ins), F32), ((3, 2, wide), F32), ((2, LANES), F32)],
        [((wide // LANES, 10 * ins, LANES), F32), ((devices,) + first_send.shape[1:], BF16), DMA((2,))],
        4,
        loose=first_halves,
    )
    masks = (both_masks,)
    hidden_one, shortcut, sums = run(
        functools.partial(first_kernel, own),
        masks,
        [(x_zero, pieces), (taps_one, 1), (short_taps, 1)],
        (vec_zero,),
        [(cube, BF16, steps(1, 12)), (cube, BF16, steps(1, 12))],
        [copies],
        [((total, B1, 3 * ins), BF16), acc],
        8,
    )
    ties = [[first_steps[1]], [first_steps[2]], [first_steps[3], edges]] + [[first_halves[1]]] * last_step
    ties[last_step] = [hidden_one]
    wide_halves, _ = gather_halves(wide_send[None], gather_orders, ties[: last_step + 1])
    top_main = to_frames(after(output_grad, hidden_one).reshape(group, -1, LANES))
    came_one = to_all(sums)
    taps_two, taps_three = run(
        functools.partial(unpack_kernel, (0, 1), gather_orders, chans),
        (code_gather,),
        [],
        (),
        [slabs, slabs],
        [],
        [slab_blocks, slab_blocks, DMA((4,))],
        5,
        loose=wide_halves,
    )
    taps_two, taps_three = conv_taps(taps_two), conv_taps(taps_three)
    residual, sums, vec_one = run(
        functools.partial(forward_kernel, own, count, 0, 2, 12, True),
        masks,
        [(hidden_one, pieces), (taps_two, 1), (shortcut, 1)],
        (came_one, pairs),
        [(cube, BF16, steps(2, 12))],
        [copies, vec],
        [(cols, BF16), acc],
        9,
    )
    came_two = to_all(sums)
    (top,) = run(
        functools.partial(top_kernel, chans),
        (place,),
        [(main, 1) for main in top_main],
        (after(edges, residual),),
        [(cube, BF16, 1)],
        [],
        [],
        10,
    )
    hidden_two, sums, vec_two = run(
        functools.partial(forward_kernel, own, count, 1, 3, 12, False),
        masks,
        [(residual, pieces), (after(taps_three, top), 1)],
        (came_two, pairs),
        [(cube, BF16, steps(3, 12))],
        [copies, vec],
        [(cols, BF16), acc],
        9,
    )
    came_three = to_all(sums)
    top_back, taps_four = run(
        functools.partial(top_back_kernel, 2, gather_orders, chans),
        (code_gather,) + masks,
        [(after(top, hidden_two), pieces)],
        (),
        [(cube, BF16, steps(3, 12)), slabs],
        [],
        [(cols, BF16), ((3, wide, 3 * wide), BF16), slab_blocks, DMA((2,))],
        8,
        loose=wide_halves,
    )
    taps_four = conv_taps(taps_four)
    late = after(both_masks, hidden_two)[:, HALO : HALO + own]
    lanes = jnp.repeat(late, B1, axis=1).astype(BF16)
    dz_three, sums, vec_three = run(
        functools.partial(top_norm_kernel, own, count),
        (),
        [(top_back, pieces), (hidden_two, pieces)],
        (came_three, pairs),
        [(cube, BF16, 1)],
        [copies, vec],
        [acc],
        4,
    )
    back_three = to_all(sums)

    def weight_grad(vector, values, d):
        blocks = (devices, slab_groups, rows, LANES)
        kept = ((devices // 2,) + blocks[1:], BF16)
        return run(
            functools.partial(weight_kernel, own, order_grads, chans),
            (code_grads,),
            [(values, pieces), (d, pieces)],
            (vector, lanes),
            [],
            [],
            [(cols, BF16), ((3, wide, own * B1), BF16), (blocks, BF16), DMA((2,))],
            9,
            [kept, kept],
        )

    four = weight_grad(vec_three, hidden_two, after(top, dz_three))
    (block_rows,) = run(
        functools.partial(last_kernel, own),
        masks,
        [(after(hidden_two, dz_three), pieces), (taps_four, 1), (residual, 1)],
        (vec_three,),
        [],
        [((chans, own, lane_rows, LANES), BF16)],
        [(cols, BF16)],
        12,
    )

    block_came = lax.all_to_all(block_rows, "chan", 0, 0, tiled=True)
    d_three, dz_two, sums, norm_three = run(
        functools.partial(middle_kernel, own, count, 4, 12, False),
        masks,
        [(dz_three, pieces), (hidden_two, pieces), (after(taps_three, block_rows, *four), 1), (residual, 1)],
        (back_three, vec_three, vec_two),
        [(cube, BF16, 1), (cube, BF16, steps(4, 12))],
        [copies, both],
        [(cols, BF16), acc, ((3, wide, 3 * wide), BF16)],
        9,
    )
    back_two = to_all(sums)
    three = weight_grad(vec_two, residual, d_three)
    low_top, dz_one, sums, norm_two = run(
        functools.partial(middle_kernel, own, count, 5, 12, True),
        masks,
        [(dz_two, pieces), (residual, pieces), (top, pieces), (after(taps_two, block_came, *three), 1), (hidden_one, 1)],
        (back_two, vec_two, vec_one),
        [(cube, BF16, 1), (cube, BF16, steps(5, 12))],
        [copies, both],
        [(cols, BF16), acc, ((3, wide, 3 * wide), BF16)],
        9,
    )
    back_one = to_all(sums)
    two = weight_grad(vec_one, hidden_one, low_top)
    d_one, dz_zero, sums, norm_one = run(
        functools.partial(bottom_kernel, own, count),
        masks,
        [(dz_one, pieces), (hidden_one, pieces), (after(taps_one, *two), 1), (short_taps, 1), (low_top, 1), (x_zero, 1)],
        (back_one, vec_one, vec_zero),
        [(cube, BF16, 1), ((own, 2, B1, ins), BF16, steps_of(0, own, 12))],
        [((devices, 1, 2 * ins), F32), both],
        [((total, B1, 2 * wide), BF16), ((2, 8, ins), F32), ((3, 2 * ins, 2 * wide), BF16)],
        8,
    )
    back_zero = to_all(sums)
    gave = lax.optimization_barrier((*two, *three, *four, dz_zero))
    wide_keep, wide_send = scatter_step(gave[:6:2], gave[1:6:2], order_grads, last_step)
    one_blocks = (devices, packed, LANES)
    one_kept = ((devices // 2,) + one_blocks[1:], BF16)
    one = run(
        functools.partial(first_weight_kernel, own, first_order, chans, shard),
        (code_first,),
        [(after(d_one, *wide_keep, *wide_send), pieces), (x_zero, 1), (low_top, 1)],
        (vec_zero, lanes),
        [],
        [],
        [
            ((total, B1, 2 * wide), BF16),
            ((3, 2 * ins, own * B1), BF16),
            ((wide // LANES, 10 * ins + per * packed, LANES), F32),
            (one_blocks, BF16),
            DMA((2,)),
        ],
        8,
        [one_kept, one_kept],
    )
    wide_keep, wide_send = scatter_step(wide_keep, wide_send, order_grads, last_step - 1)
    input_rows, norm_zero = run(
        functools.partial(input_kernel, own, count_zero),
        (),
        [(after(dz_zero, *one), 1), (x_zero, 1)],
        (back_zero, vec_zero),
        [],
        [((chans, own, lane_rows, LANES), BF16), ((2, ins), F32)],
        [],
        8,
    )

    input_came = lax.all_to_all(input_rows, "chan", 0, 0, tiled=True)
    block_out = block_came.reshape(group, -1).astype(F32)
    input_grad = input_came.reshape(group, -1).astype(F32)

    wide_keep, wide_send = scatter_step(wide_keep, wide_send, order_grads, last_step - 2)
    wide_keep, wide_send = ([after(x[0], input_rows)] for x in (wide_keep, wide_send))
    first_keep, first_send_half = ([after(x, input_rows)] for x in one)
    wide_sum = scatter_steps(wide_keep, wide_send, order_grads, last_step - 2).astype(F32)
    lane_slab = jnp.arange(LANES) // columns
    real_slabs = lane_slab[None] * slab_groups + jnp.arange(slab_groups)[:, None] < 9
    packed_wide = wide_sum.reshape(3, slab_groups, rows, LANES)
    own_squares = jnp.sum(jnp.where(real_slabs[None, :, None], packed_wide * packed_wide, 0.0))
    wide_sum = jnp.transpose(wide_sum.reshape(3, slab_groups, rows, per, columns), (0, 3, 1, 2, 4))
    wide_sum = wide_sum.reshape(3, per * slab_groups, rows, columns)[:, :9]
    grad_wide = lax.optimization_barrier(jnp.transpose(wide_sum, (0, 2, 1, 3)).reshape(wide_weight.shape))
    first_sum = scatter_steps(first_keep, first_send_half, first_order, last_step + 1).astype(F32)
    real_rows = lane_slab[None] * packed + jnp.arange(packed)[:, None] < shard
    own_squares = own_squares + jnp.sum(jnp.where(real_rows, first_sum * first_sum, 0.0))
    grad_first = jnp.transpose(first_sum.reshape(packed, per, columns), (1, 0, 2)).reshape(-1, columns)[:shard]
    grad_first = lax.optimization_barrier(grad_first)

    norm_sums = [norm_zero, norm_one, norm_two, norm_three]
    grad_norms = jnp.stack([pack_norms([s[1] for s in norm_sums]), pack_norms([s[0] for s in norm_sums])], axis=1)
    grad_norms = lax.dynamic_slice_in_dim(grad_norms, chan * norm_params.shape[2], norm_params.shape[2], 2)
    own_squares = own_squares + jnp.where(lax.axis_index("frames") == 0, jnp.sum(grad_norms * grad_norms), 0.0)
    squares = jnp.sum(to_all(after(jnp.broadcast_to(own_squares, (devices, 1, LANES)), input_came))[:, 0, 0])
    grad_norm = jnp.sqrt(squares)
    factor = clip_limit / jnp.maximum(grad_norm, clip_limit)
    first_next, first_mean_next, first_square_next = adam_step(
        first_weight, first_mean, first_square, grad_first * factor, conv_rate, weight_decay
    )
    wide_next, wide_mean_next, wide_square_next = adam_step(
        wide_weight, wide_mean, wide_square, grad_wide * factor, conv_rate, weight_decay
    )
    norm_arrays = [jnp.transpose(array, (1, 0, 2)) for array in (norm_params, norm_mean, norm_square)]
    norm_next, norm_mean_next, norm_square_next = (
        jnp.transpose(array, (1, 0, 2)) for array in adam_step(*norm_arrays, grad_norms * factor, norm_rate, 0.0)
    )
    return (
        block_out,
        input_grad,
        grad_norm,
        first_next,
        first_mean_next,
        first_square_next,
        first_next.astype(BF16),
        wide_next,
        wide_mean_next,
        wide_square_next,
        wide_next.astype(BF16),
        norm_next,
        norm_mean_next,
        norm_square_next,
    )


def solution(mesh):
    rows = P("frames", "chan")
    deep = P(None, "frames", "chan")
    norms = P(None, None, "chan")
    in_specs = (rows, P("frames"), rows, rows, rows, rows, deep, deep, deep, norms, norms, norms)
    out_specs = (rows, rows, P(), rows, rows, rows, rows, deep, deep, deep, deep, norms, norms, norms)
    return jax.shard_map(body, mesh=mesh, in_specs=in_specs, out_specs=out_specs, check_vma=False)
```
